32 devices in a mesh: section: 2 (over core), shard: 4 (over z), replica: 4 (over y, x).
Axes of the slice: x: 2, y: 2, z: 4, core: 2. Of those that a mesh axis runs over, the one named last changes fastest.
Arguments:
- inputs: bfloat16 [2, 16, 256, 1152], P(None, ('shard', 'replica')), may hold values from -6 to 6
- cotangent: bfloat16 [2, 16, 256, 1152], P(None, ('shard', 'replica')), may hold values from -6 to 6
- timesteps: int32 [2, 16], P(None, ('shard', 'replica')), may hold values from 0 to 999
- labels: int32 [2, 16], P(None, ('shard', 'replica')), may hold values from 0 to 999
- class_table: bfloat16 [1000, 1152], replicated, may hold values from -6 to 6
- qkv_weight: bfloat16 [2, 1152, 3456], P('section', 'shard'), may hold values from -0.1875 to 0.1875
- qv_bias: bfloat16 [2, 2304], P('section', 'shard'), may hold values from -4 to 4
- proj_weight: bfloat16 [2, 1152, 1152], P('section', 'shard'), may hold values from -1 to 1
- proj_bias: bfloat16 [2, 1152], P('section', 'shard'), may hold values from -4 to 4
- up_projection_weight: bfloat16 [2, 1152, 4608], P('section', 'shard'), may hold values from -0.1875 to 0.1875
- up_bias: bfloat16 [2, 4608], P('section', 'shard'), may hold values from -4 to 4
- down_projection_weight: bfloat16 [2, 4608, 1152], P('section', 'shard'), may hold values from -0.09375 to 0.09375
- down_bias: bfloat16 [2, 1152], P('section', 'shard'), may hold values from -4 to 4
- ada_weight: bfloat16 [2, 1152, 6912], P('section', 'shard'), may hold values from -0.1875 to 0.1875
- ada_bias: bfloat16 [2, 6912], P('section', 'shard'), may hold values from -3.5 to 3.5
Outputs:
- block_outputs: bfloat16 [2, 2, 16, 256, 1152], P('section', None, ('shard', 'replica'))
- input_grads: float32 [2, 2, 16, 256, 1152], P('section', None, ('shard', 'replica'))
- table_grad: float32 [1000, 1152], P(('section', 'shard'))
- qkv_grad: float32 [2, 1152, 3456], P('section', 'shard')
- qv_bias_grad: float32 [2, 2304], P('section', 'shard')
- proj_grad: float32 [2, 1152, 1152], P('section', 'shard')
- proj_bias_grad: float32 [2, 1152], P('section', 'shard')
- up_grad: float32 [2, 1152, 4608], P('section', 'shard')
- up_bias_grad: float32 [2, 4608], P('section', 'shard')
- down_grad: float32 [2, 4608, 1152], P('section', 'shard')
- down_bias_grad: float32 [2, 1152], P('section', 'shard')
- ada_grad: float32 [2, 1152, 6912], P('section', 'shard')
- ada_bias_grad: float32 [2, 6912], P('section', 'shard')
The draws below stay inside these ranges and needn't reach their ends.
All inputs are finite; a program needn't handle non-finite values.
Results may differ from the reference program's by a relative error of at most 0.035.
Values may be sent and summed in bfloat16 or wider, within the bound.
No kernel may reach another device: no remote copies, remote signals or barrier semaphores. Data moves between devices by JAX's collectives and lax.ppermute only.
A program may use at most 384 MiB of HBM per device.

```python
import math
import jax
import jax.numpy as jnp
from jax import lax

D = 1152
HEADS = 16
HEAD_DIM = 72
FF = 4608
CLASSES = 1000
SEQ = 256
MICRO = 2
LATENTS = 16
N_SECTION = 2


def with_ends(result, stream_key, low, high):
    longest = result.shape.index(max(result.shape))
    spots = []
    for shift in (0, 1):
        where = [jax.random.randint(jax.random.fold_in(stream_key, axis), (), 0, length) for axis, length in enumerate(result.shape)]
        where[longest] = (where[longest] + shift) % result.shape[longest]
        spots.append(tuple(where))
    return result.at[spots[0]].set(low).at[spots[1]].set(high)


def levels(key, extent, cuts, smallest, top_value):
    level = 1.0
    for axis_at, blocks in cuts:
        draws = jax.random.uniform(jax.random.fold_in(jax.random.fold_in(key, 6), axis_at), (blocks,), jnp.float32, smallest / len(cuts), top_value / len(cuts))
        level = level * jnp.repeat(jnp.exp(draws), extent[axis_at] // blocks).reshape((-1,) + (1,) * (len(extent) - 1 - axis_at))
    return level


def bell_draw(stream_key, extent, scale, most, pieces=(), held_as=jnp.bfloat16):
    values = scale * jax.random.normal(stream_key, extent, jnp.float32)
    if pieces:
        values = values * levels(stream_key, extent, pieces, -0.22, 0.18)
    return jnp.clip(values, -most, most).astype(held_as)


def setup_inputs(seed: int = 0) -> dict:
    key_of = jax.random.split(jax.random.key(seed), 16)
    return {
        "inputs": bell_draw(key_of[0], (MICRO, LATENTS, SEQ, D), 1.0, 6.0, ((1, 16),)),
        "cotangent": bell_draw(key_of[1], (MICRO, LATENTS, SEQ, D), 1.0, 6.0, ((1, 16),)),
        "timesteps": with_ends(jax.random.randint(key_of[2], (MICRO, LATENTS), 0, 1000), jax.random.fold_in(key_of[2], 1), 0, 999).astype(jnp.int32),
        "labels": with_ends(jax.random.randint(key_of[3], (MICRO, LATENTS), 0, CLASSES), jax.random.fold_in(key_of[3], 1), 0, CLASSES - 1).astype(jnp.int32),
        "class_table": bell_draw(key_of[4], (CLASSES, D), 1.0, 6.0),
        "qkv_weight": bell_draw(key_of[5], (N_SECTION, D, 3 * D), D ** -0.5, 0.1875, ((0, 2), (1, 4))),
        "qv_bias": bell_draw(key_of[6], (N_SECTION, 2 * D), 1.0, 4.0, ((0, 2), (1, 4))),
        "proj_weight": bell_draw(key_of[7], (N_SECTION, D, D), (D // 32) ** -0.5, 1.0, ((0, 2), (1, 4))),
        "proj_bias": bell_draw(key_of[8], (N_SECTION, D), 1.0, 4.0, ((0, 2), (1, 4))),
        "up_projection_weight": bell_draw(key_of[9], (N_SECTION, D, FF), D ** -0.5, 0.1875, ((0, 2), (1, 4))),
        "up_bias": bell_draw(key_of[10], (N_SECTION, FF), 1.0, 4.0, ((0, 2), (1, 4))),
        "down_projection_weight": bell_draw(key_of[11], (N_SECTION, FF, D), FF ** -0.5, 0.09375, ((0, 2), (1, 4))),
        "down_bias": bell_draw(key_of[12], (N_SECTION, D), 1.0, 4.0, ((0, 2), (1, 4))),
        "ada_weight": bell_draw(key_of[13], (N_SECTION, D, 6 * D), D ** -0.5, 0.1875, ((0, 2), (1, 4))),
        "ada_bias": bell_draw(key_of[14], (N_SECTION, 6 * D), 0.8, 3.5, ((0, 2), (1, 4))),
    }


precise = lax.Precision.HIGHEST

@jax.custom_vjp
def low(v):
    return lax.optimization_barrier(v.astype(jnp.bfloat16)).astype(jnp.float32)

@jax.custom_vjp
def low_back(v):
    return v

def low_keep(v):
    return (low(v), None)

def low_pass(kept, grad):
    return (grad,)

def back_keep(v):
    return (v, None)

def back_low(kept, grad):
    return (low(grad),)
low.defvjp(low_keep, low_pass)
low_back.defvjp(back_keep, back_low)

def matmul(left, right):
    return jnp.dot(left, right, precision=precise)

def normalize(values, shift_vec, scale_vec):
    mean_val = lax.optimization_barrier(jnp.mean(values, axis=-1, keepdims=True))
    centred = values - mean_val
    variance = lax.optimization_barrier(jnp.mean(centred * centred, axis=-1, keepdims=True))
    return centred * lax.rsqrt(variance + 1e-06) * (1.0 + scale_vec[:, None, :]) + shift_vec[:, None, :]

def embed_time(step_ids):
    half_width = D // 2
    frequency = jnp.exp(-math.log(10000.0) * jnp.arange(half_width, dtype=jnp.float32) / half_width)
    angles = step_ids.astype(jnp.float32)[:, None] * frequency[None, :]
    return jnp.concatenate([jnp.cos(angles), jnp.sin(angles)], axis=-1)

def block(block_in, cond, weights):
    qkv_weight, qv_bias, proj_weight, proj_bias, up_projection_weight, up_bias, down_projection_weight, down_bias, ada_weight, ada_bias = weights
    lat_count = block_in.shape[0]
    seq_len = block_in.shape[1]
    silu_cond = low(jax.nn.silu(cond))
    ada_out = low_back(matmul(silu_cond, ada_weight) + ada_bias)
    shift_attn, scale_attn, gate_attn, shift_mlp, scale_mlp, gate_mlp = jnp.split(ada_out, 6, axis=-1)
    attn_in = low(normalize(block_in, shift_attn, scale_attn))
    proj_qkv = matmul(attn_in, qkv_weight)
    factor = HEAD_DIM ** (-0.5)
    queries = low(low_back(proj_qkv[..., :D] + qv_bias[:D]) * factor)
    key_rows = low(low_back(proj_qkv[..., D:2 * D]))
    value_rows = low(low_back(proj_qkv[..., 2 * D:] + qv_bias[D:]))
    queries = queries.reshape(lat_count, seq_len, HEADS, HEAD_DIM)
    key_rows = key_rows.reshape(lat_count, seq_len, HEADS, HEAD_DIM)
    value_rows = value_rows.reshape(lat_count, seq_len, HEADS, HEAD_DIM)
    scores = low_back(jnp.einsum('lqhd,lkhd->lhqk', queries, key_rows, precision=precise))
    attn_probs = low(jax.nn.softmax(scores, axis=-1))
    attn_mixed = jnp.einsum('lhqk,lkhd->lqhd', attn_probs, value_rows, precision=precise)
    attn_mixed = low_back(low(attn_mixed.reshape(lat_count, seq_len, D)))
    attended = low_back(matmul(attn_mixed, proj_weight) + proj_bias)
    resid_mid = block_in + gate_attn[:, None, :] * attended
    feedforward_input = low(normalize(resid_mid, shift_mlp, scale_mlp))
    hidden = low_back(matmul(feedforward_input, up_projection_weight) + up_bias)
    gelu_activation = low(jax.nn.gelu(hidden, approximate=True))
    branch = low_back(matmul(gelu_activation, down_projection_weight) + down_bias)
    return resid_mid + gate_mlp[:, None, :] * branch

def two_blocks(x_float, perturb, table_full, weights, time_embed, class_ids):
    cond = time_embed + table_full[class_ids]
    first_block = tuple((weight_all[0] for weight_all in weights))
    second_block = tuple((weight_all[1] for weight_all in weights))
    out_first = low(block(x_float, cond, first_block))
    out_second = low(block(low_back(out_first + perturb), cond, second_block))
    return (out_first, out_second)

def reference(inputs, cotangent, timesteps, labels, class_table, qkv_weight, qv_bias, proj_weight, proj_bias, up_projection_weight, up_bias, down_projection_weight, down_bias, ada_weight, ada_bias):
    weights = tuple((weight_arg.astype(jnp.float32) for weight_arg in (qkv_weight, qv_bias, proj_weight, proj_bias, up_projection_weight, up_bias, down_projection_weight, down_bias, ada_weight, ada_bias)))
    table_full = class_table.astype(jnp.float32)
    group_size = math.gcd(LATENTS, 16)
    group_count = MICRO * LATENTS // group_size
    x_groups = inputs.reshape(group_count, group_size, SEQ, D)
    cot_groups = cotangent.reshape(group_count, group_size, SEQ, D)
    step_groups = timesteps.reshape(group_count, group_size)
    class_groups = labels.reshape(group_count, group_size)

    def one_group(totals, group_item):
        x_rows, cot_rows, step_ids, class_ids = group_item
        time_embed = embed_time(step_ids)
        perturb = jnp.zeros((group_size, SEQ, D), jnp.float32)

        def run_blocks(x_float, perturb_in, table_in, weight_in):
            return two_blocks(x_float, perturb_in, table_in, weight_in, time_embed, class_ids)
        (out_first, out_second), pull_back = jax.vjp(run_blocks, x_rows.astype(jnp.float32), perturb, table_full, weights)
        grad_input, grad_perturb, grad_table, grad_weights = pull_back((jnp.zeros_like(out_first), cot_rows.astype(jnp.float32)))
        table_total, weight_totals = totals
        new_totals = (table_total + grad_table, tuple((total_part + extra_part for total_part, extra_part in zip(weight_totals, grad_weights))))
        return (new_totals, (out_first.astype(jnp.bfloat16), out_second.astype(jnp.bfloat16), grad_input, grad_perturb))
    initial = (jnp.zeros_like(table_full), tuple((jnp.zeros_like(weight_all) for weight_all in weights)))
    (table_grad, grad_weights), (firsts, seconds, grads_first, grads_second) = lax.scan(one_group, initial, (x_groups, cot_groups, step_groups, class_groups))
    block_outputs = jnp.stack([firsts.reshape(MICRO, LATENTS, SEQ, D), seconds.reshape(MICRO, LATENTS, SEQ, D)])
    input_grads = jnp.stack([grads_first.reshape(MICRO, LATENTS, SEQ, D), grads_second.reshape(MICRO, LATENTS, SEQ, D)])
    return (block_outputs, input_grads, table_grad, grad_weights[0], grad_weights[1], grad_weights[2], grad_weights[3], grad_weights[4], grad_weights[5], grad_weights[6], grad_weights[7], grad_weights[8], grad_weights[9])
```

```python
import functools
import math

import jax
import jax.numpy as jnp
from jax import lax
from jax.experimental import pallas as pl
from jax.experimental.pallas import tpu as pltpu
from jax.sharding import PartitionSpec as P

S = "section"
Z = "shard"
R = "replica"
ALL = (S, Z, R)
BF = jnp.bfloat16
F32 = jnp.float32
D = 1152
HEAD_DIM = 72
HEADS = 16
FF = 4608
HALF = 2304
ROWS = 288
PIECE = 144
NZ = 4
SHARDS = (1, 2, 3)
VMEM_LIMIT = 50 * 1024 * 1024


def move(value, to):
    ns, nz, nr = (lax.axis_size(a) for a in ALL)
    pairs = []
    for s in range(ns):
        for z in range(nz):
            for r in range(nr):
                there = to(s, z, r)
                if there is not None:
                    a, b, c = there
                    pairs.append(((s * nz + z) * nr + r, (a * nz + b) * nr + c))
    return lax.ppermute(value, ALL, pairs)


def swap(value):
    return move(value, lambda s, z, r: (1 - s, z, r))


def to_core(value, core):
    return move(value, lambda s, z, r: (core, z, r) if s != core else None)


def zshift(value, by=1):
    nz = lax.axis_size(Z)
    return move(value, lambda s, z, r: (s, (z + by) % nz, r))


def cross(value, bit):
    return move(value, lambda s, z, r: (s, z, r ^ bit))


def place():
    return lax.axis_index(S), lax.axis_index(Z), lax.rem(lax.axis_index(R), 4)


def assemble_kernel(block, by_rows, mine, other, *refs):
    own, far, out, sems = refs[:4], refs[4:8], refs[8], refs[9]
    c, z, r = place()
    copies = []
    height = D if by_rows else ROWS
    target = out.at[pl.ds(z * height, height), :]
    shard_mine = pltpu.make_async_copy(mine, target, sems.at[0])
    shard_other = pltpu.make_async_copy(other, target, sems.at[0])

    @pl.when(c == block)
    def _():
        shard_mine.start()

    @pl.when(c != block)
    def _():
        shard_other.start()

    for side, group in ((0, own), (1, far)):
        core = c if side == 0 else 1 - c
        for m in range(4):
            low = lax.rem(r + m, 2)
            high = lax.rem(r // 2 + m // 2, 2)
            for k in SHARDS:
                zp = lax.rem(z + NZ - k, NZ)
                if by_rows:
                    row = zp * D + core * (D // 2) + (high * 2 + low) * PIECE
                    spot = out.at[pl.ds(row, PIECE), :]
                else:
                    row = zp * ROWS + low * PIECE
                    col = pl.multiple_of((core * 2 + high) * D, D)
                    spot = out.at[pl.ds(row, PIECE), pl.ds(col, D)]
                n = 1 + (side * 4 + m) * 3 + k - 1
                copies.append(pltpu.make_async_copy(group[m].at[k - 1], spot, sems.at[n]))
    for copy in copies:
        copy.start()
    shard_mine.wait()
    for copy in copies:
        copy.wait()


def assemble(block, by_rows, mine, other, own, far):
    shape = (FF, D) if by_rows else (D, FF)
    return pl.pallas_call(
        functools.partial(assemble_kernel, block, by_rows),
        out_shape=jax.ShapeDtypeStruct(shape, BF),
        in_specs=[pl.BlockSpec(memory_space=pl.ANY)] * 10,
        out_specs=pl.BlockSpec(memory_space=pl.ANY),
        scratch_shapes=[pltpu.SemaphoreType.DMA((25,))],
        cost_estimate=pl.CostEstimate(flops=0, bytes_accessed=4 * D * FF, transcendentals=0),
    )(mine, other, *own, *far)


def own_piece(block, by_rows, mine, other):
    c, z, r = place()
    if by_rows:
        start = ((c * 4 + r) * PIECE, 0)
    else:
        start = (lax.rem(r, 2) * PIECE, (c * 2 + r // 2) * D)
    part = [lax.dynamic_slice(w, start, (PIECE, D)) for w in (mine, other)]
    return jnp.where(c == block, part[0], part[1])


def gather_item(block, by_rows, mine, other, x_first):
    first = own_piece(block, by_rows, mine, other)
    ring = []
    value = first
    for _ in SHARDS:
        value = zshift(value)
        ring.append(value)
    p0 = jnp.stack(ring)
    p1 = cross(p0, 1)
    p2 = cross(p0, 2)
    p3 = cross(p1, 2) if x_first else cross(p2, 1)
    own = (p0, p1, p2, p3)
    far = tuple(swap(p) for p in own)
    return assemble(block, by_rows, mine, other, own, far)


def wgrad_kernel(kind, lo, lx, ro, rx, g0, g1, g2, g3, acc):
    c, z, r = place()
    outs = (g0, g1, g2, g3)
    for g in range(2):
        u = lax.rem(g + r // 2, 2)
        if kind == 0:
            left = c * u
        elif kind == 1:
            left = 0
        else:
            left = u
        cols = pl.ds(0, D) if kind == 2 else pl.ds(pl.multiple_of(u * D, D), D)
        acc[...] = jnp.dot(lo[left], ro[:, cols], preferred_element_type=F32) + jnp.dot(
            lx[left], rx[:, cols], preferred_element_type=F32
        )
        for par in range(2):

            @pl.when(lax.rem(r, 2) == par)
            def _():
                for zp in range(NZ):
                    k = lax.rem(z - zp + NZ, NZ)
                    for h in range(2):
                        row = (zp * 2 + h) * PIECE
                        outs[g * 2 + (h ^ par)][k] = acc[row : row + PIECE, :].astype(BF)


def wgrad(kind, lo, lx, ro, rx):
    part = jax.ShapeDtypeStruct((NZ, PIECE, D), BF)
    return pl.pallas_call(
        functools.partial(wgrad_kernel, kind),
        out_shape=(part,) * 4,
        in_specs=[pl.BlockSpec(memory_space=pltpu.VMEM)] * 4,
        out_specs=(pl.BlockSpec(memory_space=pltpu.VMEM),) * 4,
        scratch_shapes=[pltpu.VMEM((D, D), F32)],
        compiler_params=pltpu.CompilerParams(vmem_limit_bytes=VMEM_LIMIT),
        cost_estimate=pl.CostEstimate(
            flops=2 * 512 * D * HALF, bytes_accessed=2 * D * HALF + 6 * 512 * D, transcendentals=0
        ),
    )(lo, lx, ro, rx)


def plus(a, b):
    return (a.astype(F32) + b.astype(F32)).astype(BF)


def reduce_item(parts, x_first):
    g0, g1, g2, g3 = parts
    if x_first:
        k0 = plus(g0, cross(g1, 1))
        k2 = plus(g2, cross(g3, 1))
        full = plus(k0, cross(k2, 2))
    else:
        k0 = plus(g0, cross(g2, 2))
        k1 = plus(g1, cross(g3, 2))
        full = plus(k0, cross(k1, 1))
    value = zshift(full[1])
    value = zshift(plus(value, full[2]))
    value = zshift(plus(value, full[3]))
    value = plus(value, full[0])
    bit = 4
    while bit < lax.axis_size(R):
        value = plus(value, cross(value, bit))
        bit *= 2
    p1 = cross(value, 1)
    p2 = cross(value, 2)
    p3 = cross(p1, 2) if x_first else cross(p2, 1)
    return (value, p1, p2, p3)


def finish_kernel(by_rows, *refs):
    sets = refs[:8], refs[8:16]
    outs = refs[16:]
    acc = outs[-1] if len(outs) == 3 else outs[0]
    c, z, r = place()
    for block in range(2):

        @pl.when(c == block)
        def _():
            for side in range(2):
                core = c if side == 0 else 1 - c
                for m in range(4):
                    low = lax.rem(r + m, 2)
                    high = lax.rem(r // 2 + m // 2, 2)
                    piece = sets[block][side * 4 + m][...].astype(F32)
                    if by_rows:
                        row = core * (D // 2) + (high * 2 + low) * PIECE
                        acc[pl.ds(row, PIECE), :] = piece
                    else:
                        col = pl.multiple_of((core * 2 + high) * D, D)
                        acc[pl.ds(low * PIECE, PIECE), pl.ds(col, D)] = piece

    if len(outs) == 3:
        outs[0][...] = acc[:, : 3 * D]
        outs[1][...] = acc[:, 3 * D :]


def finish(kind, parts):
    by_rows = kind == 2
    if kind == 0:
        shapes = ((ROWS, 3 * D), (ROWS, D))
        scratch = [pltpu.VMEM((ROWS, FF), F32)]
    else:
        shapes = ((D, D),) if by_rows else ((ROWS, FF),)
        scratch = []
    return pl.pallas_call(
        functools.partial(finish_kernel, by_rows),
        out_shape=tuple(jax.ShapeDtypeStruct(s, F32) for s in shapes),
        in_specs=[pl.BlockSpec(memory_space=pltpu.VMEM)] * 16,
        out_specs=(pl.BlockSpec(memory_space=pltpu.VMEM),) * len(shapes),
        scratch_shapes=scratch,
        compiler_params=pltpu.CompilerParams(vmem_limit_bytes=VMEM_LIMIT),
        cost_estimate=pl.CostEstimate(flops=0, bytes_accessed=8 * ROWS * FF, transcendentals=0),
    )(*parts[0], *parts[1])


def standard(v):
    mean = jnp.mean(v, axis=-1, keepdims=True)
    centred = v - mean
    rstd = lax.rsqrt(jnp.mean(centred * centred, axis=-1, keepdims=True) + 1e-06)
    return centred * rstd, rstd


def mm(a, b):
    return jnp.dot(a, b, preferred_element_type=F32)


def mmt(a, b):
    return lax.dot_general(a, b, (((1,), (1,)), ((), ())), preferred_element_type=F32)


def heads(v):
    return v.reshape(v.shape[0], HEADS, HEAD_DIM).transpose(1, 0, 2)


def joined(v):
    return v.transpose(1, 0, 2).reshape(v.shape[1], D)


def batched(a, b, ca, cb):
    return lax.dot_general(a, b, (((ca,), (cb,)), ((0,), (0,))), preferred_element_type=F32)


def forward(x, ada, weights, biases):
    wa, wu, wd = weights
    qv_bias, proj_bias, up_bias, down_bias = biases
    sh_a, sc_a, g_a, sh_m, sc_m, g_m = ada
    xf = x.astype(F32)
    n1, r1 = standard(xf)
    attn_in = (n1 * (1.0 + sc_a) + sh_a).astype(BF)
    proj = mm(attn_in, wa[:, : 3 * D])
    q = heads(((proj[:, :D] + qv_bias[:D]) * HEAD_DIM**-0.5).astype(BF))
    k = heads(proj[:, D : 2 * D].astype(BF))
    v = heads((proj[:, 2 * D :] + qv_bias[D:]).astype(BF))
    soft = jax.nn.softmax(batched(q, k, 2, 2), axis=-1)
    probs = soft.astype(BF)
    mixed = joined(batched(probs, v, 2, 1)).astype(BF)
    attended = mm(mixed, wa[:, 3 * D :]) + proj_bias
    mid = xf + g_a * attended
    n2, r2 = standard(mid)
    mlp_in = (n2 * (1.0 + sc_m) + sh_m).astype(BF)
    hidden = mm(mlp_in, wu) + up_bias
    act = jax.nn.gelu(hidden, approximate=True).astype(BF)
    branch = mm(act, wd) + down_bias
    out = (mid + g_m * branch).astype(BF)
    kept = (n1, r1, attn_in, q, k, v, soft, probs, mixed, attended, n2, r2, mlp_in, hidden, act, branch)
    return out, kept


def rows_sum(v):
    return jnp.sum(v.astype(F32), axis=0)


def norm_back(g, n, rstd):
    return rstd * (
        g - jnp.mean(g, axis=-1, keepdims=True) - n * jnp.mean(g * n, axis=-1, keepdims=True)
    )


def backward(grad, ada, weights, kept):
    wa, wu, wd = weights
    sh_a, sc_a, g_a, sh_m, sc_m, g_m = ada
    (n1, r1, attn_in, q, k, v, soft, probs, mixed, attended, n2, r2, mlp_in, hidden, act, branch) = kept
    d_branch = (g_m * grad).astype(BF)
    d_gate_m = rows_sum(grad * branch)
    d_act = mmt(d_branch, wd)
    _, back = jax.vjp(functools.partial(jax.nn.gelu, approximate=True), hidden)
    d_hidden = back(d_act)[0].astype(BF)
    d_mlp_in = mmt(d_hidden, wu)
    d_shift_m = rows_sum(d_mlp_in)
    d_scale_m = rows_sum(d_mlp_in * n2)
    d_mid = grad + norm_back(d_mlp_in * (1.0 + sc_m), n2, r2)
    d_att = (g_a * d_mid).astype(BF)
    d_gate_a = rows_sum(d_mid * attended)
    d_mixed = heads(mmt(d_att, wa[:, 3 * D :]).astype(BF))
    d_v = batched(probs, d_mixed, 1, 1).astype(BF)
    d_probs = batched(d_mixed, v, 2, 2)
    d_s = (soft * (d_probs - jnp.sum(d_probs * soft, axis=-1, keepdims=True))).astype(BF)
    d_q = (batched(d_s, k, 2, 1) * HEAD_DIM**-0.5).astype(BF)
    d_k = batched(d_s, q, 1, 1).astype(BF)
    d_qkv = jnp.concatenate([joined(d_q), joined(d_k), joined(d_v)], axis=-1)
    d_attn_in = mmt(d_qkv, wa[:, : 3 * D])
    d_shift_a = rows_sum(d_attn_in)
    d_scale_a = rows_sum(d_attn_in * n1)
    d_x = d_mid + norm_back(d_attn_in * (1.0 + sc_a), n1, r1)
    d_ada = jnp.concatenate(
        [d_shift_a, d_scale_a, d_gate_a, d_shift_m, d_scale_m, d_gate_m]
    ).astype(BF)
    sums_qkv = rows_sum(d_qkv)
    sums = jnp.concatenate(
        [sums_qkv[:D], sums_qkv[2 * D :], rows_sum(d_att), rows_sum(d_hidden), rows_sum(d_branch)]
    )
    lefts = (jnp.stack([attn_in.T, mixed.T]), mlp_in.T[None], act.T)
    rights = (jnp.concatenate([d_qkv, d_att], axis=-1), d_hidden, d_branch)
    return d_x, d_ada, sums, lefts, rights


def item_grads(kind, left, right):
    c = lax.axis_index(S)
    if kind == 2:
        groups = left.reshape(NZ, 2, 2, ROWS, left.shape[-1])

        def part(core):
            half = lax.dynamic_index_in_dim(groups, core, 1, keepdims=False)
            return half.transpose(1, 0, 2, 3).reshape(2, D, left.shape[-1])

        lo, lx = part(c), swap(part(1 - c))
        ro, rx = right, swap(right)
    else:
        lo, lx = left, swap(left)
        ro = lax.dynamic_slice_in_dim(right, c * HALF, HALF, 1)
        rx = swap(lax.dynamic_slice_in_dim(right, (1 - c) * HALF, HALF, 1))
    return wgrad(kind, lo, lx, ro, rx)


def embed_time(steps):
    half = D // 2
    freq = jnp.exp(-math.log(10000.0) * jnp.arange(half, dtype=F32) / half)
    angles = steps.astype(F32)[:, None] * freq[None, :]
    return jnp.concatenate([jnp.cos(angles), jnp.sin(angles)], axis=-1)


def by_shard(rel):
    z = lax.axis_index(Z)
    order = lax.rem(z - jnp.arange(NZ) + NZ, NZ)
    return jnp.take(rel, order, axis=0)


def per_device(
    inputs,
    cotangent,
    timesteps,
    labels,
    class_table,
    qkv_weight,
    qv_bias,
    proj_weight,
    proj_bias,
    up_weight,
    up_bias,
    down_weight,
    down_bias,
    ada_weight,
    ada_bias,
):
    c = lax.axis_index(S)
    z = lax.axis_index(Z)
    is_first = c == 0

    ids = jnp.concatenate([timesteps, labels], axis=1)
    ids_rel = jnp.stack([ids] + [zshift(ids, k) for k in SHARDS])
    vectors = jnp.concatenate(
        [qv_bias[0], proj_bias[0], up_bias[0], down_bias[0], ada_bias[0]]
    )[None]
    vec_rel = jnp.concatenate([vectors] + [zshift(vectors, k) for k in SHARDS])
    vec_mine = by_shard(vec_rel).astype(F32)
    vec_other = by_shard(swap(vec_rel)).astype(F32)

    def cond_of(steps, classes):
        return embed_time(steps) + jnp.take(class_table, classes, axis=0).astype(F32)

    cond_rel = cond_of(ids_rel[..., 0].reshape(-1), ids_rel[..., 1].reshape(-1))
    silu_rel = jax.nn.silu(cond_rel).astype(BF)
    rows_rel = lax.dynamic_slice_in_dim(silu_rel, z * ROWS, ROWS, 1)
    partial_rel = mm(rows_rel, ada_weight[0]).reshape(NZ, 2, -1)
    ada_sum = partial_rel[0]
    for k in SHARDS:
        ada_sum = ada_sum + zshift(partial_rel[k], -k)
    lengths = (qv_bias.shape[1], proj_bias.shape[1], up_bias.shape[1], down_bias.shape[1], ada_bias.shape[1])

    def split_vectors(vec):
        out = []
        at = 0
        for n in lengths:
            out.append(vec[:, at : at + n].reshape(-1))
            at += n
        return out

    mine_split = split_vectors(vec_mine)
    other_split = split_vectors(vec_other)
    ada_sum = ada_sum + mine_split[4][None]
    ada_keep = lax.dynamic_index_in_dim(ada_sum, c, 0, keepdims=False)
    ada_got = swap(lax.dynamic_index_in_dim(ada_sum, 1 - c, 0, keepdims=False))
    adas = []
    biases = []
    for block in range(2):
        here = c == block
        adas.append(jnp.split(jnp.where(here, ada_keep, ada_got), 6))
        biases.append(
            [jnp.where(here, a, b) for a, b in zip(mine_split[:4], other_split[:4])]
        )

    mine = (
        jnp.concatenate([qkv_weight[0], proj_weight[0]], axis=1),
        up_weight[0],
        down_weight[0],
    )
    other = tuple(swap(w) for w in mine)
    weights = []
    for block in range(2):
        weights.append(
            [
                gather_item(block, kind == 2, mine[kind], other[kind], (block + kind) % 2 == 0)
                for kind in range(3)
            ]
        )

    x = lax.dynamic_index_in_dim(inputs, c, 0, keepdims=False)[0]
    cot = lax.dynamic_index_in_dim(cotangent, c, 0, keepdims=False)[0]
    y0, kept0 = forward(x, adas[0], weights[0], biases[0])
    y1, kept1 = forward(y0, adas[1], weights[1], biases[1])
    dx1, dada1, sums1, lefts1, rights1 = backward(cot.astype(F32), adas[1], weights[1], kept1)
    dx1 = dx1.astype(BF)
    reduced = {}
    for kind in (2, 1, 0):
        reduced[1, kind] = reduce_item(item_grads(kind, lefts1[kind], rights1[kind]), kind % 2 == 0)
    dx0, dada0, sums0, lefts0, rights0 = backward(dx1.astype(F32), adas[0], weights[0], kept0)
    for kind in (2, 1, 0):
        reduced[0, kind] = reduce_item(item_grads(kind, lefts0[kind], rights0[kind]), kind % 2 == 1)
    grads = []
    for kind in range(3):
        parts = []
        for block in range(2):
            own = reduced[block, kind]
            parts.append(own + tuple(to_core(p, block) for p in own))
        grads.append(finish(kind, parts))
    (qkv_grad, proj_grad), (up_grad,), (down_grad,) = grads

    def both_micros(v0, v1):
        keep = jnp.where(is_first, v0, v1)
        got = swap(jnp.where(is_first, v1, v0))
        return jnp.stack([jnp.where(is_first, keep, got), jnp.where(is_first, got, keep)])

    block_outputs = both_micros(y0, y1)[None, :, None]
    input_grads = both_micros(dx0, dx1.astype(F32))[None, :, None]

    sums = lax.psum(jnp.stack([sums0, sums1]), ALL)
    sums = lax.dynamic_index_in_dim(sums, c, 0, keepdims=False)

    def own_slice(vec):
        n = vec.shape[0] // NZ
        return lax.dynamic_slice_in_dim(vec, z * n, n, 0)[None]

    qv_bias_grad = own_slice(sums[: 2 * D])
    proj_bias_grad = own_slice(sums[2 * D : 3 * D])
    up_bias_grad = own_slice(sums[3 * D : 3 * D + FF])
    down_bias_grad = own_slice(sums[3 * D + FF :])

    ids_all = lax.all_gather(ids, (Z, R), axis=1, tiled=False).reshape(2, -1, 2)
    cond_all = cond_of(ids_all[..., 0].reshape(-1), ids_all[..., 1].reshape(-1))
    labels_all = ids_all[..., 1].reshape(-1)
    dada_all = lax.all_gather(jnp.stack([dada0, dada1]), ALL, axis=0, tiled=False)
    dada_own = lax.dynamic_index_in_dim(dada_all, c, 1, keepdims=False)
    cond_rows = lax.dynamic_slice_in_dim(cond_all, z * ROWS, ROWS, 1)
    silu_rows = jax.nn.silu(cond_rows).astype(BF)
    ada_grad = lax.dot_general(
        silu_rows, dada_own, (((0,), (0,)), ((), ())), preferred_element_type=F32
    )
    ada_bias_grad = own_slice(rows_sum(dada_own))
    d_silu = mmt(dada_own, ada_weight[0])
    _, silu_back = jax.vjp(jax.nn.silu, cond_rows)
    d_cond = silu_back(d_silu)[0]
    d_cond = d_cond + swap(d_cond)
    cond_rel_all = jnp.stack([d_cond] + [zshift(d_cond, k) for k in SHARDS])
    d_cond_all = by_shard(cond_rel_all).transpose(1, 0, 2).reshape(-1, D)
    row_count = class_table.shape[0] // (2 * NZ)
    row_ids = (c * NZ + z) * row_count + jnp.arange(row_count, dtype=jnp.int32)
    owner = (row_ids[:, None] == labels_all[None, :]).astype(F32)
    table_grad = jnp.dot(owner, d_cond_all, precision=lax.Precision.HIGHEST)

    return (
        block_outputs,
        input_grads,
        table_grad,
        qkv_grad[None],
        qv_bias_grad,
        proj_grad[None],
        proj_bias_grad,
        up_grad[None],
        up_bias_grad,
        down_grad[None],
        down_bias_grad,
        ada_grad[None],
        ada_bias_grad,
    )


def solution(mesh):
    rows = P(None, (Z, R), None, None)
    matrix = P(S, Z, None)
    vector = P(S, Z)
    pair = P(None, (Z, R))
    in_specs = (rows, rows, pair, pair, P()) + (matrix, vector) * 5
    acts = P(S, None, (Z, R), None, None)
    out_specs = (acts, acts, P((S, Z), None)) + (matrix, vector) * 5
    return jax.shard_map(
        per_device, mesh=mesh, in_specs=in_specs, out_specs=out_specs, check_vma=False
    )
```

```python
import functools
import math

import jax
import jax.numpy as jnp
from jax import lax
from jax.experimental import pallas as pl
from jax.experimental.pallas import tpu as pltpu
from jax.sharding import PartitionSpec as P

S = "section"
Z = "shard"
R = "replica"
ALL = (S, Z, R)
BF = jnp.bfloat16
F32 = jnp.float32
D = 1152
HEAD_DIM = 72
HEADS = 16
FF = 4608
HALF = 2304
ROWS = 288
PIECE = 144
NZ = 4
SHARDS = (1, 2, 3)
VMEM_LIMIT = 50 * 1024 * 1024


def move(value, to):
    ns, nz, nr = (lax.axis_size(a) for a in ALL)
    pairs = []
    for s in range(ns):
        for z in range(nz):
            for r in range(nr):
                there = to(s, z, r)
                if there is not None:
                    a, b, c = there
                    pairs.append(((s * nz + z) * nr + r, (a * nz + b) * nr + c))
    return lax.ppermute(value, ALL, pairs)


def swap(value):
    return move(value, lambda s, z, r: (1 - s, z, r))


def to_core(value, core):
    return move(value, lambda s, z, r: (core, z, r) if s != core else None)


def zshift(value, by=1):
    nz = lax.axis_size(Z)
    return move(value, lambda s, z, r: (s, (z + by) % nz, r))


def trade(value):
    return lax.all_to_all(value, Z, split_axis=0, concat_axis=0, tiled=True)


def along_z(value):
    return trade(jnp.stack([value] * NZ))


def cross(value, bit):
    return move(value, lambda s, z, r: (s, z, r ^ bit))


def place():
    return lax.axis_index(S), lax.axis_index(Z), lax.rem(lax.axis_index(R), 4)


ANYWHERE = pl.BlockSpec(memory_space=pl.ANY)
INSIDE = pl.BlockSpec(memory_space=pltpu.VMEM)
PARAMS = pltpu.CompilerParams(vmem_limit_bytes=VMEM_LIMIT)
ONE = jax.ShapeDtypeStruct((PIECE, D), BF)


def cost(nbytes, flops=0):
    return pl.CostEstimate(flops=flops, bytes_accessed=nbytes, transcendentals=0)


def fence(arrays, after):
    n = len(arrays)
    return pl.pallas_call(
        lambda *refs: None,
        out_shape=tuple(jax.ShapeDtypeStruct(a.shape, a.dtype) for a in arrays),
        in_specs=[ANYWHERE] * (n + 1),
        out_specs=(ANYWHERE,) * n,
        input_output_aliases={i: i for i in range(n)},
        cost_estimate=cost(0),
    )(*arrays, after)


def stack_kernel(every, _, out):
    z = lax.axis_index(Z)
    for i in range(every.shape[1]):
        for k in SHARDS:
            out[i, k - 1] = every[lax.rem(z + NZ - k, NZ), i]


def stacked(every, after):
    n = every.shape[1]
    return pl.pallas_call(
        stack_kernel,
        out_shape=jax.ShapeDtypeStruct((n, 3, PIECE, D), BF),
        in_specs=[INSIDE, ANYWHERE],
        out_specs=INSIDE,
        compiler_params=PARAMS,
        cost_estimate=cost(12 * n * PIECE * D),
    )(every, after)


def join_kernel(*refs):
    out = refs[-1]
    for i in range(out.shape[0]):
        out[i] = refs[i][...]


def joined(parts, after):
    n = len(parts)
    return pl.pallas_call(
        join_kernel,
        out_shape=jax.ShapeDtypeStruct((n, PIECE, D), BF),
        in_specs=[INSIDE] * n + [ANYWHERE],
        out_specs=INSIDE,
        compiler_params=PARAMS,
        cost_estimate=cost(4 * n * PIECE * D),
    )(*parts, after)


def plus_kernel(n, *refs):
    outs = refs[2 * n + 1 :]
    for i in range(n):
        for j in range(2):
            whole = refs[i][j].astype(F32) + refs[n + i][j].astype(F32)
            outs[2 * i + j][...] = whole.astype(BF)


def plus(a, b, after):
    n = len(a)
    shapes = [jax.ShapeDtypeStruct(v.shape[1:], BF) for v in a for _ in range(2)]
    return pl.pallas_call(
        functools.partial(plus_kernel, n),
        out_shape=tuple(shapes),
        in_specs=[INSIDE] * (2 * n) + [ANYWHERE],
        out_specs=(INSIDE,) * (2 * n),
        compiler_params=PARAMS,
        cost_estimate=cost(6 * sum(v.size for v in a)),
    )(*a, *b, after)


def merge_kernel(*refs):
    out = refs[-1]
    for i in range(2):
        whole = refs[i][...].astype(F32) + refs[2 + i][...].astype(F32)
        out[2 * i : 2 * i + 2] = whole.astype(BF)


def merged(a, b, after):
    return pl.pallas_call(
        merge_kernel,
        out_shape=jax.ShapeDtypeStruct((NZ, PIECE, D), BF),
        in_specs=[INSIDE] * 4 + [ANYWHERE],
        out_specs=INSIDE,
        compiler_params=PARAMS,
        cost_estimate=cost(12 * NZ * PIECE * D),
    )(*a, *b, after)


def sum_kernel(parts, _, out):
    whole = parts[0].astype(F32)
    for i in range(1, parts.shape[0]):
        whole = whole + parts[i].astype(F32)
    out[...] = whole.astype(BF)


def summed(parts, after):
    n = parts.shape[0]
    return pl.pallas_call(
        sum_kernel,
        out_shape=ONE,
        in_specs=[INSIDE, ANYWHERE],
        out_specs=INSIDE,
        compiler_params=PARAMS,
        cost_estimate=cost(2 * (n + 1) * PIECE * D),
    )(parts, after)


def pair_kernel(own, far, _, out):
    c = lax.axis_index(S)
    for core in range(2):

        @pl.when(c == core)
        def _():
            for i in range(3):
                out[i, core] = own[i]
                out[i, 1 - core] = far[i]


def paired(own, far, after):
    return pl.pallas_call(
        pair_kernel,
        out_shape=jax.ShapeDtypeStruct((3, 2, PIECE, D), BF),
        in_specs=[INSIDE] * 2 + [ANYWHERE],
        out_specs=INSIDE,
        compiler_params=PARAMS,
        cost_estimate=cost(24 * PIECE * D),
    )(own, far, after)


def chosen(block, mine, other, act):
    c = lax.axis_index(S)

    @pl.when(c == block)
    def _():
        act(mine)

    @pl.when(c != block)
    def _():
        act(other)


def arrays_of(kind):
    return 2 if kind == 0 else 1


def extract_kernel(items, *refs):
    out, sems = refs[-2:]
    c, z, r = place()
    unit = c * 2 + r // 2
    at = 0
    for i, (block, kind) in enumerate(items):
        n = arrays_of(kind)
        mine, other = refs[at : at + n], refs[at + n : at + 2 * n]
        at += 2 * n

        def copy(source):
            for j in range(NZ):
                pltpu.make_async_copy(source, out.at[j, i], sems.at[j, i]).start()

        def act(source):
            if kind == 2:
                copy(source[0].at[pl.ds((c * 4 + r) * PIECE, PIECE), :])
                return
            height = pl.ds(lax.rem(r, 2) * PIECE, PIECE)

            def take(ref, index):
                cols = pl.ds(pl.multiple_of(index * D, D), D)
                copy(ref.at[height, cols])

            if kind == 1:
                take(source[0], unit)
                return

            @pl.when(unit == 3)
            def _():
                take(source[1], 0)

            @pl.when(unit != 3)
            def _():
                take(source[0], unit)

        chosen(block, mine, other, act)
    for i in range(len(items)):
        for j in range(NZ):
            pltpu.make_async_copy(out.at[j, i], out.at[j, i], sems.at[j, i]).wait()


def extract(items, mine, other, after):
    n = len(items)
    operands = []
    for _, kind in items:
        operands += [*mine[kind], *other[kind]]
    return pl.pallas_call(
        functools.partial(extract_kernel, items),
        out_shape=jax.ShapeDtypeStruct((NZ, n, PIECE, D), BF),
        in_specs=[ANYWHERE] * (len(operands) + 1),
        out_specs=INSIDE,
        scratch_shapes=[pltpu.SemaphoreType.DMA((NZ, n))],
        compiler_params=PARAMS,
        cost_estimate=cost(4 * n * PIECE * D),
    )(*operands, after)


def weight_copies(block, kind, index, mine, other, own, far, out, sems):
    n = arrays_of(kind)
    c, z, r = place()
    copies = []
    height = D if kind == 2 else ROWS
    rows = pl.ds(z * height, height)
    if kind == 0:
        targets = (out.at[rows, pl.ds(0, 3 * D)], out.at[rows, pl.ds(3 * D, D)])
    else:
        targets = (out.at[rows, :],)

    def act(source):
        for i in range(n):
            pltpu.make_async_copy(source[i], targets[i], sems.at[i]).start()

    chosen(block, mine, other, act)
    for side, group in ((0, own), (1, far)):
        core = c if side == 0 else 1 - c
        for m in range(4):
            low = lax.rem(r + m, 2)
            high = lax.rem(r // 2 + m // 2, 2)
            for k in SHARDS:
                zp = lax.rem(z + NZ - k, NZ)
                if kind == 2:
                    row = zp * D + core * (D // 2) + (high * 2 + low) * PIECE
                    spot = out.at[pl.ds(row, PIECE), :]
                else:
                    row = zp * ROWS + low * PIECE
                    col = pl.multiple_of((core * 2 + high) * D, D)
                    spot = out.at[pl.ds(row, PIECE), pl.ds(col, D)]
                if m < 3:
                    piece = group[m].at[index, k - 1]
                elif own[0].shape[0] == 2:
                    piece = group[3 + index].at[0, k - 1]
                elif k == 1:
                    piece = group[3].at[0, 0]
                else:
                    piece = group[4].at[0, k - 2]
                sem = sems.at[2 + (side * 4 + m) * 3 + k - 1]
                copies.append(pltpu.make_async_copy(piece, spot, sem))
    for copy in copies:
        copy.start()

    def wait():
        for i in range(n):
            pltpu.make_async_copy(mine[i], targets[i], sems.at[i]).wait()
        for copy in copies:
            copy.wait()

    return wait


GROUPS = (((0, 0),), ((0, 1), (0, 2)), ((1, 0),), ((1, 1), (1, 2)))


class Gatherer:
    def __init__(self, mine, other, after):
        self.mine = mine
        self.other = other
        self.after = after
        self.state = {}

    def extract(self, g):
        self.after = extract(GROUPS[g], self.mine, self.other, self.after)
        self.state[g] = trade(self.after)

    def stack(self, g):
        p0 = stacked(self.state[g], self.after)
        self.after = p0
        self.state[g] = p0, cross(p0, 1), cross(p0, 2), swap(p0)

    def onward(self, g):
        p0, p1, p2, f0 = self.state[g]
        p1, p2 = fence((p1, p2), self.after)
        self.after = p1
        part = (p2[:1], p1[1:]) if len(GROUPS[g]) == 2 else (p2[:, :1], p1[:, 1:])
        p3 = cross(part[0], 1), cross(part[1], 2)
        self.state[g] = (p0, p1, p2), p3, (f0, swap(p1), swap(p2))

    def share(self, g):
        own, p3, far = self.state[g]
        p3 = fence(p3, self.after)
        self.after = p3[0]
        self.state[g] = own + tuple(p3), far + tuple(swap(p) for p in p3)

    def operands(self, g):
        own, far = self.state[g]
        shards = []
        for _, kind in GROUPS[g]:
            shards += [*self.mine[kind], *self.other[kind]]
        return (*own, *far, *shards, self.after)


def tdot(a, b):
    return lax.dot_general(a, b, (((0,), (0,)), ((), ())), preferred_element_type=F32)


def wgrad_kernel(kind, *refs):
    n = 4
    ins = refs[:n]
    keep_x, send_x, keep_y, send_y, acc = refs[n + 1 :]
    c, z, r = place()
    for g in range(2):
        u = lax.rem(g + r // 2, 2)
        if kind == 2:
            lo, lx, ro, rx = ins
            for zp in range(NZ):
                rows = pl.ds(pl.multiple_of(u * ROWS, ROWS), ROWS)
                acc[zp * ROWS : (zp + 1) * ROWS, :] = jnp.dot(
                    lo[zp, c, rows, :], ro[...], preferred_element_type=F32
                ) + jnp.dot(lx[zp, rows, :], rx[...], preferred_element_type=F32)
        else:
            ro, rx = ins[-2:]
            mine = pl.ds(pl.multiple_of(c * HALF + u * D, D), D)
            other = pl.ds(pl.multiple_of(u * D, D), D)

            def product(lo, lx):
                acc[...] = tdot(lo[...], ro[:, mine]) + tdot(lx[...], rx[:, other])

            if kind == 1:
                product(ins[0], ins[1])
            else:

                @pl.when(c * u == 0)
                def _():
                    product(ins[0].at[0], ins[1].at[0])

                @pl.when(c * u == 1)
                def _():
                    product(ins[0].at[1], ins[1].at[1])

        for par in range(2):

            @pl.when(lax.rem(r, 2) == par)
            def _():
                for zp in range(NZ):
                    for h in range(2):
                        start = (zp * 2 + h) * PIECE
                        piece = acc[start : start + PIECE, :].astype(BF)
                        low = h ^ par
                        if zp < 2:
                            (send_x if low else keep_x)[g, zp] = piece
                        else:
                            (send_y if g else keep_y)[low, zp - 2] = piece


def wgrad(kind, operands, after):
    part = jax.ShapeDtypeStruct((2, 2, PIECE, D), BF)
    return pl.pallas_call(
        functools.partial(wgrad_kernel, kind),
        out_shape=(part,) * 4,
        in_specs=[INSIDE] * len(operands) + [ANYWHERE],
        out_specs=(INSIDE,) * 4,
        scratch_shapes=[pltpu.VMEM((D, D), F32)],
        compiler_params=PARAMS,
        cost_estimate=cost(2 * D * HALF + 6 * 512 * D, 2 * 512 * D * HALF),
    )(*operands, after)


def finish_kernel(block, kind, n, *refs):
    pieces = refs[:5]
    acc, sems = refs[-2:]
    outs = refs[-2 - n : -2]
    c, z, r = place()

    @pl.when(c == block)
    def _():
        for core in range(2):
            for m in range(4):
                low = lax.rem(r + m, 2)
                high = lax.rem(r // 2 + m // 2, 2)
                if m < 3:
                    piece = pieces[m][kind, core]
                else:
                    flat = kind * 2 + core
                    piece = pieces[3][flat] if flat < 3 else pieces[4][flat - 3]
                piece = piece.astype(F32)
                if kind == 2:
                    row = pl.multiple_of(core * (D // 2) + (high * 2 + low) * PIECE, PIECE)
                    acc[pl.ds(row, PIECE), :] = piece
                else:
                    row = pl.multiple_of(low * PIECE, PIECE)
                    col = pl.multiple_of((core * 2 + high) * D, D)
                    acc[pl.ds(row, PIECE), pl.ds(col, D)] = piece
        if n == 2:
            parts = (acc.at[:, pl.ds(0, 3 * D)], acc.at[:, pl.ds(3 * D, D)])
        else:
            parts = (acc,)
        copies = [pltpu.make_async_copy(parts[i], outs[i], sems.at[i]) for i in range(n)]
        for copy in copies:
            copy.start()
        for copy in copies:
            copy.wait()


def finish(block, kind, pieces, before, after):
    if kind == 0:
        shapes = ((ROWS, 3 * D), (ROWS, D))
    else:
        shapes = ((D, D),) if kind == 2 else ((ROWS, FF),)
    n = len(shapes)
    return pl.pallas_call(
        functools.partial(finish_kernel, block, kind, n),
        out_shape=tuple(jax.ShapeDtypeStruct(s, F32) for s in shapes),
        in_specs=[INSIDE] * 5 + [ANYWHERE] * (1 + len(before)),
        out_specs=(ANYWHERE,) * n,
        scratch_shapes=[
            pltpu.VMEM((D, D) if kind == 2 else (ROWS, FF), F32),
            pltpu.SemaphoreType.DMA((2,)),
        ],
        input_output_aliases={6 + i: i for i in range(len(before))},
        compiler_params=PARAMS,
        cost_estimate=cost(8 * ROWS * FF),
    )(*pieces, after, *before)


def on_core(value, bit, core):
    return move(value, lambda s, z, r: (s, z, r ^ bit) if s == core else None)


class Reducer:
    def __init__(self, after):
        self.after = after
        self.items = []
        self.state = []
        self.own = {}
        self.ready = {}
        self.results = {0: (), 1: (), 2: ()}

    def begin(self, block, kind, operands):
        keep_x, send_x, keep_y, send_y = wgrad(kind, operands, self.after)
        self.after = keep_x
        self.items.append((block, kind))
        self.state.append(((keep_x, keep_y), (cross(send_x, 1), cross(send_y, 2))))

    def first(self, i):
        xk, xs, yk, ys = plus(*self.state[i], self.after)
        self.after = xk
        self.state[i] = (xk, yk), (cross(xs, 2), cross(ys, 1))

    def second(self, i):
        f = merged(*self.state[i], self.after)
        self.after = f
        self.state[i] = trade(f)

    def third(self, i):
        v = summed(self.state[i], self.after)
        bit = 4
        while bit < lax.axis_size(R):
            v = summed(jnp.stack([v, cross(v, bit)]), v)
            bit *= 2
        self.after = v
        self.own[self.items[i]] = v

    def unite(self, block):
        own = joined([self.own[block, kind] for kind in range(3)], self.after)
        self.after = own
        self.ready[block] = own, to_core(own, block)

    def spread(self, block):
        p0 = paired(*self.ready[block], self.after)
        self.after = p0
        self.ready[block] = p0, on_core(p0, 1, block), on_core(p0, 2, block)

    def spread_on(self, block):
        p0, p1, p2 = self.ready[block]
        p1, p2 = fence((p1, p2), self.after)
        self.after = p1
        flat1, flat2 = p1.reshape(6, PIECE, D), p2.reshape(6, PIECE, D)
        pa, pb = on_core(flat2[:3], 1, block), on_core(flat1[3:], 2, block)
        self.ready[block] = p0, p1, p2, pa, pb

    def finish(self, block):
        for kind in range(3):
            out = finish(block, kind, self.ready[block], self.results[kind], self.after)
            self.results[kind] = out
            self.after = out[0]


def standard(v):
    mean = jnp.mean(v, axis=-1, keepdims=True)
    centred = v - mean
    rstd = lax.rsqrt(jnp.mean(centred * centred, axis=-1, keepdims=True) + 1e-06)
    return centred * rstd, rstd


def mm(a, b):
    return jnp.dot(a, b, preferred_element_type=F32)


def mmt(a, b):
    return lax.dot_general(a, b, (((1,), (1,)), ((), ())), preferred_element_type=F32)


def head_cols(h, base=0):
    return slice(base + h * HEAD_DIM, base + (h + 1) * HEAD_DIM)


def softmax_of(q, k):
    scores = mmt(q, k)
    e = jnp.exp(scores - jnp.max(scores, axis=-1, keepdims=True))
    return e / jnp.sum(e, axis=-1, keepdims=True)


def shape_of(dtype, *dims):
    return jax.ShapeDtypeStruct(dims, dtype)


def row(ref, i):
    return ref[i : i + 1, :]


def attend_kernel(block, *refs):
    x, ada, qv_bias, proj_bias = refs[:4]
    own, far, mine, other = refs[4:9], refs[9:14], refs[14:16], refs[16:18]
    w_out, sides, q, k, v, attended, mid, mlp_in, w, sems = refs[19:]
    attn_in, mixed = sides.at[0], sides.at[1]
    wait = weight_copies(block, 0, 0, mine, other, own, far, w, sems)
    xf = x[...].astype(F32)
    n1, _ = standard(xf)
    attn_in[...] = (n1 * (1.0 + row(ada, 1)) + row(ada, 0)).astype(BF)
    wait()
    keep = pltpu.make_async_copy(w, w_out, sems.at[26])
    keep.start()
    q[...] = ((mm(attn_in[...], w[:, :D]) + qv_bias[:, :D]) * HEAD_DIM**-0.5).astype(BF)
    k[...] = mm(attn_in[...], w[:, D : 2 * D]).astype(BF)
    v[...] = (mm(attn_in[...], w[:, 2 * D : 3 * D]) + qv_bias[:, D:]).astype(BF)
    for h in range(HEADS):
        cols = head_cols(h)
        probs = softmax_of(q[:, cols], k[:, cols]).astype(BF)
        mixed[:, cols] = mm(probs, v[:, cols]).astype(BF)
    attended[...] = mm(mixed[...], w[:, 3 * D :]) + proj_bias[...]
    mid[...] = x[...].astype(F32) + row(ada, 2) * attended[...]
    n2, _ = standard(mid[...])
    mlp_in[...] = (n2 * (1.0 + row(ada, 4)) + row(ada, 3)).astype(BF)
    keep.wait()


def attend(block, x, ada, biases, gathered):
    t = x.shape[0]
    low = shape_of(BF, t, D)
    high = shape_of(F32, t, D)
    return pl.pallas_call(
        functools.partial(attend_kernel, block),
        out_shape=(shape_of(BF, D, FF), shape_of(BF, 2, t, D), low, low, low, high, high, low),
        in_specs=[INSIDE] * 4 + [ANYWHERE] * 15,
        out_specs=(ANYWHERE,) + (INSIDE,) * 7,
        scratch_shapes=[pltpu.VMEM((D, FF), BF), pltpu.SemaphoreType.DMA((27,))],
        compiler_params=PARAMS,
        cost_estimate=cost(4 * D * FF, 2 * t * D * FF),
    )(x, ada, biases[0], biases[1], *gathered)


def mlp_kernel(block, *refs):
    mid, mlp_in, ada, up_bias, down_bias = refs[:5]
    own, far = refs[5:10], refs[10:15]
    wu_out, wd_out, hidden, act_t, branch, y, wu, wd, act, sems_u, sems_d = refs[20:]
    wait_u = weight_copies(block, 1, 0, refs[15:16], refs[16:17], own, far, wu, sems_u)
    wait_d = weight_copies(block, 2, 1, refs[17:18], refs[18:19], own, far, wd, sems_d)
    wait_u()
    keep_u = pltpu.make_async_copy(wu, wu_out, sems_u.at[26])
    keep_u.start()
    for j in range(4):
        cols = slice(j * D, (j + 1) * D)
        hid = mm(mlp_in[...], wu[:, cols]) + up_bias[:, cols]
        hidden[:, cols] = hid
        part = jax.nn.gelu(hid, approximate=True)
        act[:, cols] = part.astype(BF)
        act_t[cols, :] = part.T.astype(BF)
    wait_d()
    keep_d = pltpu.make_async_copy(wd, wd_out, sems_d.at[26])
    keep_d.start()
    branch[...] = mm(act[...], wd[...]) + down_bias[...]
    y[...] = (mid[...] + row(ada, 5) * branch[...]).astype(BF)
    keep_u.wait()
    keep_d.wait()


def mlp(block, mid, mlp_in, ada, biases, gathered):
    t = mid.shape[0]
    return pl.pallas_call(
        functools.partial(mlp_kernel, block),
        out_shape=(
            shape_of(BF, D, FF),
            shape_of(BF, FF, D),
            shape_of(F32, t, FF),
            shape_of(BF, FF, t),
            shape_of(F32, t, D),
            shape_of(BF, t, D),
        ),
        in_specs=[INSIDE] * 5 + [ANYWHERE] * 15,
        out_specs=(ANYWHERE,) * 2 + (INSIDE,) * 4,
        scratch_shapes=[
            pltpu.VMEM((D, FF), BF),
            pltpu.VMEM((FF, D), BF),
            pltpu.VMEM((t, FF), BF),
            pltpu.SemaphoreType.DMA((27,)),
            pltpu.SemaphoreType.DMA((27,)),
        ],
        compiler_params=PARAMS,
        cost_estimate=cost(8 * D * FF, 4 * t * D * FF),
    )(mid, mlp_in, ada, biases[2], biases[3], *gathered)


def column_sum(v):
    return jnp.sum(v, axis=0, keepdims=True)


def norm_back(g, n, rstd):
    return rstd * (
        g - jnp.mean(g, axis=-1, keepdims=True) - n * jnp.mean(g * n, axis=-1, keepdims=True)
    )


def gelu_slope(v):
    c = math.sqrt(2.0 / math.pi)
    t = jnp.tanh(c * (v + 0.044715 * v * v * v))
    return 0.5 * (1.0 + t) + 0.5 * v * (1.0 - t * t) * (c * (1.0 + 3.0 * 0.044715 * v * v))


def mlp_back_kernel(*refs):
    grad, d_branch, ada, mid, attended, hidden, branch, wu_in, wd_in = refs[:9]
    d_hidden, d_mid, d_att, stats, hidden_sum, wu, wd, acc, sems = refs[10:]
    copies = []
    for j in range(4):
        part = slice(j * D, (j + 1) * D)
        down = pltpu.make_async_copy(wd_in.at[part, :], wd.at[part, :], sems.at[2 * j])
        up = pltpu.make_async_copy(wu_in.at[:, part], wu.at[:, part], sems.at[2 * j + 1])
        copies.append((down, up))
    for down, up in copies:
        down.start()
        up.start()
    stats[2:3, :] = column_sum(grad[...].astype(F32) * branch[...])
    stats[4:5, :] = column_sum(d_branch[...].astype(F32))
    for j in range(4):
        part = slice(j * D, (j + 1) * D)
        copies[j][0].wait()
        d_act = mmt(d_branch[...], wd[part, :])
        d_hid = (d_act * gelu_slope(hidden[:, part])).astype(BF)
        d_hidden[:, part] = d_hid
        hidden_sum[:, part] = column_sum(d_hid.astype(F32))
        copies[j][1].wait()
        product = mmt(d_hidden[:, part], wu[:, part])
        if j == 0:
            acc[...] = product
        else:
            acc[...] += product
    n2, r2 = standard(mid[...])
    stats[0:1, :] = column_sum(acc[...])
    stats[1:2, :] = column_sum(acc[...] * n2)
    whole = grad[...].astype(F32) + norm_back(acc[...] * (1.0 + row(ada, 4)), n2, r2)
    d_mid[...] = whole
    d_att[...] = (row(ada, 2) * whole).astype(BF)
    stats[3:4, :] = column_sum(whole * attended[...])
    stats[5:6, :] = column_sum(d_att[...].astype(F32))


def mlp_back(grad, d_branch, ada, mid, attended, hidden, branch, wu, wd, after):
    t = grad.shape[0]
    return pl.pallas_call(
        mlp_back_kernel,
        out_shape=(
            shape_of(BF, t, FF),
            shape_of(F32, t, D),
            shape_of(BF, t, D),
            shape_of(F32, 8, D),
            shape_of(F32, 1, FF),
        ),
        in_specs=[INSIDE] * 7 + [ANYWHERE] * 3,
        out_specs=(INSIDE,) * 5,
        scratch_shapes=[
            pltpu.VMEM((D, FF), BF),
            pltpu.VMEM((FF, D), BF),
            pltpu.VMEM((t, D), F32),
            pltpu.SemaphoreType.DMA((8,)),
        ],
        compiler_params=PARAMS,
        cost_estimate=cost(5 * D * FF, 4 * t * D * FF),
    )(grad, d_branch, ada, mid, attended, hidden, branch, wu, wd, after)


def attend_back_kernel(*refs):
    x, d_mid, d_att, ada, q_ref, k_ref, v_ref, w_in = refs[:8]
    out, d_x, d_x_low, stats, w, mixed, sem = refs[9:]
    copies = [
        pltpu.make_async_copy(w_in.at[:, 3 * D :], w.at[:, 3 * D :], sem.at[0]),
        pltpu.make_async_copy(w_in.at[:, : 3 * D], w.at[:, : 3 * D], sem.at[1]),
    ]
    for copy in copies:
        copy.start()
    copies[0].wait()
    mixed[...] = mmt(d_att[...], w[:, 3 * D :]).astype(BF)
    for h in range(HEADS):
        cols = head_cols(h)
        q, k, v, dm = (ref[:, cols] for ref in (q_ref, k_ref, v_ref, mixed))
        soft = softmax_of(q, k)
        d_probs = mmt(dm, v)
        inner = jnp.sum(d_probs * soft, axis=-1, keepdims=True)
        d_s = (soft * (d_probs - inner)).astype(BF)
        out[:, cols] = (mm(d_s, k) * HEAD_DIM**-0.5).astype(BF)
        out[:, head_cols(h, D)] = tdot(d_s, q).astype(BF)
        out[:, head_cols(h, 2 * D)] = tdot(soft.astype(BF), dm).astype(BF)
    out[:, 3 * D :] = d_att[...]
    stats[2:3, :] = column_sum(out[:, :D].astype(F32))
    stats[3:4, :] = column_sum(out[:, 2 * D : 3 * D].astype(F32))
    copies[1].wait()
    d_in = mmt(out[:, :D], w[:, :D])
    d_in += mmt(out[:, D : 2 * D], w[:, D : 2 * D])
    d_in += mmt(out[:, 2 * D : 3 * D], w[:, 2 * D : 3 * D])
    n1, r1 = standard(x[...].astype(F32))
    stats[0:1, :] = column_sum(d_in)
    stats[1:2, :] = column_sum(d_in * n1)
    whole = d_mid[...] + norm_back(d_in * (1.0 + row(ada, 1)), n1, r1)
    d_x[...] = whole
    d_x_low[...] = whole.astype(BF)


def attend_back(x, d_mid, d_att, ada, q, k, v, wa, after):
    t = x.shape[0]
    return pl.pallas_call(
        attend_back_kernel,
        out_shape=(
            shape_of(BF, t, FF),
            shape_of(F32, t, D),
            shape_of(BF, t, D),
            shape_of(F32, 8, D),
        ),
        in_specs=[INSIDE] * 7 + [ANYWHERE] * 2,
        out_specs=(INSIDE,) * 4,
        scratch_shapes=[
            pltpu.VMEM((D, FF), BF),
            pltpu.VMEM((t, D), BF),
            pltpu.SemaphoreType.DMA((2,)),
        ],
        compiler_params=PARAMS,
        cost_estimate=cost(3 * D * FF, 2 * t * D * FF),
    )(x, d_mid, d_att, ada, q, k, v, wa, after)


def far_half(right):
    c = lax.axis_index(S)
    return swap(lax.dynamic_slice_in_dim(right, (1 - c) * HALF, HALF, 1))


def far_rows(act_t):
    c = lax.axis_index(S)
    return swap(lax.dynamic_index_in_dim(act_t, 1 - c, 1, keepdims=False))


def rows_sum(v):
    return jnp.sum(v.astype(F32), axis=0)


def embed_time(steps):
    half = D // 2
    freq = jnp.exp(-math.log(10000.0) * jnp.arange(half, dtype=F32) / half)
    angles = steps.astype(F32)[:, None] * freq[None, :]
    return jnp.concatenate([jnp.cos(angles), jnp.sin(angles)], axis=-1)


def everywhere(value):
    nr = lax.axis_size(R)
    out = along_z(value)[None]
    bit = 1
    while bit < nr:
        out = jnp.concatenate([out, cross(out, bit)])
        bit *= 2
    return jnp.take(out, lax.axis_index(R) ^ jnp.arange(nr), axis=0)


def total(value):
    value = value + swap(value)
    for bit in (1, 2):
        value = value + move(value, lambda s, z, r: (s, z ^ bit, r))
    bit = 1
    while bit < lax.axis_size(R):
        value = value + cross(value, bit)
        bit *= 2
    return value


def per_device(
    inputs,
    cotangent,
    timesteps,
    labels,
    class_table,
    qkv_weight,
    qv_bias,
    proj_weight,
    proj_bias,
    up_weight,
    up_bias,
    down_weight,
    down_bias,
    ada_weight,
    ada_bias,
):
    c = lax.axis_index(S)
    z = lax.axis_index(Z)
    is_first = c == 0

    ids = jnp.concatenate([timesteps, labels], axis=1)
    vectors = [v[0].astype(F32) for v in (qv_bias, proj_bias, up_bias, down_bias, ada_bias)]
    small = along_z(jnp.concatenate(vectors + [ids.reshape(-1).astype(F32)]))
    ids_z = small[:, -4:].astype(jnp.int32).reshape(NZ, 2, 2)
    vec_mine = small[:, :-4]
    vec_other = swap(vec_mine)

    def cond_of(steps, classes):
        return embed_time(steps) + jnp.take(class_table, classes, axis=0).astype(F32)

    cond_z = cond_of(ids_z[..., 0].reshape(-1), ids_z[..., 1].reshape(-1))
    silu_z = jax.nn.silu(cond_z).astype(BF)
    rows_z = lax.dynamic_slice_in_dim(silu_z, z * ROWS, ROWS, 1)
    partial = mm(rows_z, ada_weight[0]).reshape(NZ, 2, -1)
    ada_sum = jnp.sum(trade(partial), axis=0)
    lengths = (qv_bias.shape[1], proj_bias.shape[1], up_bias.shape[1], down_bias.shape[1], ada_bias.shape[1])

    def split_vectors(vec):
        out = []
        at = 0
        for n in lengths:
            out.append(vec[:, at : at + n].reshape(-1))
            at += n
        return out

    mine_split = split_vectors(vec_mine)
    other_split = split_vectors(vec_other)
    ada_sum = ada_sum + mine_split[4][None]
    ada_keep = lax.dynamic_index_in_dim(ada_sum, c, 0, keepdims=False)
    ada_got = swap(lax.dynamic_index_in_dim(ada_sum, 1 - c, 0, keepdims=False))
    adas = []
    biases = []
    for block in range(2):
        here = c == block
        adas.append(jnp.where(here, ada_keep, ada_got).reshape(6, D))
        biases.append(
            [jnp.where(here, a, b)[None] for a, b in zip(mine_split[:4], other_split[:4])]
        )

    mine = ((qkv_weight[0], proj_weight[0]), (up_weight[0],), (down_weight[0],))
    other = tuple(tuple(swap(w) for w in group) for group in mine)
    gatherer = Gatherer(mine, other, qkv_weight[0])
    x = lax.dynamic_index_in_dim(inputs, c, 0, keepdims=False)[0]
    cot = lax.dynamic_index_in_dim(cotangent, c, 0, keepdims=False)[0]
    kept = []
    kept_mlp = []

    def run_attend(block, value):
        got = attend(block, value, adas[block], biases[block], gatherer.operands(2 * block))
        gatherer.after = got[-1]
        kept.append(got)

    def run_mlp(block):
        mid, mlp_in = kept[block][-2:]
        got = mlp(block, mid, mlp_in, adas[block], biases[block], gatherer.operands(2 * block + 1))
        gatherer.after = got[-1]
        act_t = got[3].reshape(NZ, 2, D // 2, -1)
        kept_mlp.append(got[:3] + (act_t,) + got[4:] + (far_rows(act_t), swap(mlp_in)))

    gatherer.extract(0)
    gatherer.stack(0)
    gatherer.extract(1)
    gatherer.onward(0)
    gatherer.share(0)
    run_attend(0, x)
    gatherer.stack(1)
    gatherer.extract(2)
    gatherer.stack(2)
    gatherer.extract(3)
    gatherer.onward(1)
    gatherer.onward(2)
    gatherer.share(1)
    run_mlp(0)
    y0 = kept_mlp[0][5]
    gatherer.share(2)
    gatherer.stack(3)
    run_attend(1, y0)
    gatherer.onward(3)
    gatherer.share(3)
    run_mlp(1)
    y1 = kept_mlp[1][5]

    reducer = Reducer(y1)

    def run_mlp_back(block, grad):
        ada = adas[block]
        d_branch = (ada[5:] * grad.astype(F32)).astype(BF)
        far_branch = swap(d_branch)
        attended, mid, mlp_in = kept[block][-3:]
        wu, wd, hidden, act_t, branch, _, far_act, far_in = kept_mlp[block]
        got = mlp_back(grad, d_branch, ada, mid, attended, hidden, branch, wu, wd, reducer.after)
        d_hidden = got[0]
        reducer.after = d_hidden
        far_hidden = far_half(d_hidden)
        reducer.begin(block, 2, (act_t, far_act, d_branch, far_branch))
        reducer.begin(block, 1, (mlp_in, far_in, d_hidden, far_hidden))
        return got

    def run_attend_back(block, value, back):
        wa, sides, q, k, v = kept[block][:5]
        _, d_mid, d_att, stats_m, hidden_sum = back
        far = swap(sides)
        d_all, d_x, d_x_low, stats_a = attend_back(
            value, d_mid, d_att, adas[block], q, k, v, wa, reducer.after
        )
        reducer.after = d_x_low
        d_ada = jnp.concatenate(
            [stats_a[0], stats_a[1], stats_m[3], stats_m[0], stats_m[1], stats_m[2]]
        ).astype(BF)
        sums = jnp.concatenate([stats_a[2], stats_a[3], stats_m[5], hidden_sum[0], stats_m[4]])
        operands = (sides, far, d_all, far_half(d_all))
        return d_x, d_x_low, d_ada, sums, operands

    back1 = run_mlp_back(1, cot)
    _, dx1, dada1, sums1, operands1 = run_attend_back(1, y0, back1)
    reducer.first(0)
    reducer.begin(1, 0, operands1)
    back0 = run_mlp_back(0, dx1)
    reducer.first(1)
    reducer.second(0)
    dx0, _, dada0, sums0, operands0 = run_attend_back(0, x, back0)
    reducer.first(2)
    reducer.begin(0, 0, operands0)
    reducer.second(1)
    reducer.third(0)
    reducer.first(3)
    reducer.second(2)
    reducer.third(1)
    reducer.first(4)
    reducer.second(3)
    reducer.third(2)
    reducer.unite(1)
    reducer.first(5)
    reducer.spread(1)
    reducer.second(4)
    reducer.third(3)
    reducer.spread_on(1)
    reducer.second(5)
    reducer.third(4)
    reducer.finish(1)
    reducer.third(5)
    reducer.unite(0)
    reducer.spread(0)
    reducer.spread_on(0)
    reducer.finish(0)
    (qkv_grad, proj_grad), (up_grad,), (down_grad,) = (reducer.results[k] for k in range(3))

    def both_micros(v0, v1):
        keep = jnp.where(is_first, v0, v1)
        got = swap(jnp.where(is_first, v1, v0))
        return jnp.stack([jnp.where(is_first, keep, got), jnp.where(is_first, got, keep)])

    block_outputs = both_micros(y0, y1)[None, :, None]
    input_grads = both_micros(dx0, dx1.astype(F32))[None, :, None]

    sums = total(jnp.stack([sums0, sums1]))
    sums = lax.dynamic_index_in_dim(sums, c, 0, keepdims=False)

    def own_slice(vec):
        n = vec.shape[0] // NZ
        return lax.dynamic_slice_in_dim(vec, z * n, n, 0)[None]

    qv_bias_grad = own_slice(sums[: 2 * D])
    proj_bias_grad = own_slice(sums[2 * D : 3 * D])
    up_bias_grad = own_slice(sums[3 * D : 3 * D + FF])
    down_bias_grad = own_slice(sums[3 * D + FF :])

    ids_all = ids_z[None]
    bit = 1
    while bit < lax.axis_size(R):
        ids_all = jnp.concatenate([ids_all, cross(ids_all, bit)])
        bit *= 2
    ids_all = jnp.take(ids_all, lax.axis_index(R) ^ jnp.arange(lax.axis_size(R)), axis=0)
    ids_all = ids_all.reshape(-1, 2)
    cond_all = cond_of(ids_all[:, 0], ids_all[:, 1])
    labels_all = ids_all[:, 1]
    dada_own = everywhere(both_micros(dada0, dada1)).reshape(-1, 6 * D)
    cond_rows = lax.dynamic_slice_in_dim(cond_all, z * ROWS, ROWS, 1)
    silu_rows = jax.nn.silu(cond_rows).astype(BF)
    ada_grad = lax.dot_general(
        silu_rows, dada_own, (((0,), (0,)), ((), ())), preferred_element_type=F32
    )
    ada_bias_grad = own_slice(rows_sum(dada_own))
    d_silu = mmt(dada_own, ada_weight[0])
    _, silu_back = jax.vjp(jax.nn.silu, cond_rows)
    d_cond = silu_back(d_silu)[0]
    d_cond = d_cond + swap(d_cond)
    d_cond_all = along_z(d_cond).transpose(1, 0, 2).reshape(-1, D)
    row_count = class_table.shape[0] // (2 * NZ)
    row_ids = (c * NZ + z) * row_count + jnp.arange(row_count, dtype=jnp.int32)
    owner = (row_ids[:, None] == labels_all[None, :]).astype(F32)
    table_grad = jnp.dot(owner, d_cond_all, precision=lax.Precision.HIGHEST)

    return (
        block_outputs,
        input_grads,
        table_grad,
        qkv_grad[None],
        qv_bias_grad,
        proj_grad[None],
        proj_bias_grad,
        up_grad[None],
        up_bias_grad,
        down_grad[None],
        down_bias_grad,
        ada_grad[None],
        ada_bias_grad,
    )


def solution(mesh):
    rows = P(None, (Z, R), None, None)
    matrix = P(S, Z, None)
    vector = P(S, Z)
    pair = P(None, (Z, R))
    in_specs = (rows, rows, pair, pair, P()) + (matrix, vector) * 5
    acts = P(S, None, (Z, R), None, None)
    out_specs = (acts, acts, P((S, Z), None)) + (matrix, vector) * 5
    return jax.shard_map(
        per_device, mesh=mesh, in_specs=in_specs, out_specs=out_specs, check_vma=False
    )
```

```python
import functools
import math

import jax
import jax.numpy as jnp
from jax import lax
from jax.experimental import pallas as pl
from jax.experimental.pallas import tpu as pltpu
from jax.sharding import PartitionSpec as P

S = "section"
Z = "shard"
R = "replica"
ALL = (S, Z, R)
BF = jnp.bfloat16
F32 = jnp.float32
D = 1152
HEAD_DIM = 72
HEADS = 16
FF = 4608
HALF = 2304
ROWS = 288
PIECE = 144
NZ = 4
SHARDS = (1, 2, 3)
VMEM_LIMIT = 50 * 1024 * 1024


def move(value, to):
    ns, nz, nr = (lax.axis_size(a) for a in ALL)
    pairs = []
    for s in range(ns):
        for z in range(nz):
            for r in range(nr):
                there = to(s, z, r)
                if there is not None:
                    a, b, c = there
                    pairs.append(((s * nz + z) * nr + r, (a * nz + b) * nr + c))
    return lax.ppermute(value, ALL, pairs)


def swap(value):
    return move(value, lambda s, z, r: (1 - s, z, r))


def to_core(value, core):
    return move(value, lambda s, z, r: (core, z, r) if s != core else None)


def zshift(value, by=1):
    nz = lax.axis_size(Z)
    return move(value, lambda s, z, r: (s, (z + by) % nz, r))


def trade(value):
    return lax.all_to_all(value, Z, split_axis=0, concat_axis=0, tiled=True)


def along_z(value):
    return trade(jnp.stack([value] * NZ))


def cross(value, bit):
    return move(value, lambda s, z, r: (s, z, r ^ bit))


def place():
    return lax.axis_index(S), lax.axis_index(Z), lax.rem(lax.axis_index(R), 4)


ANYWHERE = pl.BlockSpec(memory_space=pl.ANY)
INSIDE = pl.BlockSpec(memory_space=pltpu.VMEM)
PARAMS = pltpu.CompilerParams(vmem_limit_bytes=VMEM_LIMIT)
ONE = jax.ShapeDtypeStruct((PIECE, D), BF)


def cost(nbytes, flops=0):
    return pl.CostEstimate(flops=0, bytes_accessed=0, transcendentals=0)


def fence(arrays, after):
    n = len(arrays)
    return pl.pallas_call(
        lambda *refs: None,
        out_shape=tuple(jax.ShapeDtypeStruct(a.shape, a.dtype) for a in arrays),
        in_specs=[ANYWHERE] * (n + 1),
        out_specs=(ANYWHERE,) * n,
        input_output_aliases={i: i for i in range(n)},
        cost_estimate=cost(0),
    )(*arrays, after)


def stack_kernel(every, _, out):
    z = lax.axis_index(Z)
    for i in range(every.shape[1]):
        for k in SHARDS:
            out[i, k - 1] = every[lax.rem(z + NZ - k, NZ), i]


def stacked(every, after):
    n = every.shape[1]
    return pl.pallas_call(
        stack_kernel,
        out_shape=jax.ShapeDtypeStruct((n, 3, PIECE, D), BF),
        in_specs=[INSIDE, ANYWHERE],
        out_specs=INSIDE,
        compiler_params=PARAMS,
        cost_estimate=cost(12 * n * PIECE * D),
    )(every, after)


def join_kernel(*refs):
    out = refs[-1]
    for i in range(out.shape[0]):
        out[i] = refs[i][...]


def joined(parts, after):
    n = len(parts)
    return pl.pallas_call(
        join_kernel,
        out_shape=jax.ShapeDtypeStruct((n, PIECE, D), BF),
        in_specs=[INSIDE] * n + [ANYWHERE],
        out_specs=INSIDE,
        compiler_params=PARAMS,
        cost_estimate=cost(4 * n * PIECE * D),
    )(*parts, after)


def plus_kernel(n, *refs):
    outs = refs[2 * n + 1 :]
    for i in range(n):
        for j in range(2):
            whole = refs[i][j].astype(F32) + refs[n + i][j].astype(F32)
            outs[2 * i + j][...] = whole.astype(BF)


def plus(a, b, after):
    n = len(a)
    shapes = [jax.ShapeDtypeStruct(v.shape[1:], BF) for v in a for _ in range(2)]
    return pl.pallas_call(
        functools.partial(plus_kernel, n),
        out_shape=tuple(shapes),
        in_specs=[INSIDE] * (2 * n) + [ANYWHERE],
        out_specs=(INSIDE,) * (2 * n),
        compiler_params=PARAMS,
        cost_estimate=cost(6 * sum(v.size for v in a)),
    )(*a, *b, after)


def merge_kernel(*refs):
    out = refs[-1]
    for i in range(2):
        whole = refs[i][...].astype(F32) + refs[2 + i][...].astype(F32)
        out[2 * i : 2 * i + 2] = whole.astype(BF)


def merged(a, b, after):
    return pl.pallas_call(
        merge_kernel,
        out_shape=jax.ShapeDtypeStruct((NZ, PIECE, D), BF),
        in_specs=[INSIDE] * 4 + [ANYWHERE],
        out_specs=INSIDE,
        compiler_params=PARAMS,
        cost_estimate=cost(12 * NZ * PIECE * D),
    )(*a, *b, after)


def sum_kernel(parts, _, out):
    whole = parts[0].astype(F32)
    for i in range(1, parts.shape[0]):
        whole = whole + parts[i].astype(F32)
    out[...] = whole.astype(BF)


def summed(parts, after):
    n = parts.shape[0]
    return pl.pallas_call(
        sum_kernel,
        out_shape=ONE,
        in_specs=[INSIDE, ANYWHERE],
        out_specs=INSIDE,
        compiler_params=PARAMS,
        cost_estimate=cost(2 * (n + 1) * PIECE * D),
    )(parts, after)


def pair_kernel(own, far, _, out):
    c = lax.axis_index(S)
    for core in range(2):

        @pl.when(c == core)
        def _():
            for i in range(3):
                out[i, core] = own[i]
                out[i, 1 - core] = far[i]


def paired(own, far, after):
    return pl.pallas_call(
        pair_kernel,
        out_shape=jax.ShapeDtypeStruct((3, 2, PIECE, D), BF),
        in_specs=[INSIDE] * 2 + [ANYWHERE],
        out_specs=INSIDE,
        compiler_params=PARAMS,
        cost_estimate=cost(24 * PIECE * D),
    )(own, far, after)


def chosen(block, mine, other, act):
    c = lax.axis_index(S)

    @pl.when(c == block)
    def _():
        act(mine)

    @pl.when(c != block)
    def _():
        act(other)


def arrays_of(kind):
    return 2 if kind == 0 else 1


def extract_kernel(items, *refs):
    out, sems = refs[-2:]
    c, z, r = place()
    unit = c * 2 + r // 2
    at = 0
    for i, (block, kind) in enumerate(items):
        n = arrays_of(kind)
        mine, other = refs[at : at + n], refs[at + n : at + 2 * n]
        at += 2 * n

        def copy(source):
            pltpu.make_async_copy(source, out.at[i], sems.at[i]).start()

        def act(source):
            if kind == 2:
                copy(source[0].at[pl.ds((c * 4 + r) * PIECE, PIECE), :])
                return
            height = pl.ds(lax.rem(r, 2) * PIECE, PIECE)

            def take(ref, index):
                cols = pl.ds(pl.multiple_of(index * D, D), D)
                copy(ref.at[height, cols])

            if kind == 1:
                take(source[0], unit)
                return

            @pl.when(unit == 3)
            def _():
                take(source[1], 0)

            @pl.when(unit != 3)
            def _():
                take(source[0], unit)

        chosen(block, mine, other, act)
    for i in range(len(items)):
        pltpu.make_async_copy(out.at[i], out.at[i], sems.at[i]).wait()


def extract(items, mine, other, after):
    n = len(items)
    operands = []
    for _, kind in items:
        operands += [*mine[kind], *other[kind]]
    return pl.pallas_call(
        functools.partial(extract_kernel, items),
        out_shape=jax.ShapeDtypeStruct((n, PIECE, D), BF),
        in_specs=[ANYWHERE] * (len(operands) + 1),
        out_specs=INSIDE,
        scratch_shapes=[pltpu.SemaphoreType.DMA((n,))],
        compiler_params=PARAMS,
        cost_estimate=cost(4 * n * PIECE * D),
    )(*operands, after)


def weight_copies(block, kind, index, mine, other, own, far, out, sems):
    n = arrays_of(kind)
    c, z, r = place()
    copies = []
    height = D if kind == 2 else ROWS
    rows = pl.ds(z * height, height)
    if kind == 0:
        targets = (out.at[rows, pl.ds(0, 3 * D)], out.at[rows, pl.ds(3 * D, D)])
    else:
        targets = (out.at[rows, :],)

    def act(source):
        for i in range(n):
            pltpu.make_async_copy(source[i], targets[i], sems.at[i]).start()

    chosen(block, mine, other, act)
    for side, group in ((0, own), (1, far)):
        core = c if side == 0 else 1 - c
        for m in range(4):
            low = lax.rem(r + m, 2)
            high = lax.rem(r // 2 + m // 2, 2)
            for k in SHARDS:
                zp = lax.rem(z + NZ - k, NZ)
                if kind == 2:
                    row = zp * D + core * (D // 2) + (high * 2 + low) * PIECE
                    spot = out.at[pl.ds(row, PIECE), :]
                else:
                    row = zp * ROWS + low * PIECE
                    col = pl.multiple_of((core * 2 + high) * D, D)
                    spot = out.at[pl.ds(row, PIECE), pl.ds(col, D)]
                if m < 3:
                    piece = group[m].at[index, k - 1]
                elif own[0].shape[0] == 2:
                    piece = group[3 + index].at[0, k - 1]
                elif k == 1:
                    piece = group[3].at[0, 0]
                else:
                    piece = group[4].at[0, k - 2]
                sem = sems.at[2 + (side * 4 + m) * 3 + k - 1]
                copies.append(pltpu.make_async_copy(piece, spot, sem))
    for copy in copies:
        copy.start()

    def wait():
        for i in range(n):
            pltpu.make_async_copy(mine[i], targets[i], sems.at[i]).wait()
        for copy in copies:
            copy.wait()

    return wait


GROUPS = (((0, 0),), ((0, 1), (0, 2)), ((1, 0),), ((1, 1), (1, 2)))


class Gatherer:
    def __init__(self, mine, other, after):
        self.mine = mine
        self.other = other
        self.after = after
        self.state = {}

    def extract(self, g):
        self.after = extract(GROUPS[g], self.mine, self.other, self.after)
        self.state[g] = lax.all_gather(self.after, Z, axis=0, tiled=False)

    def stack(self, g):
        p0 = stacked(self.state[g], self.after)
        self.after = p0
        self.state[g] = p0, cross(p0, 1), cross(p0, 2), swap(p0)

    def onward(self, g):
        p0, p1, p2, f0 = self.state[g]
        p1, p2 = fence((p1, p2), self.after)
        self.after = p1
        part = (p2[:1], p1[1:]) if len(GROUPS[g]) == 2 else (p2[:, :1], p1[:, 1:])
        p3 = cross(part[0], 1), cross(part[1], 2)
        self.state[g] = (p0, p1, p2), p3, (f0, swap(p1), swap(p2))

    def share(self, g):
        own, p3, far = self.state[g]
        p3 = fence(p3, self.after)
        self.after = p3[0]
        self.state[g] = own + tuple(p3), far + tuple(swap(p) for p in p3)

    def hold(self, *values):
        values = fence(values, self.after)
        self.after = values[0]
        return values

    def operands(self, g):
        own, far = self.state[g]
        shards = []
        for _, kind in GROUPS[g]:
            shards += [*self.mine[kind], *self.other[kind]]
        return (*own, *far, *shards, self.after)


def tdot(a, b):
    return lax.dot_general(a, b, (((0,), (0,)), ((), ())), preferred_element_type=F32)


def wgrad_kernel(kind, *refs):
    n = 4
    ins = refs[:n]
    keep_x, send_x, keep_y, send_y, acc = refs[n + 1 :]
    c, z, r = place()
    for g in range(2):
        u = lax.rem(g + r // 2, 2)
        if kind == 2:
            lo, lx, ro, rx = ins
            for zp in range(NZ):
                rows = pl.ds(pl.multiple_of(u * ROWS, ROWS), ROWS)
                acc[zp * ROWS : (zp + 1) * ROWS, :] = jnp.dot(
                    lo[c, zp, rows, :], ro[...], preferred_element_type=F32
                ) + jnp.dot(lx[zp, rows, :], rx[...], preferred_element_type=F32)
        else:
            ro, rx = ins[-2:]
            cols = pl.ds(pl.multiple_of(u * D, D), D)

            def product(lo, lx):
                acc[...] = tdot(lo[...], ro[c, :, cols]) + tdot(lx[...], rx[:, cols])

            if kind == 1:
                product(ins[0], ins[1])
            else:

                @pl.when(c * u == 0)
                def _():
                    product(ins[0].at[0], ins[1].at[0])

                @pl.when(c * u == 1)
                def _():
                    product(ins[0].at[1], ins[1].at[1])

        for par in range(2):

            @pl.when(lax.rem(r, 2) == par)
            def _():
                for zp in range(NZ):
                    for h in range(2):
                        start = (zp * 2 + h) * PIECE
                        piece = acc[start : start + PIECE, :].astype(BF)
                        low = h ^ par
                        if zp < 2:
                            (send_x if low else keep_x)[g, zp] = piece
                        else:
                            (send_y if g else keep_y)[low, zp - 2] = piece


def wgrad(kind, operands, after):
    part = jax.ShapeDtypeStruct((2, 2, PIECE, D), BF)
    return pl.pallas_call(
        functools.partial(wgrad_kernel, kind),
        out_shape=(part,) * 4,
        in_specs=[INSIDE] * len(operands) + [ANYWHERE],
        out_specs=(INSIDE,) * 4,
        scratch_shapes=[pltpu.VMEM((D, D), F32)],
        compiler_params=PARAMS,
        cost_estimate=cost(2 * D * HALF + 6 * 512 * D, 2 * 512 * D * HALF),
    )(*operands, after)


def finish_kernel(block, *refs):
    p0, p1, p2, pa, pb = refs[:5]
    outs = refs[-8:-4]
    raw, acc, sems_in, sems_out = refs[-4:]
    c, z, r = place()

    @pl.when(c == block)
    def _():
        copies = {}
        for kind in range(3):
            for core in range(2):
                flat = kind * 2 + core
                last = pa.at[flat] if flat < 3 else pb.at[flat - 3]
                for m, piece in enumerate((p0.at[kind, core], p1.at[kind, core], p2.at[kind, core], last)):
                    n = flat * 4 + m
                    copy = pltpu.make_async_copy(piece, raw.at[n], sems_in.at[n])
                    copy.start()
                    copies[n] = copy
        done = []
        for kind in range(3):
            for core in range(2):
                for m in range(4):
                    n = (kind * 2 + core) * 4 + m
                    copies[n].wait()
                    low = lax.rem(r + m, 2)
                    unit = core * 2 + lax.rem(r // 2 + m // 2, 2)
                    piece = raw[n].astype(F32)
                    if kind == 2:
                        at = pl.multiple_of((unit * 2 + low) * PIECE, PIECE)
                        acc[pl.ds(2 * 4 * ROWS + at, PIECE), :] = piece
                    else:
                        at = pl.multiple_of((kind * 4 + unit) * ROWS + low * PIECE, PIECE)
                        acc[pl.ds(at, PIECE), :] = piece
            if kind == 2:
                done.append(pltpu.make_async_copy(acc.at[8 * ROWS :, :], outs[3], sems_out.at[8]))
                done[-1].start()
                continue
            for unit in range(4):
                source = acc.at[(kind * 4 + unit) * ROWS : (kind * 4 + unit + 1) * ROWS, :]
                if kind == 0 and unit == 3:
                    target = outs[1]
                else:
                    target = outs[0 if kind == 0 else 2].at[:, unit * D : (unit + 1) * D]
                done.append(pltpu.make_async_copy(source, target, sems_out.at[kind * 4 + unit]))
                done[-1].start()
        for copy in done:
            copy.wait()


def finish(block, pieces, before, after):
    shapes = ((ROWS, 3 * D), (ROWS, D), (ROWS, FF), (D, D))
    return pl.pallas_call(
        functools.partial(finish_kernel, block),
        out_shape=tuple(jax.ShapeDtypeStruct(s, F32) for s in shapes),
        in_specs=[ANYWHERE] * (6 + len(before)),
        out_specs=(ANYWHERE,) * 4,
        scratch_shapes=[
            pltpu.VMEM((24, PIECE, D), BF),
            pltpu.VMEM((12 * ROWS, D), F32),
            pltpu.SemaphoreType.DMA((24,)),
            pltpu.SemaphoreType.DMA((9,)),
        ],
        input_output_aliases={6 + i: i for i in range(len(before))},
        compiler_params=PARAMS,
        cost_estimate=cost(8 * ROWS * FF),
    )(*pieces, after, *before)


def on_core(value, bit, core):
    return move(value, lambda s, z, r: (s, z, r ^ bit) if s == core else None)


class Reducer:
    def __init__(self, after):
        self.after = after
        self.items = []
        self.state = []
        self.own = {}
        self.ready = {}
        self.results = ()

    def begin(self, block, kind, operands):
        keep_x, send_x, keep_y, send_y = wgrad(kind, operands, self.after)
        self.after = keep_x
        self.items.append((block, kind))
        self.state.append(((keep_x, keep_y), (cross(send_x, 1), cross(send_y, 2))))

    def first(self, i):
        xk, xs, yk, ys = plus(*self.state[i], self.after)
        self.after = xk
        self.state[i] = (xk, yk), (cross(xs, 2), cross(ys, 1))

    def second(self, i):
        f = merged(*self.state[i], self.after)
        self.after = f
        self.state[i] = trade(f)

    def third(self, i):
        v = summed(self.state[i], self.after)
        bit = 4
        while bit < lax.axis_size(R):
            v = summed(jnp.stack([v, cross(v, bit)]), v)
            bit *= 2
        self.after = v
        self.own[self.items[i]] = v

    def unite(self, block):
        own = joined([self.own[block, kind] for kind in range(3)], self.after)
        self.after = own
        self.ready[block] = own, to_core(own, block)

    def spread(self, block):
        p0 = paired(*self.ready[block], self.after)
        self.after = p0
        self.ready[block] = p0, on_core(p0, 1, block), on_core(p0, 2, block)

    def spread_on(self, block):
        p0, p1, p2 = self.ready[block]
        p1, p2 = fence((p1, p2), self.after)
        self.after = p1
        flat1, flat2 = p1.reshape(6, PIECE, D), p2.reshape(6, PIECE, D)
        pa, pb = on_core(flat2[:3], 1, block), on_core(flat1[3:], 2, block)
        self.ready[block] = p0, p1, p2, pa, pb

    def finish(self, block):
        self.results = finish(block, self.ready[block], self.results, self.after)
        self.after = self.results[0]

    def hold(self, *values):
        values = fence(values, self.after)
        self.after = values[0]
        return values


def standard(v):
    mean = jnp.mean(v, axis=-1, keepdims=True)
    centred = v - mean
    rstd = lax.rsqrt(jnp.mean(centred * centred, axis=-1, keepdims=True) + 1e-06)
    return centred * rstd, rstd


def mm(a, b):
    return jnp.dot(a, b, preferred_element_type=F32)


def mmt(a, b):
    return lax.dot_general(a, b, (((1,), (1,)), ((), ())), preferred_element_type=F32)


def head_cols(h, base=0):
    return slice(base + h * HEAD_DIM, base + (h + 1) * HEAD_DIM)


def softmax_of(q, k):
    scores = mmt(q, k)
    e = jnp.exp(scores - jnp.max(scores, axis=-1, keepdims=True))
    return e / jnp.sum(e, axis=-1, keepdims=True)


def shape_of(dtype, *dims):
    return jax.ShapeDtypeStruct(dims, dtype)


def row(ref, i):
    return ref[i : i + 1, :]


def attend_kernel(block, *refs):
    x, ada, qv_bias, proj_bias = refs[:4]
    own, far, mine, other = refs[4:9], refs[9:14], refs[14:16], refs[16:18]
    w_out, sides, q, k, v, attended, mid, mlp_in, w, sems = refs[19:]
    attn_in, mixed = sides.at[0], sides.at[1]
    wait = weight_copies(block, 0, 0, mine, other, own, far, w, sems)
    xf = x[...].astype(F32)
    n1, _ = standard(xf)
    attn_in[...] = (n1 * (1.0 + row(ada, 1)) + row(ada, 0)).astype(BF)
    wait()
    keep = pltpu.make_async_copy(w, w_out, sems.at[26])
    keep.start()
    q[...] = ((mm(attn_in[...], w[:, :D]) + qv_bias[:, :D]) * HEAD_DIM**-0.5).astype(BF)
    k[...] = mm(attn_in[...], w[:, D : 2 * D]).astype(BF)
    v[...] = (mm(attn_in[...], w[:, 2 * D : 3 * D]) + qv_bias[:, D:]).astype(BF)
    for h in range(HEADS):
        cols = head_cols(h)
        probs = softmax_of(q[:, cols], k[:, cols]).astype(BF)
        mixed[:, cols] = mm(probs, v[:, cols]).astype(BF)
    attended[...] = mm(mixed[...], w[:, 3 * D :]) + proj_bias[...]
    mid[...] = x[...].astype(F32) + row(ada, 2) * attended[...]
    n2, _ = standard(mid[...])
    mlp_in[...] = (n2 * (1.0 + row(ada, 4)) + row(ada, 3)).astype(BF)
    keep.wait()


def attend(block, x, ada, biases, gathered):
    t = x.shape[0]
    low = shape_of(BF, t, D)
    high = shape_of(F32, t, D)
    return pl.pallas_call(
        functools.partial(attend_kernel, block),
        out_shape=(shape_of(BF, D, FF), shape_of(BF, 2, t, D), low, low, low, high, high, low),
        in_specs=[INSIDE] * 4 + [ANYWHERE] * 15,
        out_specs=(ANYWHERE,) + (INSIDE,) * 7,
        scratch_shapes=[pltpu.VMEM((D, FF), BF), pltpu.SemaphoreType.DMA((27,))],
        compiler_params=PARAMS,
        cost_estimate=cost(4 * D * FF, 2 * t * D * FF),
    )(x, ada, biases[0], biases[1], *gathered)


def mlp_kernel(block, *refs):
    mid, mlp_in, ada, up_bias, down_bias = refs[:5]
    own, far = refs[5:10], refs[10:15]
    wu_out, wd_out, hidden, act_t, branch, y, wu, wd, act, sems_u, sems_d = refs[20:]
    wait_u = weight_copies(block, 1, 0, refs[15:16], refs[16:17], own, far, wu, sems_u)
    wait_d = weight_copies(block, 2, 1, refs[17:18], refs[18:19], own, far, wd, sems_d)
    wait_u()
    keep_u = pltpu.make_async_copy(wu, wu_out, sems_u.at[26])
    keep_u.start()
    for j in range(4):
        cols = slice(j * D, (j + 1) * D)
        hid = mm(mlp_in[...], wu[:, cols]) + up_bias[:, cols]
        hidden[:, cols] = hid
        part = jax.nn.gelu(hid, approximate=True)
        act[:, cols] = part.astype(BF)
        turned = part.T.astype(BF)
        act_t[0, j] = turned[: D // 2]
        act_t[1, j] = turned[D // 2 :]
    wait_d()
    keep_d = pltpu.make_async_copy(wd, wd_out, sems_d.at[26])
    keep_d.start()
    branch[...] = mm(act[...], wd[...]) + down_bias[...]
    y[...] = (mid[...] + row(ada, 5) * branch[...]).astype(BF)
    keep_u.wait()
    keep_d.wait()


def mlp(block, mid, mlp_in, ada, biases, gathered):
    t = mid.shape[0]
    return pl.pallas_call(
        functools.partial(mlp_kernel, block),
        out_shape=(
            shape_of(BF, D, FF),
            shape_of(BF, FF, D),
            shape_of(F32, t, FF),
            shape_of(BF, 2, NZ, D // 2, t),
            shape_of(F32, t, D),
            shape_of(BF, t, D),
        ),
        in_specs=[INSIDE] * 5 + [ANYWHERE] * 15,
        out_specs=(ANYWHERE,) * 2 + (INSIDE,) * 4,
        scratch_shapes=[
            pltpu.VMEM((D, FF), BF),
            pltpu.VMEM((FF, D), BF),
            pltpu.VMEM((t, FF), BF),
            pltpu.SemaphoreType.DMA((27,)),
            pltpu.SemaphoreType.DMA((27,)),
        ],
        compiler_params=PARAMS,
        cost_estimate=cost(8 * D * FF, 4 * t * D * FF),
    )(mid, mlp_in, ada, biases[2], biases[3], *gathered)


def column_sum(v):
    return jnp.sum(v, axis=0, keepdims=True)


def norm_back(g, n, rstd):
    return rstd * (
        g - jnp.mean(g, axis=-1, keepdims=True) - n * jnp.mean(g * n, axis=-1, keepdims=True)
    )


def gelu_slope(v):
    c = math.sqrt(2.0 / math.pi)
    t = jnp.tanh(c * (v + 0.044715 * v * v * v))
    return 0.5 * (1.0 + t) + 0.5 * v * (1.0 - t * t) * (c * (1.0 + 3.0 * 0.044715 * v * v))


def mlp_back_kernel(*refs):
    grad, d_branch, ada, mid, attended, hidden, branch, wu_in, wd_in = refs[:9]
    d_hidden, d_mid, d_att, stats, wu, wd, acc, sems = refs[10:]
    copies = []
    for j in range(4):
        part = slice(j * D, (j + 1) * D)
        down = pltpu.make_async_copy(wd_in.at[part, :], wd.at[part, :], sems.at[2 * j])
        up = pltpu.make_async_copy(wu_in.at[:, part], wu.at[:, part], sems.at[2 * j + 1])
        copies.append((down, up))
    for down, up in copies:
        down.start()
        up.start()
    stats[...] = jnp.zeros_like(stats)
    stats[5:6, :] = column_sum(grad[...].astype(F32) * branch[...])
    stats[13:14, :] = column_sum(d_branch[...].astype(F32))
    for j in range(4):
        part = slice(j * D, (j + 1) * D)
        copies[j][0].wait()
        d_act = mmt(d_branch[...], wd[part, :])
        d_hid = (d_act * gelu_slope(hidden[:, part])).astype(BF)
        d_hidden[j // 2, :, (j % 2) * D : (j % 2 + 1) * D] = d_hid
        stats[9 + j : 10 + j, :] = column_sum(d_hid.astype(F32))
        copies[j][1].wait()
        product = mmt(d_hid, wu[:, part])
        if j == 0:
            acc[...] = product
        else:
            acc[...] += product
    n2, r2 = standard(mid[...])
    stats[3:4, :] = column_sum(acc[...])
    stats[4:5, :] = column_sum(acc[...] * n2)
    whole = grad[...].astype(F32) + norm_back(acc[...] * (1.0 + row(ada, 4)), n2, r2)
    d_mid[...] = whole
    d_att[...] = (row(ada, 2) * whole).astype(BF)
    stats[2:3, :] = column_sum(whole * attended[...])
    stats[8:9, :] = column_sum(d_att[...].astype(F32))


def mlp_back(grad, d_branch, ada, mid, attended, hidden, branch, wu, wd, after):
    t = grad.shape[0]
    return pl.pallas_call(
        mlp_back_kernel,
        out_shape=(
            shape_of(BF, 2, t, HALF),
            shape_of(F32, t, D),
            shape_of(BF, t, D),
            shape_of(F32, 16, D),
        ),
        in_specs=[INSIDE] * 7 + [ANYWHERE] * 3,
        out_specs=(INSIDE,) * 4,
        scratch_shapes=[
            pltpu.VMEM((D, FF), BF),
            pltpu.VMEM((FF, D), BF),
            pltpu.VMEM((t, D), F32),
            pltpu.SemaphoreType.DMA((8,)),
        ],
        compiler_params=PARAMS,
        cost_estimate=cost(5 * D * FF, 4 * t * D * FF),
    )(grad, d_branch, ada, mid, attended, hidden, branch, wu, wd, after)


def attend_back_kernel(*refs):
    x, d_mid, d_att, ada, q_ref, k_ref, v_ref, stats, w_in = refs[:9]
    out, d_x, d_x_low, small, w, mixed, sem = refs[10:]
    copies = [
        pltpu.make_async_copy(w_in.at[:, 3 * D :], w.at[:, 3 * D :], sem.at[0]),
        pltpu.make_async_copy(w_in.at[:, : 3 * D], w.at[:, : 3 * D], sem.at[1]),
    ]
    for copy in copies:
        copy.start()
    copies[0].wait()
    mixed[...] = mmt(d_att[...], w[:, 3 * D :]).astype(BF)
    for h in range(HEADS):
        cols = head_cols(h)
        q, k, v, dm = (ref[:, cols] for ref in (q_ref, k_ref, v_ref, mixed))
        soft = softmax_of(q, k)
        d_probs = mmt(dm, v)
        inner = jnp.sum(d_probs * soft, axis=-1, keepdims=True)
        d_s = (soft * (d_probs - inner)).astype(BF)
        out[0, :, cols] = (mm(d_s, k) * HEAD_DIM**-0.5).astype(BF)
        out[0, :, head_cols(h, D)] = tdot(d_s, q).astype(BF)
        out[1, :, cols] = tdot(soft.astype(BF), dm).astype(BF)
    out[1, :, D:] = d_att[...]
    copies[1].wait()
    d_in = mmt(out[0, :, :D], w[:, :D])
    d_in += mmt(out[0, :, D:], w[:, D : 2 * D])
    d_in += mmt(out[1, :, :D], w[:, 2 * D : 3 * D])
    n1, r1 = standard(x[...].astype(F32))
    rows = [
        column_sum(d_in),
        column_sum(d_in * n1),
        stats[2:6, :],
        column_sum(out[0, :, :D].astype(F32)),
        column_sum(out[1, :, :D].astype(F32)),
        stats[8:, :],
    ]
    small[...] = jnp.concatenate(rows, axis=0).astype(BF)
    whole = d_mid[...] + norm_back(d_in * (1.0 + row(ada, 1)), n1, r1)
    d_x[...] = whole
    d_x_low[...] = whole.astype(BF)


def attend_back(x, d_mid, d_att, ada, q, k, v, stats, wa, after):
    t = x.shape[0]
    return pl.pallas_call(
        attend_back_kernel,
        out_shape=(
            shape_of(BF, 2, t, HALF),
            shape_of(F32, t, D),
            shape_of(BF, t, D),
            shape_of(BF, 16, D),
        ),
        in_specs=[INSIDE] * 8 + [ANYWHERE] * 2,
        out_specs=(INSIDE,) * 4,
        scratch_shapes=[
            pltpu.VMEM((D, FF), BF),
            pltpu.VMEM((t, D), BF),
            pltpu.SemaphoreType.DMA((2,)),
        ],
        compiler_params=PARAMS,
        cost_estimate=cost(3 * D * FF, 2 * t * D * FF),
    )(x, d_mid, d_att, ada, q, k, v, stats, wa, after)


def far_half(halves):
    c = lax.axis_index(S)
    return swap(lax.dynamic_index_in_dim(halves, 1 - c, 0, keepdims=False))


def rows_sum(v):
    return jnp.sum(v.astype(F32), axis=0)


def embed_time(steps):
    half = D // 2
    freq = jnp.exp(-math.log(10000.0) * jnp.arange(half, dtype=F32) / half)
    angles = steps.astype(F32)[:, None] * freq[None, :]
    return jnp.concatenate([jnp.cos(angles), jnp.sin(angles)], axis=-1)


def across(value):
    out = value[None]
    bit = 1
    while bit < lax.axis_size(R):
        out = jnp.concatenate([out, cross(out, bit)])
        bit *= 2
    return out


def in_order(value):
    nr = lax.axis_size(R)
    return jnp.take(value, lax.axis_index(R) ^ jnp.arange(nr), axis=0)


def per_device(
    inputs,
    cotangent,
    timesteps,
    labels,
    class_table,
    qkv_weight,
    qv_bias,
    proj_weight,
    proj_bias,
    up_weight,
    up_bias,
    down_weight,
    down_bias,
    ada_weight,
    ada_bias,
):
    c = lax.axis_index(S)
    z = lax.axis_index(Z)
    is_first = c == 0

    ids = jnp.concatenate([timesteps, labels], axis=1)
    vectors = [v[0].astype(F32) for v in (qv_bias, proj_bias, up_bias, down_bias, ada_bias)]
    small = along_z(jnp.concatenate(vectors + [ids.reshape(-1).astype(F32)]))
    ids_z = small[:, -4:].astype(jnp.int32).reshape(NZ, 2, 2)
    vec_mine = small[:, :-4]
    vec_other = swap(vec_mine)

    def cond_of(steps, classes):
        return embed_time(steps) + jnp.take(class_table, classes, axis=0).astype(F32)

    cond_z = cond_of(ids_z[..., 0].reshape(-1), ids_z[..., 1].reshape(-1))
    silu_z = jax.nn.silu(cond_z).astype(BF)
    rows_z = lax.dynamic_slice_in_dim(silu_z, z * ROWS, ROWS, 1)
    partial = mm(rows_z, ada_weight[0]).reshape(NZ, 2, -1)
    ada_sum = jnp.sum(trade(partial), axis=0)
    lengths = (qv_bias.shape[1], proj_bias.shape[1], up_bias.shape[1], down_bias.shape[1], ada_bias.shape[1])

    def split_vectors(vec):
        out = []
        at = 0
        for n in lengths:
            out.append(vec[:, at : at + n].reshape(-1))
            at += n
        return out

    mine_split = split_vectors(vec_mine)
    other_split = split_vectors(vec_other)
    ada_sum = ada_sum + mine_split[4][None]
    ada_keep = lax.dynamic_index_in_dim(ada_sum, c, 0, keepdims=False)
    ada_got = swap(lax.dynamic_index_in_dim(ada_sum, 1 - c, 0, keepdims=False))
    adas = []
    biases = []
    for block in range(2):
        here = c == block
        adas.append(jnp.where(here, ada_keep, ada_got).reshape(6, D))
        biases.append(
            [jnp.where(here, a, b)[None] for a, b in zip(mine_split[:4], other_split[:4])]
        )

    mine = ((qkv_weight[0], proj_weight[0]), (up_weight[0],), (down_weight[0],))
    other = tuple(tuple(swap(w) for w in group) for group in mine)
    gatherer = Gatherer(mine, other, qkv_weight[0])
    x = lax.dynamic_index_in_dim(inputs, c, 0, keepdims=False)[0]
    cot = lax.dynamic_index_in_dim(cotangent, c, 0, keepdims=False)[0]
    kept = []
    kept_mlp = []

    def run_attend(block, value):
        got = attend(block, value, adas[block], biases[block], gatherer.operands(2 * block))
        gatherer.after = got[-1]
        kept.append(got)
        return swap(got[1])

    def run_mlp(block):
        mid, mlp_in = kept[block][-2:]
        got = mlp(block, mid, mlp_in, adas[block], biases[block], gatherer.operands(2 * block + 1))
        gatherer.after = got[-1]
        kept_mlp.append(got)
        return far_half(got[3]), swap(mlp_in)

    def branch_grad(block, grad):
        return (adas[block][5:] * grad.astype(F32)).astype(BF)

    for g in range(4):
        gatherer.extract(g)
    ids_all = in_order(across(ids_z)).reshape(-1, 2)
    gatherer.after = ids_all
    gatherer.stack(0)
    gatherer.onward(0)
    gatherer.share(0)
    far_sides0 = run_attend(0, x)
    gatherer.stack(1)
    d_branch1 = branch_grad(1, cot)
    far_branch1 = swap(d_branch1)
    far_sides0, far_branch1 = gatherer.hold(far_sides0, far_branch1)
    gatherer.onward(1)
    gatherer.stack(2)
    gatherer.share(1)
    far_mlp0 = run_mlp(0)
    y0 = kept_mlp[0][5]
    gatherer.onward(2)
    gatherer.stack(3)
    far_mlp0 = gatherer.hold(*far_mlp0)
    gatherer.share(2)
    far_sides1 = run_attend(1, y0)
    gatherer.onward(3)
    (far_sides1,) = gatherer.hold(far_sides1)
    gatherer.share(3)
    far_mlp1 = run_mlp(1)
    y1 = kept_mlp[1][5]

    reducer = Reducer(y1)

    def run_mlp_back(block, grad, d_branch):
        attended, mid, mlp_in = kept[block][-3:]
        wu, wd, hidden, act_t, branch, _ = kept_mlp[block]
        got = mlp_back(
            grad, d_branch, adas[block], mid, attended, hidden, branch, wu, wd, reducer.after
        )
        reducer.after = got[0]
        return got, far_half(got[0])

    def run_attend_back(block, value, back):
        wa, sides, q, k, v = kept[block][:5]
        _, d_mid, d_att, stats = back
        got = attend_back(
            value, d_mid, d_att, adas[block], q, k, v, stats, wa, reducer.after
        )
        reducer.after = got[2]
        return got

    def begin(block, kind, *operands):
        reducer.begin(block, kind, operands)

    back1, far_hidden1 = run_mlp_back(1, cot, d_branch1)
    begin(1, 2, kept_mlp[1][3], far_mlp1[0], d_branch1, far_branch1)
    begin(1, 1, kept[1][-1], far_mlp1[1], back1[0], far_hidden1)
    d_all1, dx1f, dx1, small1 = run_attend_back(1, y0, back1)
    far_all1 = far_half(d_all1)
    d_branch0 = branch_grad(0, dx1)
    far_branch0 = swap(d_branch0)
    reducer.first(0)
    begin(1, 0, kept[1][1], far_sides1, d_all1, far_all1)
    back0, far_hidden0 = run_mlp_back(0, dx1, d_branch0)
    begin(0, 2, kept_mlp[0][3], far_mlp0[0], d_branch0, far_branch0)
    reducer.first(1)
    reducer.second(0)
    begin(0, 1, kept[0][-1], far_mlp0[1], back0[0], far_hidden0)
    d_all0, dx0, dx0_low, small0 = run_attend_back(0, x, back0)
    far_all0 = far_half(d_all0)
    reducer.first(2)
    reducer.second(1)
    reducer.third(0)
    begin(0, 0, kept[0][1], far_sides0, d_all0, far_all0)
    small_keep = jnp.where(is_first, small0, small1)
    small_got = swap(jnp.where(is_first, small1, small0))
    reducer.first(3)
    reducer.second(2)
    reducer.third(1)
    (small_got,) = reducer.hold(small_got)
    small = jnp.stack(
        [jnp.where(is_first, small_keep, small_got), jnp.where(is_first, small_got, small_keep)]
    )
    reducer.first(4)
    reducer.second(3)
    reducer.third(2)
    small = along_z(small)
    reducer.unite(1)
    reducer.first(5)
    (small,) = reducer.hold(small)
    small = small[None]
    bits = [1 << i for i in range(lax.axis_size(R).bit_length() - 1)]
    hop = cross(small, 1)
    reducer.spread(1)
    reducer.second(4)
    reducer.third(3)
    (hop,) = reducer.hold(hop)
    small = jnp.concatenate([small, hop])
    hop = cross(small, 2)
    reducer.spread_on(1)
    reducer.second(5)
    reducer.third(4)
    (hop,) = reducer.hold(hop)
    small = jnp.concatenate([small, hop])
    for bit in bits[2:]:
        small = jnp.concatenate([small, cross(small, bit)])
    reducer.finish(1)
    reducer.third(5)
    reducer.unite(0)
    reducer.spread(0)
    reducer.spread_on(0)
    reducer.finish(0)
    qkv_grad, proj_grad, up_grad, down_grad = reducer.results

    def both_micros(v0, v1):
        keep = jnp.where(is_first, v0, v1)
        got = swap(jnp.where(is_first, v1, v0))
        return jnp.stack([jnp.where(is_first, keep, got), jnp.where(is_first, got, keep)])

    block_outputs = both_micros(y0, y1)[None, :, None]
    input_grads = both_micros(dx0, dx1.astype(F32))[None, :, None]

    small = in_order(small).reshape(-1, 16, D)
    sums = rows_sum(small[:, 6:14])
    dada_own = small[:, :6].reshape(-1, 6 * D)

    def own_slice(vec):
        vec = vec.reshape(-1)
        n = vec.shape[0] // NZ
        return lax.dynamic_slice_in_dim(vec, z * n, n, 0)[None]

    qv_bias_grad = own_slice(sums[:2])
    proj_bias_grad = own_slice(sums[2])
    up_bias_grad = own_slice(sums[3:7])
    down_bias_grad = own_slice(sums[7])

    cond_all = cond_of(ids_all[:, 0], ids_all[:, 1])
    labels_all = ids_all[:, 1]
    cond_rows = lax.dynamic_slice_in_dim(cond_all, z * ROWS, ROWS, 1)
    silu_rows = jax.nn.silu(cond_rows).astype(BF)
    ada_grad = lax.dot_general(
        silu_rows, dada_own, (((0,), (0,)), ((), ())), preferred_element_type=F32
    )
    ada_bias_grad = own_slice(rows_sum(dada_own))
    d_silu = mmt(dada_own, ada_weight[0])
    _, silu_back = jax.vjp(jax.nn.silu, cond_rows)
    d_cond = silu_back(d_silu)[0]
    d_cond = d_cond + swap(d_cond)
    d_cond_all = along_z(d_cond).transpose(1, 0, 2).reshape(-1, D)
    row_count = class_table.shape[0] // (2 * NZ)
    row_ids = (c * NZ + z) * row_count + jnp.arange(row_count, dtype=jnp.int32)
    owner = (row_ids[:, None] == labels_all[None, :]).astype(F32)
    table_grad = jnp.dot(owner, d_cond_all, precision=lax.Precision.HIGHEST)

    return (
        block_outputs,
        input_grads,
        table_grad,
        qkv_grad[None],
        qv_bias_grad,
        proj_grad[None],
        proj_bias_grad,
        up_grad[None],
        up_bias_grad,
        down_grad[None],
        down_bias_grad,
        ada_grad[None],
        ada_bias_grad,
    )


def solution(mesh):
    rows = P(None, (Z, R), None, None)
    matrix = P(S, Z, None)
    vector = P(S, Z)
    pair = P(None, (Z, R))
    in_specs = (rows, rows, pair, pair, P()) + (matrix, vector) * 5
    acts = P(S, None, (Z, R), None, None)
    out_specs = (acts, acts, P((S, Z), None)) + (matrix, vector) * 5
    return jax.shard_map(
        per_device, mesh=mesh, in_specs=in_specs, out_specs=out_specs, check_vma=False
    )
```

```python
import functools
import math

import jax
import jax.numpy as jnp
from jax import lax
from jax.experimental import pallas as pl
from jax.experimental.pallas import tpu as pltpu
from jax.sharding import PartitionSpec as P

S = "section"
Z = "shard"
R = "replica"
ALL = (S, Z, R)
BF = jnp.bfloat16
F32 = jnp.float32
D = 1152
HEAD_DIM = 72
HEADS = 16
FF = 4608
HALF = 2304
ROWS = 288
PIECE = 144
NZ = 4
SHARDS = (1, 2, 3)
VMEM_LIMIT = 50 * 1024 * 1024


def move(value, to):
    ns, nz, nr = (lax.axis_size(a) for a in ALL)
    pairs = []
    for s in range(ns):
        for z in range(nz):
            for r in range(nr):
                there = to(s, z, r)
                if there is not None:
                    a, b, c = there
                    pairs.append(((s * nz + z) * nr + r, (a * nz + b) * nr + c))
    return lax.ppermute(value, ALL, pairs)


def swap(value):
    return move(value, lambda s, z, r: (1 - s, z, r))


def to_core(value, core):
    return move(value, lambda s, z, r: (core, z, r) if s != core else None)


def zshift(value, by=1):
    nz = lax.axis_size(Z)
    return move(value, lambda s, z, r: (s, (z + by) % nz, r))


def trade(value):
    return lax.all_to_all(value, Z, split_axis=0, concat_axis=0, tiled=True)


def along_z(value):
    return trade(jnp.stack([value] * NZ))


def cross(value, bit):
    return move(value, lambda s, z, r: (s, z, r ^ bit))


def place():
    return lax.axis_index(S), lax.axis_index(Z), lax.rem(lax.axis_index(R), 4)


ANYWHERE = pl.BlockSpec(memory_space=pl.ANY)
INSIDE = pl.BlockSpec(memory_space=pltpu.VMEM)
PARAMS = pltpu.CompilerParams(vmem_limit_bytes=VMEM_LIMIT)
ONE = jax.ShapeDtypeStruct((PIECE, D), BF)


def cost(nbytes, flops=0):
    return pl.CostEstimate(flops=flops, bytes_accessed=nbytes, transcendentals=0)


def free():
    return pl.CostEstimate(flops=0, bytes_accessed=0, transcendentals=0)


def fence(arrays, after):
    n = len(arrays)
    return pl.pallas_call(
        lambda *refs: None,
        out_shape=tuple(jax.ShapeDtypeStruct(a.shape, a.dtype) for a in arrays),
        in_specs=[ANYWHERE] * (n + 1),
        out_specs=(ANYWHERE,) * n,
        input_output_aliases={i: i for i in range(n)},
        cost_estimate=free(),
    )(*arrays, after)


def stack_kernel(every, _, out):
    z = lax.axis_index(Z)
    for i in range(every.shape[1]):
        for k in SHARDS:
            out[i, k - 1] = every[lax.rem(z + NZ - k, NZ), i]


def stacked(every, after):
    n = every.shape[1]
    return pl.pallas_call(
        stack_kernel,
        out_shape=jax.ShapeDtypeStruct((n, 3, PIECE, D), BF),
        in_specs=[INSIDE, ANYWHERE],
        out_specs=INSIDE,
        compiler_params=PARAMS,
        cost_estimate=cost(12 * n * PIECE * D),
    )(every, after)


def collect_kernel(p0, p1, p2, _, big, to_x, to_y):
    n = p0.shape[0]
    for m, part in enumerate((p0, p1, p2)):
        big[m] = part[...]
    if n == 2:
        to_x[...] = p2[:1]
        to_y[...] = p1[1:]
    else:
        to_x[...] = p2[:, :1]
        to_y[...] = p1[:, 1:]


def collected(p0, p1, p2, after):
    n = p0.shape[0]
    if n == 2:
        cut = (1, 3), (1, 3)
    else:
        cut = (1, 1), (1, 2)
    shapes = ((3, n, 3), *cut)
    return pl.pallas_call(
        collect_kernel,
        out_shape=tuple(jax.ShapeDtypeStruct((*s, PIECE, D), BF) for s in shapes),
        in_specs=[INSIDE] * 3 + [ANYWHERE],
        out_specs=(INSIDE,) * 3,
        compiler_params=PARAMS,
        cost_estimate=cost(1),
    )(p0, p1, p2, after)


def combine_kernel(pa, pb, _, out):
    if out.shape[0] == 2:
        out[:1] = pa[...]
        out[1:] = pb[...]
    else:
        out[:, :1] = pa[...]
        out[:, 1:] = pb[...]


def combined(pa, pb, after):
    n = 2 if pa.shape[1] == 3 else 1
    return pl.pallas_call(
        combine_kernel,
        out_shape=jax.ShapeDtypeStruct((n, 3, PIECE, D), BF),
        in_specs=[INSIDE] * 2 + [ANYWHERE],
        out_specs=INSIDE,
        compiler_params=PARAMS,
        cost_estimate=cost(1),
    )(pa, pb, after)


def join_kernel(*refs):
    out = refs[-1]
    for i in range(out.shape[0]):
        out[i] = refs[i][...]


def joined(parts, after):
    n = len(parts)
    return pl.pallas_call(
        join_kernel,
        out_shape=jax.ShapeDtypeStruct((n, PIECE, D), BF),
        in_specs=[INSIDE] * n + [ANYWHERE],
        out_specs=INSIDE,
        compiler_params=PARAMS,
        cost_estimate=free(),
    )(*parts, after)


def plus_kernel(n, *refs):
    outs = refs[2 * n + 1 :]
    for i in range(n):
        for j in range(2):
            whole = refs[i][j].astype(F32) + refs[n + i][j].astype(F32)
            outs[2 * i + j][...] = whole.astype(BF)


def plus(a, b, after):
    n = len(a)
    shapes = [jax.ShapeDtypeStruct(v.shape[1:], BF) for v in a for _ in range(2)]
    return pl.pallas_call(
        functools.partial(plus_kernel, n),
        out_shape=tuple(shapes),
        in_specs=[INSIDE] * (2 * n) + [ANYWHERE],
        out_specs=(INSIDE,) * (2 * n),
        compiler_params=PARAMS,
        cost_estimate=free(),
    )(*a, *b, after)


def merge_kernel(n, *refs):
    out = refs[-1]
    for i in range(n):
        whole = refs[i][...].astype(F32) + refs[n + i][...].astype(F32)
        rows = refs[i].shape[0]
        out[i * rows : (i + 1) * rows] = whole.astype(BF)


def merged(a, b, after):
    n = len(a)
    return pl.pallas_call(
        functools.partial(merge_kernel, n),
        out_shape=jax.ShapeDtypeStruct((NZ, PIECE, D), BF),
        in_specs=[INSIDE] * (2 * n) + [ANYWHERE],
        out_specs=INSIDE,
        compiler_params=PARAMS,
        cost_estimate=free(),
    )(*a, *b, after)


def sum_kernel(n, *refs):
    if n == 1:
        parts = [refs[0][i] for i in range(refs[0].shape[0])]
    else:
        parts = [ref[...] for ref in refs[:n]]
    whole = parts[0].astype(F32)
    for part in parts[1:]:
        whole = whole + part.astype(F32)
    refs[-1][...] = whole.astype(BF)


def summed(parts, after):
    n = len(parts)
    return pl.pallas_call(
        functools.partial(sum_kernel, n),
        out_shape=ONE,
        in_specs=[INSIDE] * n + [ANYWHERE],
        out_specs=INSIDE,
        compiler_params=PARAMS,
        cost_estimate=free(),
    )(*parts, after)


def fold_kernel(parts, _, keep, send):
    for m in range(4):
        whole = parts[0, m].astype(F32)
        for i in SHARDS:
            whole = whole + parts[i, m].astype(F32)
        (send if m % 2 else keep)[m // 2] = whole.astype(BF)


def folded(parts, after):
    half = jax.ShapeDtypeStruct((2, PIECE, D), BF)
    return pl.pallas_call(
        fold_kernel,
        out_shape=(half, half),
        in_specs=[INSIDE, ANYWHERE],
        out_specs=(INSIDE, INSIDE),
        compiler_params=PARAMS,
        cost_estimate=free(),
    )(parts, after)


def pair_kernel(own, far, _, out):
    c = lax.axis_index(S)
    for core in range(2):

        @pl.when(c == core)
        def _():
            for i in range(own.shape[0]):
                out[i, core] = own[i]
                out[i, 1 - core] = far[i]


def paired(own, far, after):
    return pl.pallas_call(
        pair_kernel,
        out_shape=jax.ShapeDtypeStruct((own.shape[0], 2, PIECE, D), BF),
        in_specs=[INSIDE] * 2 + [ANYWHERE],
        out_specs=INSIDE,
        compiler_params=PARAMS,
        cost_estimate=free(),
    )(own, far, after)


def chosen(block, mine, other, act):
    c = lax.axis_index(S)

    @pl.when(c == block)
    def _():
        act(mine)

    @pl.when(c != block)
    def _():
        act(other)


def arrays_of(kind):
    return 2 if kind == 0 else 1


def extract_kernel(items, *refs):
    out, sems = refs[-2:]
    c, z, r = place()
    unit = c * 2 + r // 2
    at = 0
    for i, (block, kind) in enumerate(items):
        n = arrays_of(kind)
        mine, other = refs[at : at + n], refs[at + n : at + 2 * n]
        at += 2 * n

        def copy(source):
            pltpu.make_async_copy(source, out.at[i], sems.at[i]).start()

        def act(source):
            if kind == 2:
                copy(source[0].at[pl.ds((c * 4 + r) * PIECE, PIECE), :])
                return
            height = pl.ds(lax.rem(r, 2) * PIECE, PIECE)

            def take(ref, index):
                cols = pl.ds(pl.multiple_of(index * D, D), D)
                copy(ref.at[height, cols])

            if kind == 1:
                take(source[0], unit)
                return

            @pl.when(unit == 3)
            def _():
                take(source[1], 0)

            @pl.when(unit != 3)
            def _():
                take(source[0], unit)

        chosen(block, mine, other, act)
    for i in range(len(items)):
        pltpu.make_async_copy(out.at[i], out.at[i], sems.at[i]).wait()


def extract(items, mine, other, after):
    n = len(items)
    operands = []
    for _, kind in items:
        operands += [*mine[kind], *other[kind]]
    return pl.pallas_call(
        functools.partial(extract_kernel, items),
        out_shape=jax.ShapeDtypeStruct((n, PIECE, D), BF),
        in_specs=[ANYWHERE] * (len(operands) + 1),
        out_specs=INSIDE,
        scratch_shapes=[pltpu.SemaphoreType.DMA((n,))],
        compiler_params=PARAMS,
        cost_estimate=cost(4 * n * PIECE * D),
    )(*operands, after)


def weight_copies(block, kind, index, mine, other, own, far, out, sems):
    n = arrays_of(kind)
    c, z, r = place()
    copies = []
    height = D if kind == 2 else ROWS
    rows = pl.ds(z * height, height)
    if kind == 0:
        targets = (out.at[rows, pl.ds(0, 3 * D)], out.at[rows, pl.ds(3 * D, D)])
    else:
        targets = (out.at[rows, :],)

    def act(source):
        for i in range(n):
            pltpu.make_async_copy(source[i], targets[i], sems.at[i]).start()

    chosen(block, mine, other, act)
    for side, group in ((0, own), (1, far)):
        core = c if side == 0 else 1 - c
        for m in range(4):
            low = lax.rem(r + m, 2)
            high = lax.rem(r // 2 + m // 2, 2)
            for k in SHARDS:
                zp = lax.rem(z + NZ - k, NZ)
                if kind == 2:
                    row = zp * D + core * (D // 2) + (high * 2 + low) * PIECE
                    spot = out.at[pl.ds(row, PIECE), :]
                else:
                    row = zp * ROWS + low * PIECE
                    col = pl.multiple_of((core * 2 + high) * D, D)
                    spot = out.at[pl.ds(row, PIECE), pl.ds(col, D)]
                if m < 3:
                    piece = group[0].at[m, index, k - 1]
                else:
                    piece = group[1].at[index, k - 1]
                sem = sems.at[2 + (side * 4 + m) * 3 + k - 1]
                copies.append(pltpu.make_async_copy(piece, spot, sem))
    for copy in copies:
        copy.start()

    def wait():
        for i in range(n):
            pltpu.make_async_copy(mine[i], targets[i], sems.at[i]).wait()
        for copy in copies:
            copy.wait()

    return wait


GROUPS = (((0, 0),), ((0, 1), (0, 2)), ((1, 0),), ((1, 1), (1, 2)))


class Gatherer:
    def __init__(self, mine, other, after):
        self.mine = mine
        self.other = other
        self.after = after
        self.state = {}

    def extract(self, g):
        self.after = extract(GROUPS[g], self.mine, self.other, self.after)
        self.state[g] = lax.all_gather(self.after, Z, axis=0, tiled=False)

    def stack(self, g):
        p0 = stacked(self.state[g], self.after)
        self.after = p0
        self.state[g] = p0, cross(p0, 1), cross(p0, 2)

    def onward(self, g):
        big, to_x, to_y = collected(*self.state[g], self.after)
        self.after = to_x
        self.state[g] = big, (cross(to_x, 1), cross(to_y, 2)), swap(big)

    def share(self, g):
        big, p3, far = self.state[g]
        p3 = combined(*p3, self.after)
        self.after = p3
        self.state[g] = (big, p3), (far, swap(p3))

    def hold(self, *values):
        values = fence(values, self.after)
        self.after = values[0]
        return values

    def operands(self, g):
        own, far = self.state[g]
        shards = []
        for _, kind in GROUPS[g]:
            shards += [*self.mine[kind], *self.other[kind]]
        return (*own, *far, *shards, self.after)


def tdot(a, b):
    return lax.dot_general(a, b, (((0,), (0,)), ((), ())), preferred_element_type=F32)


def wgrad_kernel(kind, mode, *refs):
    n = 4
    ins = refs[:n]
    outs = refs[n + 1 : -1]
    acc = refs[-1]
    c, z, r = place()
    for g in range(2):
        u = lax.rem(g + r // 2, 2)
        if kind == 2:
            lo, lx, ro, rx = ins
            for zp in range(NZ):
                rows = pl.ds(pl.multiple_of(u * ROWS, ROWS), ROWS)
                acc[zp * ROWS : (zp + 1) * ROWS, :] = jnp.dot(
                    lo[c, zp, rows, :], ro[...], preferred_element_type=F32
                ) + jnp.dot(lx[zp, rows, :], rx[...], preferred_element_type=F32)
        else:
            ro, rx = ins[-2:]
            cols = pl.ds(pl.multiple_of(u * D, D), D)

            def product(lo, lx):
                acc[...] = tdot(lo[...], ro[c, :, cols]) + tdot(lx[...], rx[:, cols])

            if kind == 1:
                product(ins[0], ins[1])
            else:

                @pl.when(c * u == 0)
                def _():
                    product(ins[0].at[0], ins[1].at[0])

                @pl.when(c * u == 1)
                def _():
                    product(ins[0].at[1], ins[1].at[1])

        for par in range(2):

            @pl.when(lax.rem(r, 2) == par)
            def _():
                for zp in range(NZ):
                    for h in range(2):
                        start = (zp * 2 + h) * PIECE
                        piece = acc[start : start + PIECE, :].astype(BF)
                        low = h ^ par
                        if mode == 0:
                            outs[0][zp, g * 2 + low] = piece
                        elif mode == 1:
                            outs[low][g, zp] = piece
                        elif mode == 2:
                            outs[g][low, zp] = piece
                        elif zp < 2:
                            outs[low][g, zp] = piece
                        else:
                            outs[2 + g][low, zp - 2] = piece


def wgrad(kind, mode, operands, after):
    leading = ((4, 4), (2, 4), (2, 4), (2, 2))[mode]
    count = (1, 2, 2, 4)[mode]
    part = jax.ShapeDtypeStruct((*leading, PIECE, D), BF)
    return pl.pallas_call(
        functools.partial(wgrad_kernel, kind, mode),
        out_shape=(part,) * count,
        in_specs=[INSIDE] * len(operands) + [ANYWHERE],
        out_specs=(INSIDE,) * count,
        scratch_shapes=[pltpu.VMEM((D, D), F32)],
        compiler_params=PARAMS,
        cost_estimate=free(),
    )(*operands, after)


def finish_kernel(block, kinds, *refs):
    count = len(kinds)
    outs = list(refs[-4 - count - (0 in kinds) : -4])
    raw, acc, sems_in, sems_out = refs[-4:]
    p0, p1, p2, pa, pb = refs[:5]
    c, z, r = place()

    @pl.when(c == block)
    def _():
        copies = []
        for i in range(count):
            for core in range(2):
                flat = i * 2 + core
                last = pa.at[flat] if flat < count else pb.at[flat - count]
                sources = (p0.at[i, core], p1.at[i, core], p2.at[i, core], last)
                for m, piece in enumerate(sources):
                    n = flat * 4 + m
                    copies.append(pltpu.make_async_copy(piece, raw.at[n], sems_in.at[n]))
                    copies[-1].start()
        done = []
        at_out = 0
        for i, kind in enumerate(kinds):
            base = i * 4 * ROWS
            for core in range(2):
                for m in range(4):
                    n = (i * 2 + core) * 4 + m
                    copies[n].wait()
                    low = lax.rem(r + m, 2)
                    unit = core * 2 + lax.rem(r // 2 + m // 2, 2)
                    at = pl.multiple_of(base + unit * ROWS + low * PIECE, PIECE)
                    acc[pl.ds(at, PIECE), :] = raw[n].astype(F32)
            if kind == 2:
                moves = [(acc.at[base : base + D, :], outs[at_out])]
            else:
                moves = []
                for unit in range(4):
                    source = acc.at[base + unit * ROWS : base + (unit + 1) * ROWS, :]
                    if kind == 0 and unit == 3:
                        moves.append((source, outs[at_out + 1]))
                    else:
                        cols = outs[at_out].at[:, unit * D : (unit + 1) * D]
                        moves.append((source, cols))
            at_out += 2 if kind == 0 else 1
            for source, target in moves:
                done.append(pltpu.make_async_copy(source, target, sems_out.at[len(done)]))
                done[-1].start()
        for copy in done:
            copy.wait()


def finish(block, kinds, pieces, before, after):
    shapes = []
    for kind in kinds:
        shapes += [[(ROWS, 3 * D), (ROWS, D)], [(ROWS, FF)], [(D, D)]][kind]
    count = len(kinds)
    return pl.pallas_call(
        functools.partial(finish_kernel, block, kinds),
        out_shape=tuple(jax.ShapeDtypeStruct(s, F32) for s in shapes),
        in_specs=[ANYWHERE] * (6 + len(before)),
        out_specs=(ANYWHERE,) * len(shapes),
        scratch_shapes=[
            pltpu.VMEM((8 * count, PIECE, D), BF),
            pltpu.VMEM((4 * count * ROWS, D), F32),
            pltpu.SemaphoreType.DMA((8 * count,)),
            pltpu.SemaphoreType.DMA((12,)),
        ],
        input_output_aliases={6 + i: i for i in range(len(before))},
        compiler_params=PARAMS,
        cost_estimate=free(),
    )(*pieces, after, *before)


def on_core(value, bit, core):
    return move(value, lambda s, z, r: (s, z, r ^ bit) if s == core else None)


class Reducer:
    def __init__(self, after):
        self.after = after
        self.items = []
        self.modes = []
        self.state = []
        self.own = {}
        self.ready = {}
        self.results = {}

    def begin(self, block, kind, mode, operands):
        out = wgrad(kind, mode, operands, self.after)
        self.after = out[0]
        self.items.append((block, kind))
        self.modes.append(mode)
        if mode == 0:
            self.state.append(trade(out[0]))
        elif mode < 3:
            self.state.append(((out[0],), (cross(out[1], mode),)))
        else:
            keep_x, send_x, keep_y, send_y = out
            self.state.append(((keep_x, keep_y), (cross(send_x, 1), cross(send_y, 2))))

    def first(self, i):
        mode = self.modes[i]
        if mode == 0:
            keep, send = folded(self.state[i], self.after)
            self.after = keep
            self.state[i] = (keep,), (cross(send, 1),)
            return
        out = plus(*self.state[i], self.after)
        self.after = out[0]
        if mode < 3:
            self.state[i] = (out[0],), (cross(out[1], 3 - mode),)
        else:
            xk, xs, yk, ys = out
            self.state[i] = (xk, yk), (cross(xs, 2), cross(ys, 1))

    def second(self, i):
        if self.modes[i] == 0:
            keep, send = plus(*self.state[i], self.after)
            self.after = keep
            self.state[i] = keep, cross(send, 2)
            return
        f = merged(*self.state[i], self.after)
        self.after = f
        self.state[i] = (trade(f),)

    def third(self, i):
        v = summed(self.state[i], self.after)
        bit = 4
        while bit < lax.axis_size(R):
            v = summed((v, cross(v, bit)), v)
            bit *= 2
        self.after = v
        self.own[self.items[i]] = v

    def unite(self, block, kinds):
        own = joined([self.own[block, kind] for kind in kinds], self.after)
        self.after = own
        self.ready[block, kinds] = own, to_core(own, block)

    def spread(self, block, kinds):
        p0 = paired(*self.ready[block, kinds], self.after)
        self.after = p0
        self.ready[block, kinds] = p0, on_core(p0, 1, block), on_core(p0, 2, block)

    def spread_on(self, block, kinds):
        p0, p1, p2 = self.ready[block, kinds]
        p1, p2 = fence((p1, p2), self.after)
        self.after = p1
        n = len(kinds)
        flat1, flat2 = p1.reshape(2 * n, PIECE, D), p2.reshape(2 * n, PIECE, D)
        pa, pb = on_core(flat2[:n], 1, block), on_core(flat1[n:], 2, block)
        self.ready[block, kinds] = p0, p1, p2, pa, pb

    def finish(self, block, kinds):
        before = []
        for kind in kinds:
            before += self.results.get(kind, [])
        out = list(finish(block, kinds, self.ready[block, kinds], before, self.after))
        self.after = out[0]
        for kind in kinds:
            n = 2 if kind == 0 else 1
            self.results[kind], out = out[:n], out[n:]

    def hold(self, *values):
        values = fence(values, self.after)
        self.after = values[0]
        return values


def standard(v):
    mean = jnp.mean(v, axis=-1, keepdims=True)
    centred = v - mean
    rstd = lax.rsqrt(jnp.mean(centred * centred, axis=-1, keepdims=True) + 1e-06)
    return centred * rstd, rstd


def mm(a, b):
    return jnp.dot(a, b, preferred_element_type=F32)


def mmt(a, b):
    return lax.dot_general(a, b, (((1,), (1,)), ((), ())), preferred_element_type=F32)


def head_cols(h, base=0):
    return slice(base + h * HEAD_DIM, base + (h + 1) * HEAD_DIM)


def softmax_of(q, k):
    scores = mmt(q, k)
    e = jnp.exp(scores - jnp.max(scores, axis=-1, keepdims=True))
    return e / jnp.sum(e, axis=-1, keepdims=True)


def shape_of(dtype, *dims):
    return jax.ShapeDtypeStruct(dims, dtype)


def row(ref, i):
    return ref[i : i + 1, :]


def attend_kernel(block, *refs):
    x, ada, qv_bias, proj_bias = refs[:4]
    own, far, mine, other = refs[4:6], refs[6:8], refs[8:10], refs[10:12]
    w_out, sides, q, k, v, attended, mid, mlp_in, w, sems = refs[13:]
    attn_in, mixed = sides.at[0], sides.at[1]
    wait = weight_copies(block, 0, 0, mine, other, own, far, w, sems)
    xf = x[...].astype(F32)
    n1, _ = standard(xf)
    attn_in[...] = (n1 * (1.0 + row(ada, 1)) + row(ada, 0)).astype(BF)
    wait()
    keep = pltpu.make_async_copy(w, w_out, sems.at[26])
    keep.start()
    q[...] = ((mm(attn_in[...], w[:, :D]) + qv_bias[:, :D]) * HEAD_DIM**-0.5).astype(BF)
    k[...] = mm(attn_in[...], w[:, D : 2 * D]).astype(BF)
    v[...] = (mm(attn_in[...], w[:, 2 * D : 3 * D]) + qv_bias[:, D:]).astype(BF)
    for h in range(HEADS):
        cols = head_cols(h)
        probs = softmax_of(q[:, cols], k[:, cols]).astype(BF)
        mixed[:, cols] = mm(probs, v[:, cols]).astype(BF)
    attended[...] = mm(mixed[...], w[:, 3 * D :]) + proj_bias[...]
    mid[...] = x[...].astype(F32) + row(ada, 2) * attended[...]
    n2, _ = standard(mid[...])
    mlp_in[...] = (n2 * (1.0 + row(ada, 4)) + row(ada, 3)).astype(BF)
    keep.wait()


def attend(block, x, ada, biases, gathered):
    t = x.shape[0]
    low = shape_of(BF, t, D)
    high = shape_of(F32, t, D)
    return pl.pallas_call(
        functools.partial(attend_kernel, block),
        out_shape=(shape_of(BF, D, FF), shape_of(BF, 2, t, D), low, low, low, high, high, low),
        in_specs=[INSIDE] * 4 + [ANYWHERE] * 9,
        out_specs=(ANYWHERE,) + (INSIDE,) * 7,
        scratch_shapes=[pltpu.VMEM((D, FF), BF), pltpu.SemaphoreType.DMA((27,))],
        compiler_params=PARAMS,
        cost_estimate=cost(4 * D * FF, 2 * t * D * FF),
    )(x, ada, biases[0], biases[1], *gathered)


def mlp_kernel(block, *refs):
    mid, mlp_in, ada, up_bias, down_bias = refs[:5]
    own, far = refs[5:7], refs[7:9]
    wu_out, wd_out, hidden, act_t, branch, y, wu, wd, act, sems_u, sems_d = refs[14:]
    wait_u = weight_copies(block, 1, 0, refs[9:10], refs[10:11], own, far, wu, sems_u)
    wait_d = weight_copies(block, 2, 1, refs[11:12], refs[12:13], own, far, wd, sems_d)
    wait_u()
    keep_u = pltpu.make_async_copy(wu, wu_out, sems_u.at[26])
    keep_u.start()
    for j in range(4):
        cols = slice(j * D, (j + 1) * D)
        hid = mm(mlp_in[...], wu[:, cols]) + up_bias[:, cols]
        hidden[:, cols] = hid
        part = jax.nn.gelu(hid, approximate=True)
        act[:, cols] = part.astype(BF)
        turned = part.T.astype(BF)
        act_t[0, j] = turned[: D // 2]
        act_t[1, j] = turned[D // 2 :]
    wait_d()
    keep_d = pltpu.make_async_copy(wd, wd_out, sems_d.at[26])
    keep_d.start()
    branch[...] = mm(act[...], wd[...]) + down_bias[...]
    y[...] = (mid[...] + row(ada, 5) * branch[...]).astype(BF)
    keep_u.wait()
    keep_d.wait()


def mlp(block, mid, mlp_in, ada, biases, gathered):
    t = mid.shape[0]
    return pl.pallas_call(
        functools.partial(mlp_kernel, block),
        out_shape=(
            shape_of(BF, D, FF),
            shape_of(BF, FF, D),
            shape_of(F32, t, FF),
            shape_of(BF, 2, NZ, D // 2, t),
            shape_of(F32, t, D),
            shape_of(BF, t, D),
        ),
        in_specs=[INSIDE] * 5 + [ANYWHERE] * 9,
        out_specs=(ANYWHERE,) * 2 + (INSIDE,) * 4,
        scratch_shapes=[
            pltpu.VMEM((D, FF), BF),
            pltpu.VMEM((FF, D), BF),
            pltpu.VMEM((t, FF), BF),
            pltpu.SemaphoreType.DMA((27,)),
            pltpu.SemaphoreType.DMA((27,)),
        ],
        compiler_params=PARAMS,
        cost_estimate=cost(8 * D * FF, 4 * t * D * FF),
    )(mid, mlp_in, ada, biases[2], biases[3], *gathered)


def column_sum(v):
    return jnp.sum(v, axis=0, keepdims=True)


def norm_back(g, n, rstd):
    return rstd * (
        g - jnp.mean(g, axis=-1, keepdims=True) - n * jnp.mean(g * n, axis=-1, keepdims=True)
    )


def gelu_slope(v):
    c = math.sqrt(2.0 / math.pi)
    t = jnp.tanh(c * (v + 0.044715 * v * v * v))
    return 0.5 * (1.0 + t) + 0.5 * v * (1.0 - t * t) * (c * (1.0 + 3.0 * 0.044715 * v * v))


def mlp_back_kernel(*refs):
    grad, d_branch, ada, mid, attended, hidden, branch, wu_in, wd_in = refs[:9]
    d_hidden, d_mid, d_att, stats, wu, wd, acc, sems = refs[10:]
    copies = []
    for j in range(4):
        part = slice(j * D, (j + 1) * D)
        down = pltpu.make_async_copy(wd_in.at[part, :], wd.at[part, :], sems.at[2 * j])
        up = pltpu.make_async_copy(wu_in.at[:, part], wu.at[:, part], sems.at[2 * j + 1])
        copies.append((down, up))
    for down, up in copies:
        down.start()
        up.start()
    stats[...] = jnp.zeros_like(stats)
    stats[5:6, :] = column_sum(grad[...].astype(F32) * branch[...])
    stats[13:14, :] = column_sum(d_branch[...].astype(F32))
    for j in range(4):
        part = slice(j * D, (j + 1) * D)
        copies[j][0].wait()
        d_act = mmt(d_branch[...], wd[part, :])
        d_hid = (d_act * gelu_slope(hidden[:, part])).astype(BF)
        d_hidden[j // 2, :, (j % 2) * D : (j % 2 + 1) * D] = d_hid
        stats[9 + j : 10 + j, :] = column_sum(d_hid.astype(F32))
        copies[j][1].wait()
        product = mmt(d_hid, wu[:, part])
        if j == 0:
            acc[...] = product
        else:
            acc[...] += product
    n2, r2 = standard(mid[...])
    stats[3:4, :] = column_sum(acc[...])
    stats[4:5, :] = column_sum(acc[...] * n2)
    whole = grad[...].astype(F32) + norm_back(acc[...] * (1.0 + row(ada, 4)), n2, r2)
    d_mid[...] = whole
    d_att[...] = (row(ada, 2) * whole).astype(BF)
    stats[2:3, :] = column_sum(whole * attended[...])
    stats[8:9, :] = column_sum(d_att[...].astype(F32))


def mlp_back(grad, d_branch, ada, mid, attended, hidden, branch, wu, wd, after):
    t = grad.shape[0]
    return pl.pallas_call(
        mlp_back_kernel,
        out_shape=(
            shape_of(BF, 2, t, HALF),
            shape_of(F32, t, D),
            shape_of(BF, t, D),
            shape_of(F32, 16, D),
        ),
        in_specs=[INSIDE] * 7 + [ANYWHERE] * 3,
        out_specs=(INSIDE,) * 4,
        scratch_shapes=[
            pltpu.VMEM((D, FF), BF),
            pltpu.VMEM((FF, D), BF),
            pltpu.VMEM((t, D), F32),
            pltpu.SemaphoreType.DMA((8,)),
        ],
        compiler_params=PARAMS,
        cost_estimate=free(),
    )(grad, d_branch, ada, mid, attended, hidden, branch, wu, wd, after)


def attend_back_kernel(*refs):
    x, d_mid, d_att, ada, q_ref, k_ref, v_ref, stats, w_in = refs[:9]
    out, d_x, d_x_low, small, w, mixed, sem = refs[10:]
    copies = [
        pltpu.make_async_copy(w_in.at[:, 3 * D :], w.at[:, 3 * D :], sem.at[0]),
        pltpu.make_async_copy(w_in.at[:, : 3 * D], w.at[:, : 3 * D], sem.at[1]),
    ]
    for copy in copies:
        copy.start()
    copies[0].wait()
    mixed[...] = mmt(d_att[...], w[:, 3 * D :]).astype(BF)
    for h in range(HEADS):
        cols = head_cols(h)
        q, k, v, dm = (ref[:, cols] for ref in (q_ref, k_ref, v_ref, mixed))
        soft = softmax_of(q, k)
        d_probs = mmt(dm, v)
        inner = jnp.sum(d_probs * soft, axis=-1, keepdims=True)
        d_s = (soft * (d_probs - inner)).astype(BF)
        out[0, :, cols] = (mm(d_s, k) * HEAD_DIM**-0.5).astype(BF)
        out[0, :, head_cols(h, D)] = tdot(d_s, q).astype(BF)
        out[1, :, cols] = tdot(soft.astype(BF), dm).astype(BF)
    out[1, :, D:] = d_att[...]
    copies[1].wait()
    d_in = mmt(out[0, :, :D], w[:, :D])
    d_in += mmt(out[0, :, D:], w[:, D : 2 * D])
    d_in += mmt(out[1, :, :D], w[:, 2 * D : 3 * D])
    n1, r1 = standard(x[...].astype(F32))
    rows = [
        column_sum(d_in),
        column_sum(d_in * n1),
        stats[2:6, :],
        column_sum(out[0, :, :D].astype(F32)),
        column_sum(out[1, :, :D].astype(F32)),
        stats[8:, :],
    ]
    small[...] = jnp.concatenate(rows, axis=0).astype(BF)
    whole = d_mid[...] + norm_back(d_in * (1.0 + row(ada, 1)), n1, r1)
    d_x[...] = whole
    d_x_low[...] = whole.astype(BF)


def attend_back(x, d_mid, d_att, ada, q, k, v, stats, wa, after):
    t = x.shape[0]
    return pl.pallas_call(
        attend_back_kernel,
        out_shape=(
            shape_of(BF, 2, t, HALF),
            shape_of(F32, t, D),
            shape_of(BF, t, D),
            shape_of(BF, 16, D),
        ),
        in_specs=[INSIDE] * 8 + [ANYWHERE] * 2,
        out_specs=(INSIDE,) * 4,
        scratch_shapes=[
            pltpu.VMEM((D, FF), BF),
            pltpu.VMEM((t, D), BF),
            pltpu.SemaphoreType.DMA((2,)),
        ],
        compiler_params=PARAMS,
        cost_estimate=free(),
    )(x, d_mid, d_att, ada, q, k, v, stats, wa, after)


def far_half(halves):
    c = lax.axis_index(S)
    return swap(lax.dynamic_index_in_dim(halves, 1 - c, 0, keepdims=False))


def rows_sum(v):
    return jnp.sum(v.astype(F32), axis=0)


def embed_time(steps):
    half = D // 2
    freq = jnp.exp(-math.log(10000.0) * jnp.arange(half, dtype=F32) / half)
    angles = steps.astype(F32)[:, None] * freq[None, :]
    return jnp.concatenate([jnp.cos(angles), jnp.sin(angles)], axis=-1)


def across(value):
    out = value[None]
    bit = 1
    while bit < lax.axis_size(R):
        out = jnp.concatenate([out, cross(out, bit)])
        bit *= 2
    return out


def in_order(value):
    nr = lax.axis_size(R)
    return jnp.take(value, lax.axis_index(R) ^ jnp.arange(nr), axis=0)


def per_device(
    inputs,
    cotangent,
    timesteps,
    labels,
    class_table,
    qkv_weight,
    qv_bias,
    proj_weight,
    proj_bias,
    up_weight,
    up_bias,
    down_weight,
    down_bias,
    ada_weight,
    ada_bias,
):
    c = lax.axis_index(S)
    z = lax.axis_index(Z)
    is_first = c == 0

    ids = jnp.concatenate([timesteps, labels], axis=1)
    vectors = [v[0].astype(F32) for v in (qv_bias, proj_bias, up_bias, down_bias, ada_bias)]
    small = along_z(jnp.concatenate(vectors + [ids.reshape(-1).astype(F32)]))
    ids_z = small[:, -4:].astype(jnp.int32).reshape(NZ, 2, 2)
    vec_mine = small[:, :-4]
    vec_other = swap(vec_mine)

    def cond_of(steps, classes):
        return embed_time(steps) + jnp.take(class_table, classes, axis=0).astype(F32)

    cond_z = cond_of(ids_z[..., 0].reshape(-1), ids_z[..., 1].reshape(-1))
    silu_z = jax.nn.silu(cond_z).astype(BF)
    rows_z = lax.dynamic_slice_in_dim(silu_z, z * ROWS, ROWS, 1)
    partial = mm(rows_z, ada_weight[0]).reshape(NZ, 2, -1)
    ada_sum = jnp.sum(trade(partial), axis=0)
    lengths = (qv_bias.shape[1], proj_bias.shape[1], up_bias.shape[1], down_bias.shape[1], ada_bias.shape[1])

    def split_vectors(vec):
        out = []
        at = 0
        for n in lengths:
            out.append(vec[:, at : at + n].reshape(-1))
            at += n
        return out

    mine_split = split_vectors(vec_mine)
    other_split = split_vectors(vec_other)
    ada_sum = ada_sum + mine_split[4][None]
    ada_keep = lax.dynamic_index_in_dim(ada_sum, c, 0, keepdims=False)
    ada_got = swap(lax.dynamic_index_in_dim(ada_sum, 1 - c, 0, keepdims=False))
    adas = []
    biases = []
    for block in range(2):
        here = c == block
        adas.append(jnp.where(here, ada_keep, ada_got).reshape(6, D))
        biases.append(
            [jnp.where(here, a, b)[None] for a, b in zip(mine_split[:4], other_split[:4])]
        )

    mine = ((qkv_weight[0], proj_weight[0]), (up_weight[0],), (down_weight[0],))
    other = tuple(tuple(swap(w) for w in group) for group in mine)
    gatherer = Gatherer(mine, other, qkv_weight[0])
    x = lax.dynamic_index_in_dim(inputs, c, 0, keepdims=False)[0]
    cot = lax.dynamic_index_in_dim(cotangent, c, 0, keepdims=False)[0]
    kept = []
    kept_mlp = []

    def run_attend(block, value):
        got = attend(block, value, adas[block], biases[block], gatherer.operands(2 * block))
        gatherer.after = got[-1]
        kept.append(got)
        return swap(got[1])

    def run_mlp(block):
        mid, mlp_in = kept[block][-2:]
        got = mlp(block, mid, mlp_in, adas[block], biases[block], gatherer.operands(2 * block + 1))
        gatherer.after = got[-1]
        kept_mlp.append(got)
        return far_half(got[3]), swap(mlp_in)

    def branch_grad(block, grad):
        return (adas[block][5:] * grad.astype(F32)).astype(BF)

    for g in range(4):
        gatherer.extract(g)
    ids_all = in_order(across(ids_z)).reshape(-1, 2)
    gatherer.stack(0)
    (ids_all,) = gatherer.hold(ids_all)
    gatherer.onward(0)
    d_branch1 = branch_grad(1, cot)
    far_branch1 = swap(d_branch1)
    gatherer.share(0)
    gatherer.stack(1)
    far_sides0 = run_attend(0, x)
    gatherer.stack(2)
    far_sides0, far_branch1 = gatherer.hold(far_sides0, far_branch1)
    gatherer.onward(1)
    gatherer.share(1)
    gatherer.onward(2)
    gatherer.stack(3)
    far_mlp0 = run_mlp(0)
    y0 = kept_mlp[0][5]
    gatherer.share(2)
    far_mlp0 = gatherer.hold(*far_mlp0)
    far_sides1 = run_attend(1, y0)
    gatherer.onward(3)
    (far_sides1,) = gatherer.hold(far_sides1)
    gatherer.share(3)
    far_mlp1 = run_mlp(1)
    y1 = kept_mlp[1][5]

    reducer = Reducer(y1)

    def run_mlp_back(block, grad, d_branch):
        attended, mid, mlp_in = kept[block][-3:]
        wu, wd, hidden, act_t, branch, _ = kept_mlp[block]
        got = mlp_back(
            grad, d_branch, adas[block], mid, attended, hidden, branch, wu, wd, reducer.after
        )
        reducer.after = got[0]
        return got, far_half(got[0])

    def run_attend_back(block, value, back):
        wa, sides, q, k, v = kept[block][:5]
        _, d_mid, d_att, stats = back
        got = attend_back(
            value, d_mid, d_att, adas[block], q, k, v, stats, wa, reducer.after
        )
        reducer.after = got[2]
        return got

    def begin(block, kind, mode, *operands):
        reducer.begin(block, kind, mode, operands)

    back1, far_hidden1 = run_mlp_back(1, cot, d_branch1)
    begin(1, 2, 0, kept_mlp[1][3], far_mlp1[0], d_branch1, far_branch1)
    begin(1, 1, 3, kept[1][-1], far_mlp1[1], back1[0], far_hidden1)
    d_all1, dx1f, dx1, small1 = run_attend_back(1, y0, back1)
    far_all1 = far_half(d_all1)
    d_branch0 = branch_grad(0, dx1)
    far_branch0 = swap(d_branch0)
    reducer.first(1)
    begin(1, 0, 3, kept[1][1], far_sides1, d_all1, far_all1)
    back0, far_hidden0 = run_mlp_back(0, dx1, d_branch0)
    begin(0, 2, 3, kept_mlp[0][3], far_mlp0[0], d_branch0, far_branch0)
    reducer.first(2)
    begin(0, 1, 3, kept[0][-1], far_mlp0[1], back0[0], far_hidden0)
    reducer.first(0)
    reducer.second(1)
    d_all0, dx0, dx0_low, small0 = run_attend_back(0, x, back0)
    far_all0 = far_half(d_all0)
    reducer.first(3)
    reducer.third(1)
    reducer.second(2)
    begin(0, 0, 3, kept[0][1], far_sides0, d_all0, far_all0)
    small_keep = jnp.where(is_first, small0, small1)
    small_got = swap(jnp.where(is_first, small1, small0))
    reducer.first(4)
    reducer.third(2)
    reducer.second(3)
    reducer.second(0)
    (small_got,) = reducer.hold(small_got)
    small = jnp.stack(
        [jnp.where(is_first, small_keep, small_got), jnp.where(is_first, small_got, small_keep)]
    )
    block1, block0, last = (2, 1, 0), (2, 1), (0,)
    reducer.first(5)
    reducer.third(0)
    reducer.unite(1, block1)
    reducer.third(3)
    small = along_z(small)
    reducer.spread(1, block1)
    (small,) = reducer.hold(small)
    small = small[None]
    bits = [1 << i for i in range(lax.axis_size(R).bit_length() - 1)]
    hop = cross(small, 1)
    reducer.second(4)
    reducer.second(5)
    reducer.third(4)
    reducer.unite(0, block0)
    reducer.spread_on(1, block1)
    (hop,) = reducer.hold(hop)
    small = jnp.concatenate([small, hop])
    hop = cross(small, 2)
    reducer.spread(0, block0)
    reducer.third(5)
    reducer.unite(0, last)
    (hop,) = reducer.hold(hop)
    small = jnp.concatenate([small, hop])
    for bit in bits[2:]:
        small = jnp.concatenate([small, cross(small, bit)])
    reducer.spread_on(0, block0)
    reducer.spread(0, last)
    reducer.spread_on(0, last)
    reducer.finish(1, block1)
    reducer.finish(0, block0)
    reducer.finish(0, last)
    (qkv_grad, proj_grad), (up_grad,), (down_grad,) = (reducer.results[k] for k in range(3))

    def both_micros(v0, v1):
        keep = jnp.where(is_first, v0, v1)
        got = swap(jnp.where(is_first, v1, v0))
        return jnp.stack([jnp.where(is_first, keep, got), jnp.where(is_first, got, keep)])

    block_outputs = both_micros(y0, y1)[None, :, None]
    input_grads = both_micros(dx0, dx1.astype(F32))[None, :, None]

    small = in_order(small).reshape(-1, 16, D)
    sums = rows_sum(small[:, 6:14])
    dada_own = small[:, :6].reshape(-1, 6 * D)

    def own_slice(vec):
        vec = vec.reshape(-1)
        n = vec.shape[0] // NZ
        return lax.dynamic_slice_in_dim(vec, z * n, n, 0)[None]

    qv_bias_grad = own_slice(sums[:2])
    proj_bias_grad = own_slice(sums[2])
    up_bias_grad = own_slice(sums[3:7])
    down_bias_grad = own_slice(sums[7])

    cond_all = cond_of(ids_all[:, 0], ids_all[:, 1])
    labels_all = ids_all[:, 1]
    cond_rows = lax.dynamic_slice_in_dim(cond_all, z * ROWS, ROWS, 1)
    silu_rows = jax.nn.silu(cond_rows).astype(BF)
    ada_grad = lax.dot_general(
        silu_rows, dada_own, (((0,), (0,)), ((), ())), preferred_element_type=F32
    )
    ada_bias_grad = own_slice(rows_sum(dada_own))
    d_silu = mmt(dada_own, ada_weight[0])
    _, silu_back = jax.vjp(jax.nn.silu, cond_rows)
    d_cond = silu_back(d_silu)[0]
    d_cond = d_cond + swap(d_cond)
    d_cond_all = along_z(d_cond).transpose(1, 0, 2).reshape(-1, D)
    row_count = class_table.shape[0] // (2 * NZ)
    row_ids = (c * NZ + z) * row_count + jnp.arange(row_count, dtype=jnp.int32)
    owner = (row_ids[:, None] == labels_all[None, :]).astype(F32)
    table_grad = jnp.dot(owner, d_cond_all, precision=lax.Precision.HIGHEST)

    return (
        block_outputs,
        input_grads,
        table_grad,
        qkv_grad[None],
        qv_bias_grad,
        proj_grad[None],
        proj_bias_grad,
        up_grad[None],
        up_bias_grad,
        down_grad[None],
        down_bias_grad,
        ada_grad[None],
        ada_bias_grad,
    )


def solution(mesh):
    rows = P(None, (Z, R), None, None)
    matrix = P(S, Z, None)
    vector = P(S, Z)
    pair = P(None, (Z, R))
    in_specs = (rows, rows, pair, pair, P()) + (matrix, vector) * 5
    acts = P(S, None, (Z, R), None, None)
    out_specs = (acts, acts, P((S, Z), None)) + (matrix, vector) * 5
    return jax.shard_map(
        per_device, mesh=mesh, in_specs=in_specs, out_specs=out_specs, check_vma=False
    )
```

```python
import functools
import math

import jax
import jax.numpy as jnp
from jax import lax
from jax.experimental import pallas as pl
from jax.experimental.pallas import tpu as pltpu
from jax.sharding import PartitionSpec as P

S = "section"
Z = "shard"
R = "replica"
ALL = (S, Z, R)
BF = jnp.bfloat16
F32 = jnp.float32
D = 1152
HEAD_DIM = 72
HEADS = 16
FF = 4608
HALF = 2304
ROWS = 288
PIECE = 144
NZ = 4
SHARDS = (1, 2, 3)
VMEM_LIMIT = 50 * 1024 * 1024


def move(value, to):
    ns, nz, nr = (lax.axis_size(a) for a in ALL)
    pairs = []
    for s in range(ns):
        for z in range(nz):
            for r in range(nr):
                there = to(s, z, r)
                if there is not None:
                    a, b, c = there
                    pairs.append(((s * nz + z) * nr + r, (a * nz + b) * nr + c))
    return lax.ppermute(value, ALL, pairs)


def swap(value):
    return move(value, lambda s, z, r: (1 - s, z, r))


def to_core(value, core):
    return move(value, lambda s, z, r: (core, z, r) if s != core else None)


def zshift(value, by=1):
    nz = lax.axis_size(Z)
    return move(value, lambda s, z, r: (s, (z + by) % nz, r))


def trade(value):
    return lax.all_to_all(value, Z, split_axis=0, concat_axis=0, tiled=True)


def along_z(value):
    return trade(jnp.stack([value] * NZ))


def cross(value, bit):
    return move(value, lambda s, z, r: (s, z, r ^ bit))


def place():
    return lax.axis_index(S), lax.axis_index(Z), lax.rem(lax.axis_index(R), 4)


ANYWHERE = pl.BlockSpec(memory_space=pl.ANY)
INSIDE = pl.BlockSpec(memory_space=pltpu.VMEM)
PARAMS = pltpu.CompilerParams(vmem_limit_bytes=VMEM_LIMIT)
ONE = jax.ShapeDtypeStruct((PIECE, D), BF)


def cost(nbytes, flops=0):
    return pl.CostEstimate(flops=flops, bytes_accessed=nbytes, transcendentals=0)


def free():
    return pl.CostEstimate(flops=0, bytes_accessed=0, transcendentals=0)


def fence(arrays, after):
    n = len(arrays)
    return pl.pallas_call(
        lambda *refs: None,
        out_shape=tuple(jax.ShapeDtypeStruct(a.shape, a.dtype) for a in arrays),
        in_specs=[ANYWHERE] * (n + 1),
        out_specs=(ANYWHERE,) * n,
        input_output_aliases={i: i for i in range(n)},
        cost_estimate=free(),
    )(*arrays, after)


def stack_kernel(every, _, out):
    z = lax.axis_index(Z)
    for i in range(every.shape[1]):
        for k in SHARDS:
            out[i, k - 1] = every[lax.rem(z + NZ - k, NZ), i]


def stacked(every, after):
    n = every.shape[1]
    return pl.pallas_call(
        stack_kernel,
        out_shape=jax.ShapeDtypeStruct((n, 3, PIECE, D), BF),
        in_specs=[INSIDE, ANYWHERE],
        out_specs=INSIDE,
        compiler_params=PARAMS,
        cost_estimate=cost(12 * n * PIECE * D),
    )(every, after)


def collect_kernel(p0, p1, p2, _, big, to_x, to_y):
    n = p0.shape[0]
    for m, part in enumerate((p0, p1, p2)):
        big[m] = part[...]
    if n == 2:
        to_x[...] = p2[:1]
        to_y[...] = p1[1:]
    else:
        to_x[...] = p2[:, :1]
        to_y[...] = p1[:, 1:]


def collected(p0, p1, p2, after):
    n = p0.shape[0]
    if n == 2:
        cut = (1, 3), (1, 3)
    else:
        cut = (1, 1), (1, 2)
    shapes = ((3, n, 3), *cut)
    return pl.pallas_call(
        collect_kernel,
        out_shape=tuple(jax.ShapeDtypeStruct((*s, PIECE, D), BF) for s in shapes),
        in_specs=[INSIDE] * 3 + [ANYWHERE],
        out_specs=(INSIDE,) * 3,
        compiler_params=PARAMS,
        cost_estimate=cost(1),
    )(p0, p1, p2, after)


def combine_kernel(pa, pb, _, out):
    if out.shape[0] == 2:
        out[:1] = pa[...]
        out[1:] = pb[...]
    else:
        out[:, :1] = pa[...]
        out[:, 1:] = pb[...]


def combined(pa, pb, after):
    n = 2 if pa.shape[1] == 3 else 1
    return pl.pallas_call(
        combine_kernel,
        out_shape=jax.ShapeDtypeStruct((n, 3, PIECE, D), BF),
        in_specs=[INSIDE] * 2 + [ANYWHERE],
        out_specs=INSIDE,
        compiler_params=PARAMS,
        cost_estimate=cost(1),
    )(pa, pb, after)


def join_kernel(*refs):
    out = refs[-1]
    for i in range(out.shape[0]):
        out[i] = refs[i][...]


def joined(parts, after):
    n = len(parts)
    return pl.pallas_call(
        join_kernel,
        out_shape=jax.ShapeDtypeStruct((n, PIECE, D), BF),
        in_specs=[INSIDE] * n + [ANYWHERE],
        out_specs=INSIDE,
        compiler_params=PARAMS,
        cost_estimate=free(),
    )(*parts, after)


def plus_kernel(n, *refs):
    outs = refs[2 * n + 1 :]
    for i in range(n):
        for j in range(2):
            whole = refs[i][j].astype(F32) + refs[n + i][j].astype(F32)
            outs[2 * i + j][...] = whole.astype(BF)


def plus(a, b, after):
    n = len(a)
    shapes = [jax.ShapeDtypeStruct(v.shape[1:], BF) for v in a for _ in range(2)]
    return pl.pallas_call(
        functools.partial(plus_kernel, n),
        out_shape=tuple(shapes),
        in_specs=[INSIDE] * (2 * n) + [ANYWHERE],
        out_specs=(INSIDE,) * (2 * n),
        compiler_params=PARAMS,
        cost_estimate=free(),
    )(*a, *b, after)


def merge_kernel(n, *refs):
    out = refs[-1]
    for i in range(n):
        whole = refs[i][...].astype(F32) + refs[n + i][...].astype(F32)
        rows = refs[i].shape[0]
        out[i * rows : (i + 1) * rows] = whole.astype(BF)


def merged(a, b, after):
    n = len(a)
    return pl.pallas_call(
        functools.partial(merge_kernel, n),
        out_shape=jax.ShapeDtypeStruct((NZ, PIECE, D), BF),
        in_specs=[INSIDE] * (2 * n) + [ANYWHERE],
        out_specs=INSIDE,
        compiler_params=PARAMS,
        cost_estimate=free(),
    )(*a, *b, after)


def sum_kernel(n, *refs):
    if n == 1:
        parts = [refs[0][i] for i in range(refs[0].shape[0])]
    else:
        parts = [ref[...] for ref in refs[:n]]
    whole = parts[0].astype(F32)
    for part in parts[1:]:
        whole = whole + part.astype(F32)
    refs[-1][...] = whole.astype(BF)


def summed(parts, after):
    n = len(parts)
    return pl.pallas_call(
        functools.partial(sum_kernel, n),
        out_shape=ONE,
        in_specs=[INSIDE] * n + [ANYWHERE],
        out_specs=INSIDE,
        compiler_params=PARAMS,
        cost_estimate=free(),
    )(*parts, after)


def fold_kernel(parts, _, keep, send):
    for m in range(4):
        whole = parts[0, m].astype(F32)
        for i in SHARDS:
            whole = whole + parts[i, m].astype(F32)
        (send if m % 2 else keep)[m // 2] = whole.astype(BF)


def folded(parts, after):
    half = jax.ShapeDtypeStruct((2, PIECE, D), BF)
    return pl.pallas_call(
        fold_kernel,
        out_shape=(half, half),
        in_specs=[INSIDE, ANYWHERE],
        out_specs=(INSIDE, INSIDE),
        compiler_params=PARAMS,
        cost_estimate=free(),
    )(parts, after)


def pair_kernel(own, far, _, out):
    c = lax.axis_index(S)
    for core in range(2):

        @pl.when(c == core)
        def _():
            for i in range(own.shape[0]):
                out[i, core] = own[i]
                out[i, 1 - core] = far[i]


def paired(own, far, after):
    return pl.pallas_call(
        pair_kernel,
        out_shape=jax.ShapeDtypeStruct((own.shape[0], 2, PIECE, D), BF),
        in_specs=[INSIDE] * 2 + [ANYWHERE],
        out_specs=INSIDE,
        compiler_params=PARAMS,
        cost_estimate=free(),
    )(own, far, after)


def chosen(block, mine, other, act):
    c = lax.axis_index(S)

    @pl.when(c == block)
    def _():
        act(mine)

    @pl.when(c != block)
    def _():
        act(other)


def arrays_of(kind):
    return 2 if kind == 0 else 1


def extract_kernel(items, *refs):
    out, sems = refs[-2:]
    c, z, r = place()
    unit = c * 2 + r // 2
    at = 0
    for i, (block, kind) in enumerate(items):
        n = arrays_of(kind)
        mine, other = refs[at : at + n], refs[at + n : at + 2 * n]
        at += 2 * n

        def copy(source):
            pltpu.make_async_copy(source, out.at[i], sems.at[i]).start()

        def act(source):
            if kind == 2:
                copy(source[0].at[pl.ds((c * 4 + r) * PIECE, PIECE), :])
                return
            height = pl.ds(lax.rem(r, 2) * PIECE, PIECE)

            def take(ref, index):
                cols = pl.ds(pl.multiple_of(index * D, D), D)
                copy(ref.at[height, cols])

            if kind == 1:
                take(source[0], unit)
                return

            @pl.when(unit == 3)
            def _():
                take(source[1], 0)

            @pl.when(unit != 3)
            def _():
                take(source[0], unit)

        chosen(block, mine, other, act)
    for i in range(len(items)):
        pltpu.make_async_copy(out.at[i], out.at[i], sems.at[i]).wait()


def extract(items, mine, other, after):
    n = len(items)
    operands = []
    for _, kind in items:
        operands += [*mine[kind], *other[kind]]
    return pl.pallas_call(
        functools.partial(extract_kernel, items),
        out_shape=jax.ShapeDtypeStruct((n, PIECE, D), BF),
        in_specs=[ANYWHERE] * (len(operands) + 1),
        out_specs=INSIDE,
        scratch_shapes=[pltpu.SemaphoreType.DMA((n,))],
        compiler_params=PARAMS,
        cost_estimate=cost(4 * n * PIECE * D),
    )(*operands, after)


def weight_copies(block, kind, index, mine, other, own, far, out, sems):
    n = arrays_of(kind)
    c, z, r = place()
    copies = []
    height = D if kind == 2 else ROWS
    rows = pl.ds(z * height, height)
    if kind == 0:
        targets = (out.at[rows, pl.ds(0, 3 * D)], out.at[rows, pl.ds(3 * D, D)])
    else:
        targets = (out.at[rows, :],)

    def act(source):
        for i in range(n):
            pltpu.make_async_copy(source[i], targets[i], sems.at[i]).start()

    chosen(block, mine, other, act)
    for side, group in ((0, own), (1, far)):
        core = c if side == 0 else 1 - c
        for m in range(4):
            low = lax.rem(r + m, 2)
            high = lax.rem(r // 2 + m // 2, 2)
            for k in SHARDS:
                zp = lax.rem(z + NZ - k, NZ)
                if kind == 2:
                    row = zp * D + core * (D // 2) + (high * 2 + low) * PIECE
                    spot = out.at[pl.ds(row, PIECE), :]
                else:
                    row = zp * ROWS + low * PIECE
                    col = pl.multiple_of((core * 2 + high) * D, D)
                    spot = out.at[pl.ds(row, PIECE), pl.ds(col, D)]
                if m < 3:
                    piece = group[0].at[m, index, k - 1]
                else:
                    piece = group[1].at[index, k - 1]
                sem = sems.at[2 + (side * 4 + m) * 3 + k - 1]
                copies.append(pltpu.make_async_copy(piece, spot, sem))
    for copy in copies:
        copy.start()

    def wait():
        for i in range(n):
            pltpu.make_async_copy(mine[i], targets[i], sems.at[i]).wait()
        for copy in copies:
            copy.wait()

    return wait


GROUPS = (((0, 0),), ((0, 1), (0, 2)), ((1, 0),), ((1, 1), (1, 2)))


class Gatherer:
    def __init__(self, mine, other, after):
        self.mine = mine
        self.other = other
        self.after = after
        self.state = {}

    def extract(self, g):
        self.after = extract(GROUPS[g], self.mine, self.other, self.after)
        self.state[g] = lax.all_gather(self.after, Z, axis=0, tiled=False)

    def stack(self, g):
        p0 = stacked(self.state[g], self.after)
        self.after = p0
        self.state[g] = p0, cross(p0, 1), cross(p0, 2)

    def onward(self, g):
        big, to_x, to_y = collected(*self.state[g], self.after)
        self.after = to_x
        self.state[g] = big, (cross(to_x, 1), cross(to_y, 2)), swap(big)

    def share(self, g):
        big, p3, far = self.state[g]
        p3 = combined(*p3, self.after)
        self.after = p3
        self.state[g] = (big, p3), (far, swap(p3))

    def hold(self, *values):
        values = fence(values, self.after)
        self.after = values[0]
        return values

    def operands(self, g):
        own, far = self.state[g]
        shards = []
        for _, kind in GROUPS[g]:
            shards += [*self.mine[kind], *self.other[kind]]
        return (*own, *far, *shards, self.after)


def tdot(a, b):
    return lax.dot_general(a, b, (((0,), (0,)), ((), ())), preferred_element_type=F32)


def wgrad_kernel(kind, mode, *refs):
    n = 4
    ins = refs[:n]
    outs = refs[n + 1 : -1]
    acc = refs[-1]
    c, z, r = place()
    for g in range(2):
        u = lax.rem(g + r // 2, 2)
        if kind == 2:
            lo, lx, ro, rx = ins
            for zp in range(NZ):
                rows = pl.ds(pl.multiple_of(u * ROWS, ROWS), ROWS)
                acc[zp * ROWS : (zp + 1) * ROWS, :] = jnp.dot(
                    lo[c, zp, rows, :], ro[...], preferred_element_type=F32
                ) + jnp.dot(lx[zp, rows, :], rx[...], preferred_element_type=F32)
        else:
            ro, rx = ins[-2:]
            cols = pl.ds(pl.multiple_of(u * D, D), D)

            def product(lo, lx):
                acc[...] = tdot(lo[...], ro[c, :, cols]) + tdot(lx[...], rx[:, cols])

            if kind == 1:
                product(ins[0], ins[1])
            else:

                @pl.when(c * u == 0)
                def _():
                    product(ins[0].at[0], ins[1].at[0])

                @pl.when(c * u == 1)
                def _():
                    product(ins[0].at[1], ins[1].at[1])

        for par in range(2):

            @pl.when(lax.rem(r, 2) == par)
            def _():
                for zp in range(NZ):
                    for h in range(2):
                        start = (zp * 2 + h) * PIECE
                        piece = acc[start : start + PIECE, :].astype(BF)
                        low = h ^ par
                        if mode == 0:
                            outs[0][zp, g * 2 + low] = piece
                        elif mode == 1:
                            outs[low][g, zp] = piece
                        elif mode == 2:
                            outs[g][low, zp] = piece
                        elif zp < 2:
                            outs[low][g, zp] = piece
                        else:
                            outs[2 + g][low, zp - 2] = piece


def wgrad(kind, mode, operands, after):
    leading = ((4, 4), (2, 4), (2, 4), (2, 2))[mode]
    count = (1, 2, 2, 4)[mode]
    part = jax.ShapeDtypeStruct((*leading, PIECE, D), BF)
    return pl.pallas_call(
        functools.partial(wgrad_kernel, kind, mode),
        out_shape=(part,) * count,
        in_specs=[INSIDE] * len(operands) + [ANYWHERE],
        out_specs=(INSIDE,) * count,
        scratch_shapes=[pltpu.VMEM((D, D), F32)],
        compiler_params=PARAMS,
        cost_estimate=free(),
    )(*operands, after)


def finish_kernel(block, kinds, *refs):
    count = len(kinds)
    outs = list(refs[-4 - count - (0 in kinds) : -4])
    raw, acc, sems_in, sems_out = refs[-4:]
    p0, p1, p2, pa, pb = refs[:5]
    c, z, r = place()

    @pl.when(c == block)
    def _():
        copies = []
        for i in range(count):
            for core in range(2):
                flat = i * 2 + core
                last = pa.at[flat] if flat < count else pb.at[flat - count]
                sources = (p0.at[i, core], p1.at[i, core], p2.at[i, core], last)
                for m, piece in enumerate(sources):
                    n = flat * 4 + m
                    copies.append(pltpu.make_async_copy(piece, raw.at[n], sems_in.at[n]))
                    copies[-1].start()
        done = []
        at_out = 0
        for i, kind in enumerate(kinds):
            base = i * 4 * ROWS
            for core in range(2):
                for m in range(4):
                    n = (i * 2 + core) * 4 + m
                    copies[n].wait()
                    low = lax.rem(r + m, 2)
                    unit = core * 2 + lax.rem(r // 2 + m // 2, 2)
                    at = pl.multiple_of(base + unit * ROWS + low * PIECE, PIECE)
                    acc[pl.ds(at, PIECE), :] = raw[n].astype(F32)
            if kind == 2:
                moves = [(acc.at[base : base + D, :], outs[at_out])]
            else:
                moves = []
                for unit in range(4):
                    source = acc.at[base + unit * ROWS : base + (unit + 1) * ROWS, :]
                    if kind == 0 and unit == 3:
                        moves.append((source, outs[at_out + 1]))
                    else:
                        cols = outs[at_out].at[:, unit * D : (unit + 1) * D]
                        moves.append((source, cols))
            at_out += 2 if kind == 0 else 1
            for source, target in moves:
                done.append(pltpu.make_async_copy(source, target, sems_out.at[len(done)]))
                done[-1].start()
        for copy in done:
            copy.wait()


def finish(block, kinds, pieces, before, after):
    shapes = []
    for kind in kinds:
        shapes += [[(ROWS, 3 * D), (ROWS, D)], [(ROWS, FF)], [(D, D)]][kind]
    count = len(kinds)
    return pl.pallas_call(
        functools.partial(finish_kernel, block, kinds),
        out_shape=tuple(pltpu.HBM(s, F32) for s in shapes),
        in_specs=[ANYWHERE] * (6 + len(before)),
        out_specs=(ANYWHERE,) * len(shapes),
        scratch_shapes=[
            pltpu.VMEM((8 * count, PIECE, D), BF),
            pltpu.VMEM((4 * count * ROWS, D), F32),
            pltpu.SemaphoreType.DMA((8 * count,)),
            pltpu.SemaphoreType.DMA((12,)),
        ],
        input_output_aliases={6 + i: i for i in range(len(before))},
        compiler_params=PARAMS,
        cost_estimate=free(),
    )(*pieces, after, *before)


def on_core(value, bit, core):
    return move(value, lambda s, z, r: (s, z, r ^ bit) if s == core else None)


class Reducer:
    def __init__(self, after):
        self.after = after
        self.items = []
        self.modes = []
        self.state = []
        self.own = {}
        self.ready = {}
        self.results = {}

    def begin(self, block, kind, mode, operands):
        out = wgrad(kind, mode, operands, self.after)
        self.after = out[0]
        self.items.append((block, kind))
        self.modes.append(mode)
        if mode == 0:
            self.state.append(trade(out[0]))
        elif mode < 3:
            self.state.append(((out[0],), (cross(out[1], mode),)))
        else:
            keep_x, send_x, keep_y, send_y = out
            self.state.append(((keep_x, keep_y), (cross(send_x, 1), cross(send_y, 2))))

    def first(self, i):
        mode = self.modes[i]
        if mode == 0:
            keep, send = folded(self.state[i], self.after)
            self.after = keep
            self.state[i] = (keep,), (cross(send, 1),)
            return
        out = plus(*self.state[i], self.after)
        self.after = out[0]
        if mode < 3:
            self.state[i] = (out[0],), (cross(out[1], 3 - mode),)
        else:
            xk, xs, yk, ys = out
            self.state[i] = (xk, yk), (cross(xs, 2), cross(ys, 1))

    def send(self, i):
        (f,) = self.hold(self.state[i])
        self.state[i] = (trade(f),)

    def second(self, i, send=True):
        if self.modes[i] == 0:
            keep, send = plus(*self.state[i], self.after)
            self.after = keep
            self.state[i] = keep, cross(send, 2)
            return
        f = merged(*self.state[i], self.after)
        self.after = f
        self.state[i] = (trade(f),) if send else f

    def third(self, i):
        v = summed(self.state[i], self.after)
        bit = 4
        while bit < lax.axis_size(R):
            v = summed((v, cross(v, bit)), v)
            bit *= 2
        self.after = v
        self.own[self.items[i]] = v

    def unite(self, block, kinds):
        own = joined([self.own[block, kind] for kind in kinds], self.after)
        self.after = own
        self.ready[block, kinds] = own, to_core(own, block)

    def spread(self, block, kinds):
        p0 = paired(*self.ready[block, kinds], self.after)
        self.after = p0
        self.ready[block, kinds] = p0, on_core(p0, 1, block), on_core(p0, 2, block)

    def spread_on(self, block, kinds):
        p0, p1, p2 = self.ready[block, kinds]
        p1, p2 = fence((p1, p2), self.after)
        self.after = p1
        n = len(kinds)
        flat1, flat2 = p1.reshape(2 * n, PIECE, D), p2.reshape(2 * n, PIECE, D)
        pa, pb = on_core(flat2[:n], 1, block), on_core(flat1[n:], 2, block)
        self.ready[block, kinds] = p0, p1, p2, pa, pb

    def finish(self, block, kinds):
        before = []
        for kind in kinds:
            before += self.results.get(kind, [])
        out = list(finish(block, kinds, self.ready[block, kinds], before, self.after))
        self.after = out[-1]
        for kind in kinds:
            n = 2 if kind == 0 else 1
            self.results[kind], out = out[:n], out[n:]

    def hold(self, *values):
        values = fence(values, self.after)
        self.after = values[0]
        return values


def standard(v):
    mean = jnp.mean(v, axis=-1, keepdims=True)
    centred = v - mean
    rstd = lax.rsqrt(jnp.mean(centred * centred, axis=-1, keepdims=True) + 1e-06)
    return centred * rstd, rstd


def mm(a, b):
    return jnp.dot(a, b, preferred_element_type=F32)


def mmt(a, b):
    return lax.dot_general(a, b, (((1,), (1,)), ((), ())), preferred_element_type=F32)


def head_cols(h, base=0):
    return slice(base + h * HEAD_DIM, base + (h + 1) * HEAD_DIM)


def softmax_of(q, k):
    scores = mmt(q, k)
    e = jnp.exp(scores - jnp.max(scores, axis=-1, keepdims=True))
    return e / jnp.sum(e, axis=-1, keepdims=True)


def shape_of(dtype, *dims):
    return jax.ShapeDtypeStruct(dims, dtype)


def row(ref, i):
    return ref[i : i + 1, :]


def attend_kernel(block, *refs):
    x, ada, qv_bias, proj_bias = refs[:4]
    own, far, mine, other = refs[4:6], refs[6:8], refs[8:10], refs[10:12]
    w_out, sides, q, k, v, attended, mid, mlp_in, w, sems = refs[13:]
    attn_in, mixed = sides.at[0], sides.at[1]
    wait = weight_copies(block, 0, 0, mine, other, own, far, w, sems)
    xf = x[...].astype(F32)
    n1, _ = standard(xf)
    attn_in[...] = (n1 * (1.0 + row(ada, 1)) + row(ada, 0)).astype(BF)
    wait()
    keep = pltpu.make_async_copy(w, w_out, sems.at[26])
    keep.start()
    q[...] = ((mm(attn_in[...], w[:, :D]) + qv_bias[:, :D]) * HEAD_DIM**-0.5).astype(BF)
    k[...] = mm(attn_in[...], w[:, D : 2 * D]).astype(BF)
    v[...] = (mm(attn_in[...], w[:, 2 * D : 3 * D]) + qv_bias[:, D:]).astype(BF)
    for h in range(HEADS):
        cols = head_cols(h)
        probs = softmax_of(q[:, cols], k[:, cols]).astype(BF)
        mixed[:, cols] = mm(probs, v[:, cols]).astype(BF)
    attended[...] = mm(mixed[...], w[:, 3 * D :]) + proj_bias[...]
    mid[...] = x[...].astype(F32) + row(ada, 2) * attended[...]
    n2, _ = standard(mid[...])
    mlp_in[...] = (n2 * (1.0 + row(ada, 4)) + row(ada, 3)).astype(BF)
    keep.wait()


def attend(block, x, ada, biases, gathered):
    t = x.shape[0]
    low = shape_of(BF, t, D)
    high = shape_of(F32, t, D)
    return pl.pallas_call(
        functools.partial(attend_kernel, block),
        out_shape=(shape_of(BF, D, FF), shape_of(BF, 2, t, D), low, low, low, high, high, low),
        in_specs=[INSIDE] * 4 + [ANYWHERE] * 9,
        out_specs=(ANYWHERE,) + (INSIDE,) * 7,
        scratch_shapes=[pltpu.VMEM((D, FF), BF), pltpu.SemaphoreType.DMA((27,))],
        compiler_params=PARAMS,
        cost_estimate=cost(4 * D * FF, 2 * t * D * FF),
    )(x, ada, biases[0], biases[1], *gathered)


def mlp_kernel(block, *refs):
    mid, mlp_in, ada, up_bias, down_bias = refs[:5]
    own, far = refs[5:7], refs[7:9]
    wu_out, wd_out, hidden, act_t, branch, y, wu, wd, act, sems_u, sems_d = refs[14:]
    wait_u = weight_copies(block, 1, 0, refs[9:10], refs[10:11], own, far, wu, sems_u)
    wait_d = weight_copies(block, 2, 1, refs[11:12], refs[12:13], own, far, wd, sems_d)
    wait_u()
    keep_u = pltpu.make_async_copy(wu, wu_out, sems_u.at[26])
    keep_u.start()
    for j in range(4):
        cols = slice(j * D, (j + 1) * D)
        hid = mm(mlp_in[...], wu[:, cols]) + up_bias[:, cols]
        hidden[:, cols] = hid
        part = jax.nn.gelu(hid, approximate=True)
        act[:, cols] = part.astype(BF)
        turned = part.T.astype(BF)
        act_t[0, j] = turned[: D // 2]
        act_t[1, j] = turned[D // 2 :]
    wait_d()
    keep_d = pltpu.make_async_copy(wd, wd_out, sems_d.at[26])
    keep_d.start()
    branch[...] = mm(act[...], wd[...]) + down_bias[...]
    y[...] = (mid[...] + row(ada, 5) * branch[...]).astype(BF)
    keep_u.wait()
    keep_d.wait()


def mlp(block, mid, mlp_in, ada, biases, gathered):
    t = mid.shape[0]
    return pl.pallas_call(
        functools.partial(mlp_kernel, block),
        out_shape=(
            shape_of(BF, D, FF),
            shape_of(BF, FF, D),
            shape_of(F32, t, FF),
            shape_of(BF, 2, NZ, D // 2, t),
            shape_of(F32, t, D),
            shape_of(BF, t, D),
        ),
        in_specs=[INSIDE] * 5 + [ANYWHERE] * 9,
        out_specs=(ANYWHERE,) * 2 + (INSIDE,) * 4,
        scratch_shapes=[
            pltpu.VMEM((D, FF), BF),
            pltpu.VMEM((FF, D), BF),
            pltpu.VMEM((t, FF), BF),
            pltpu.SemaphoreType.DMA((27,)),
            pltpu.SemaphoreType.DMA((27,)),
        ],
        compiler_params=PARAMS,
        cost_estimate=cost(8 * D * FF, 4 * t * D * FF),
    )(mid, mlp_in, ada, biases[2], biases[3], *gathered)


def column_sum(v):
    return jnp.sum(v, axis=0, keepdims=True)


def norm_back(g, n, rstd):
    return rstd * (
        g - jnp.mean(g, axis=-1, keepdims=True) - n * jnp.mean(g * n, axis=-1, keepdims=True)
    )


def gelu_slope(v):
    c = math.sqrt(2.0 / math.pi)
    t = jnp.tanh(c * (v + 0.044715 * v * v * v))
    return 0.5 * (1.0 + t) + 0.5 * v * (1.0 - t * t) * (c * (1.0 + 3.0 * 0.044715 * v * v))


def mlp_back_kernel(*refs):
    grad, d_branch, ada, mid, attended, hidden, branch, wu_in, wd_in = refs[:9]
    d_hidden, d_mid, d_att, stats, wu, wd, acc, sems = refs[10:]
    copies = []
    for j in range(4):
        part = slice(j * D, (j + 1) * D)
        down = pltpu.make_async_copy(wd_in.at[part, :], wd.at[part, :], sems.at[2 * j])
        up = pltpu.make_async_copy(wu_in.at[:, part], wu.at[:, part], sems.at[2 * j + 1])
        copies.append((down, up))
    for down, up in copies:
        down.start()
        up.start()
    stats[...] = jnp.zeros_like(stats)
    stats[5:6, :] = column_sum(grad[...].astype(F32) * branch[...])
    stats[13:14, :] = column_sum(d_branch[...].astype(F32))
    for j in range(4):
        part = slice(j * D, (j + 1) * D)
        copies[j][0].wait()
        d_act = mmt(d_branch[...], wd[part, :])
        d_hid = (d_act * gelu_slope(hidden[:, part])).astype(BF)
        d_hidden[j // 2, :, (j % 2) * D : (j % 2 + 1) * D] = d_hid
        stats[9 + j : 10 + j, :] = column_sum(d_hid.astype(F32))
        copies[j][1].wait()
        product = mmt(d_hid, wu[:, part])
        if j == 0:
            acc[...] = product
        else:
            acc[...] += product
    n2, r2 = standard(mid[...])
    stats[3:4, :] = column_sum(acc[...])
    stats[4:5, :] = column_sum(acc[...] * n2)
    whole = grad[...].astype(F32) + norm_back(acc[...] * (1.0 + row(ada, 4)), n2, r2)
    d_mid[...] = whole
    d_att[...] = (row(ada, 2) * whole).astype(BF)
    stats[2:3, :] = column_sum(whole * attended[...])
    stats[8:9, :] = column_sum(d_att[...].astype(F32))


def mlp_back(grad, d_branch, ada, mid, attended, hidden, branch, wu, wd, after):
    t = grad.shape[0]
    return pl.pallas_call(
        mlp_back_kernel,
        out_shape=(
            shape_of(BF, 2, t, HALF),
            shape_of(F32, t, D),
            shape_of(BF, t, D),
            shape_of(F32, 16, D),
        ),
        in_specs=[INSIDE] * 7 + [ANYWHERE] * 3,
        out_specs=(INSIDE,) * 4,
        scratch_shapes=[
            pltpu.VMEM((D, FF), BF),
            pltpu.VMEM((FF, D), BF),
            pltpu.VMEM((t, D), F32),
            pltpu.SemaphoreType.DMA((8,)),
        ],
        compiler_params=PARAMS,
        cost_estimate=free(),
    )(grad, d_branch, ada, mid, attended, hidden, branch, wu, wd, after)


def attend_back_kernel(*refs):
    x, d_mid, d_att, ada, q_ref, k_ref, v_ref, stats, w_in = refs[:9]
    out, d_x, d_x_low, small, w, mixed, sem = refs[10:]
    copies = [
        pltpu.make_async_copy(w_in.at[:, 3 * D :], w.at[:, 3 * D :], sem.at[0]),
        pltpu.make_async_copy(w_in.at[:, : 3 * D], w.at[:, : 3 * D], sem.at[1]),
    ]
    for copy in copies:
        copy.start()
    copies[0].wait()
    mixed[...] = mmt(d_att[...], w[:, 3 * D :]).astype(BF)
    for h in range(HEADS):
        cols = head_cols(h)
        q, k, v, dm = (ref[:, cols] for ref in (q_ref, k_ref, v_ref, mixed))
        soft = softmax_of(q, k)
        d_probs = mmt(dm, v)
        inner = jnp.sum(d_probs * soft, axis=-1, keepdims=True)
        d_s = (soft * (d_probs - inner)).astype(BF)
        out[0, :, cols] = (mm(d_s, k) * HEAD_DIM**-0.5).astype(BF)
        out[0, :, head_cols(h, D)] = tdot(d_s, q).astype(BF)
        out[1, :, cols] = tdot(soft.astype(BF), dm).astype(BF)
    out[1, :, D:] = d_att[...]
    copies[1].wait()
    d_in = mmt(out[0, :, :D], w[:, :D])
    d_in += mmt(out[0, :, D:], w[:, D : 2 * D])
    d_in += mmt(out[1, :, :D], w[:, 2 * D : 3 * D])
    n1, r1 = standard(x[...].astype(F32))
    rows = [
        column_sum(d_in),
        column_sum(d_in * n1),
        stats[2:6, :],
        column_sum(out[0, :, :D].astype(F32)),
        column_sum(out[1, :, :D].astype(F32)),
        stats[8:, :],
    ]
    small[...] = jnp.concatenate(rows, axis=0).astype(BF)
    whole = d_mid[...] + norm_back(d_in * (1.0 + row(ada, 1)), n1, r1)
    d_x[...] = whole
    d_x_low[...] = whole.astype(BF)


def attend_back(x, d_mid, d_att, ada, q, k, v, stats, wa, after):
    t = x.shape[0]
    return pl.pallas_call(
        attend_back_kernel,
        out_shape=(
            shape_of(BF, 2, t, HALF),
            shape_of(F32, t, D),
            shape_of(BF, t, D),
            shape_of(BF, 16, D),
        ),
        in_specs=[INSIDE] * 8 + [ANYWHERE] * 2,
        out_specs=(INSIDE,) * 4,
        scratch_shapes=[
            pltpu.VMEM((D, FF), BF),
            pltpu.VMEM((t, D), BF),
            pltpu.SemaphoreType.DMA((2,)),
        ],
        compiler_params=PARAMS,
        cost_estimate=free(),
    )(x, d_mid, d_att, ada, q, k, v, stats, wa, after)


def far_half(halves):
    c = lax.axis_index(S)
    return swap(lax.dynamic_index_in_dim(halves, 1 - c, 0, keepdims=False))


def rows_sum(v):
    return jnp.sum(v.astype(F32), axis=0)


def embed_time(steps):
    half = D // 2
    freq = jnp.exp(-math.log(10000.0) * jnp.arange(half, dtype=F32) / half)
    angles = steps.astype(F32)[:, None] * freq[None, :]
    return jnp.concatenate([jnp.cos(angles), jnp.sin(angles)], axis=-1)


def across(value):
    out = value[None]
    bit = 1
    while bit < lax.axis_size(R):
        out = jnp.concatenate([out, cross(out, bit)])
        bit *= 2
    return out


def in_order(value):
    nr = lax.axis_size(R)
    return jnp.take(value, lax.axis_index(R) ^ jnp.arange(nr), axis=0)


def per_device(
    inputs,
    cotangent,
    timesteps,
    labels,
    class_table,
    qkv_weight,
    qv_bias,
    proj_weight,
    proj_bias,
    up_weight,
    up_bias,
    down_weight,
    down_bias,
    ada_weight,
    ada_bias,
):
    c = lax.axis_index(S)
    z = lax.axis_index(Z)
    is_first = c == 0

    ids = jnp.concatenate([timesteps, labels], axis=1)
    vectors = [v[0].astype(F32) for v in (qv_bias, proj_bias, up_bias, down_bias, ada_bias)]
    small = along_z(jnp.concatenate(vectors + [ids.reshape(-1).astype(F32)]))
    ids_z = small[:, -4:].astype(jnp.int32).reshape(NZ, 2, 2)
    vec_mine = small[:, :-4]
    vec_other = swap(vec_mine)

    def cond_of(steps, classes):
        return embed_time(steps) + jnp.take(class_table, classes, axis=0).astype(F32)

    cond_z = cond_of(ids_z[..., 0].reshape(-1), ids_z[..., 1].reshape(-1))
    silu_z = jax.nn.silu(cond_z).astype(BF)
    rows_z = lax.dynamic_slice_in_dim(silu_z, z * ROWS, ROWS, 1)
    partial = mm(rows_z, ada_weight[0]).reshape(NZ, 2, -1)
    ada_sum = jnp.sum(trade(partial), axis=0)
    lengths = (qv_bias.shape[1], proj_bias.shape[1], up_bias.shape[1], down_bias.shape[1], ada_bias.shape[1])

    def split_vectors(vec):
        out = []
        at = 0
        for n in lengths:
            out.append(vec[:, at : at + n].reshape(-1))
            at += n
        return out

    mine_split = split_vectors(vec_mine)
    other_split = split_vectors(vec_other)
    ada_sum = ada_sum + mine_split[4][None]
    ada_keep = lax.dynamic_index_in_dim(ada_sum, c, 0, keepdims=False)
    ada_got = swap(lax.dynamic_index_in_dim(ada_sum, 1 - c, 0, keepdims=False))
    adas = []
    biases = []
    for block in range(2):
        here = c == block
        adas.append(jnp.where(here, ada_keep, ada_got).reshape(6, D))
        biases.append(
            [jnp.where(here, a, b)[None] for a, b in zip(mine_split[:4], other_split[:4])]
        )

    mine = ((qkv_weight[0], proj_weight[0]), (up_weight[0],), (down_weight[0],))
    other = tuple(tuple(swap(w) for w in group) for group in mine)
    gatherer = Gatherer(mine, other, qkv_weight[0])
    x = lax.dynamic_index_in_dim(inputs, c, 0, keepdims=False)[0]
    cot = lax.dynamic_index_in_dim(cotangent, c, 0, keepdims=False)[0]
    kept = []
    kept_mlp = []

    def run_attend(block, value):
        got = attend(block, value, adas[block], biases[block], gatherer.operands(2 * block))
        gatherer.after = got[-1]
        kept.append(got)
        return swap(got[1])

    def run_mlp(block):
        mid, mlp_in = kept[block][-2:]
        got = mlp(block, mid, mlp_in, adas[block], biases[block], gatherer.operands(2 * block + 1))
        gatherer.after = got[-1]
        kept_mlp.append(got)
        return far_half(got[3]), swap(mlp_in)

    def branch_grad(block, grad):
        return (adas[block][5:] * grad.astype(F32)).astype(BF)

    for g in range(4):
        gatherer.extract(g)
    ids_all = in_order(across(ids_z)).reshape(-1, 2)
    gatherer.stack(0)
    (ids_all,) = gatherer.hold(ids_all)
    gatherer.onward(0)
    d_branch1 = branch_grad(1, cot)
    far_branch1 = swap(d_branch1)
    gatherer.share(0)
    gatherer.stack(1)
    far_sides0 = run_attend(0, x)
    gatherer.stack(2)
    far_sides0, far_branch1 = gatherer.hold(far_sides0, far_branch1)
    gatherer.onward(1)
    gatherer.share(1)
    gatherer.onward(2)
    gatherer.stack(3)
    far_mlp0 = run_mlp(0)
    y0 = kept_mlp[0][5]
    gatherer.share(2)
    far_mlp0 = gatherer.hold(*far_mlp0)
    far_sides1 = run_attend(1, y0)
    gatherer.onward(3)
    (far_sides1,) = gatherer.hold(far_sides1)
    gatherer.share(3)
    far_mlp1 = run_mlp(1)
    y1 = kept_mlp[1][5]

    reducer = Reducer(y1)

    def run_mlp_back(block, grad, d_branch):
        attended, mid, mlp_in = kept[block][-3:]
        wu, wd, hidden, act_t, branch, _ = kept_mlp[block]
        got = mlp_back(
            grad, d_branch, adas[block], mid, attended, hidden, branch, wu, wd, reducer.after
        )
        reducer.after = got[0]
        return got, far_half(got[0])

    def run_attend_back(block, value, back):
        wa, sides, q, k, v = kept[block][:5]
        _, d_mid, d_att, stats = back
        got = attend_back(
            value, d_mid, d_att, adas[block], q, k, v, stats, wa, reducer.after
        )
        reducer.after = got[2]
        return got

    def begin(block, kind, mode, *operands):
        reducer.begin(block, kind, mode, operands)

    back1, far_hidden1 = run_mlp_back(1, cot, d_branch1)
    begin(1, 2, 0, kept_mlp[1][3], far_mlp1[0], d_branch1, far_branch1)
    begin(1, 1, 3, kept[1][-1], far_mlp1[1], back1[0], far_hidden1)
    d_all1, dx1f, dx1, small1 = run_attend_back(1, y0, back1)
    far_all1 = far_half(d_all1)
    d_branch0 = branch_grad(0, dx1)
    far_branch0 = swap(d_branch0)
    reducer.first(1)
    begin(1, 0, 3, kept[1][1], far_sides1, d_all1, far_all1)
    back0, far_hidden0 = run_mlp_back(0, dx1, d_branch0)
    begin(0, 2, 3, kept_mlp[0][3], far_mlp0[0], d_branch0, far_branch0)
    reducer.first(2)
    reducer.second(1, send=False)
    begin(0, 1, 3, kept[0][-1], far_mlp0[1], back0[0], far_hidden0)
    reducer.first(0)
    reducer.send(1)
    d_all0, dx0, dx0_low, small0 = run_attend_back(0, x, back0)
    far_all0 = far_half(d_all0)
    reducer.first(3)
    reducer.third(1)
    reducer.second(2)
    begin(0, 0, 3, kept[0][1], far_sides0, d_all0, far_all0)
    small_keep = jnp.where(is_first, small0, small1)
    small_got = swap(jnp.where(is_first, small1, small0))
    reducer.first(4)
    reducer.third(2)
    reducer.second(3)
    reducer.second(0)
    (small_got,) = reducer.hold(small_got)
    small = jnp.stack(
        [jnp.where(is_first, small_keep, small_got), jnp.where(is_first, small_got, small_keep)]
    )
    block1, block0, last = (2, 1, 0), (2, 1), (0,)
    reducer.first(5)
    reducer.third(0)
    reducer.unite(1, block1)
    reducer.third(3)
    small = along_z(small)
    reducer.spread(1, block1)
    (small,) = reducer.hold(small)
    small = small[None]
    bits = [1 << i for i in range(lax.axis_size(R).bit_length() - 1)]
    hop = cross(small, 1)
    reducer.second(4)
    reducer.second(5)
    reducer.third(4)
    reducer.unite(0, block0)
    reducer.spread_on(1, block1)
    (hop,) = reducer.hold(hop)
    small = jnp.concatenate([small, hop])
    hop = cross(small, 2)
    reducer.spread(0, block0)
    reducer.third(5)
    reducer.unite(0, last)
    (hop,) = reducer.hold(hop)
    small = jnp.concatenate([small, hop])
    for bit in bits[2:]:
        small = jnp.concatenate([small, cross(small, bit)])
    reducer.spread_on(0, block0)
    reducer.spread(0, last)
    reducer.spread_on(0, last)
    reducer.finish(1, block1)
    reducer.finish(0, block0)
    reducer.finish(0, last)
    (qkv_grad, proj_grad), (up_grad,), (down_grad,) = (reducer.results[k] for k in range(3))

    def both_micros(v0, v1):
        keep = jnp.where(is_first, v0, v1)
        got = swap(jnp.where(is_first, v1, v0))
        return jnp.stack([jnp.where(is_first, keep, got), jnp.where(is_first, got, keep)])

    block_outputs = both_micros(y0, y1)[None, :, None]
    input_grads = both_micros(dx0, dx1.astype(F32))[None, :, None]

    small = in_order(small).reshape(-1, 16, D)
    sums = rows_sum(small[:, 6:14])
    dada_own = small[:, :6].reshape(-1, 6 * D)

    def own_slice(vec):
        vec = vec.reshape(-1)
        n = vec.shape[0] // NZ
        return lax.dynamic_slice_in_dim(vec, z * n, n, 0)[None]

    qv_bias_grad = own_slice(sums[:2])
    proj_bias_grad = own_slice(sums[2])
    up_bias_grad = own_slice(sums[3:7])
    down_bias_grad = own_slice(sums[7])

    cond_all = cond_of(ids_all[:, 0], ids_all[:, 1])
    labels_all = ids_all[:, 1]
    cond_rows = lax.dynamic_slice_in_dim(cond_all, z * ROWS, ROWS, 1)
    silu_rows = jax.nn.silu(cond_rows).astype(BF)
    ada_grad = lax.dot_general(
        silu_rows, dada_own, (((0,), (0,)), ((), ())), preferred_element_type=F32
    )
    ada_bias_grad = own_slice(rows_sum(dada_own))
    d_silu = mmt(dada_own, ada_weight[0])
    _, silu_back = jax.vjp(jax.nn.silu, cond_rows)
    d_cond = silu_back(d_silu)[0]
    d_cond = d_cond + swap(d_cond)
    d_cond_all = along_z(d_cond).transpose(1, 0, 2).reshape(-1, D)
    row_count = class_table.shape[0] // (2 * NZ)
    row_ids = (c * NZ + z) * row_count + jnp.arange(row_count, dtype=jnp.int32)
    owner = (row_ids[:, None] == labels_all[None, :]).astype(F32)
    table_grad = jnp.dot(owner, d_cond_all, precision=lax.Precision.HIGHEST)

    return (
        block_outputs,
        input_grads,
        table_grad,
        qkv_grad[None],
        qv_bias_grad,
        proj_grad[None],
        proj_bias_grad,
        up_grad[None],
        up_bias_grad,
        down_grad[None],
        down_bias_grad,
        ada_grad[None],
        ada_bias_grad,
    )


def solution(mesh):
    rows = P(None, (Z, R), None, None)
    matrix = P(S, Z, None)
    vector = P(S, Z)
    pair = P(None, (Z, R))
    in_specs = (rows, rows, pair, pair, P()) + (matrix, vector) * 5
    acts = P(S, None, (Z, R), None, None)
    out_specs = (acts, acts, P((S, Z), None)) + (matrix, vector) * 5
    return jax.shard_map(
        per_device, mesh=mesh, in_specs=in_specs, out_specs=out_specs, check_vma=False
    )
```

```python
import functools
import math

import jax
import jax.numpy as jnp
from jax import lax
from jax.experimental import pallas as pl
from jax.experimental.pallas import tpu as pltpu
from jax.sharding import PartitionSpec as P

S = "section"
Z = "shard"
R = "replica"
ALL = (S, Z, R)
BF = jnp.bfloat16
F32 = jnp.float32
D = 1152
HEAD_DIM = 72
HEADS = 16
FF = 4608
HALF = 2304
ROWS = 288
PIECE = 144
NZ = 4
SHARDS = (1, 2, 3)
VMEM_LIMIT = 50 * 1024 * 1024


def move(value, to):
    ns, nz, nr = (lax.axis_size(a) for a in ALL)
    pairs = []
    for s in range(ns):
        for z in range(nz):
            for r in range(nr):
                there = to(s, z, r)
                if there is not None:
                    a, b, c = there
                    pairs.append(((s * nz + z) * nr + r, (a * nz + b) * nr + c))
    return lax.ppermute(value, ALL, pairs)


def swap(value):
    return move(value, lambda s, z, r: (1 - s, z, r))


def to_core(value, core):
    return move(value, lambda s, z, r: (core, z, r) if s != core else None)


def zshift(value, by=1):
    nz = lax.axis_size(Z)
    return move(value, lambda s, z, r: (s, (z + by) % nz, r))


def trade(value):
    return lax.all_to_all(value, Z, split_axis=0, concat_axis=0, tiled=True)


def along_z(value):
    return trade(jnp.stack([value] * NZ))


def cross(value, bit):
    return move(value, lambda s, z, r: (s, z, r ^ bit))


def place():
    return lax.axis_index(S), lax.axis_index(Z), lax.rem(lax.axis_index(R), 4)


ANYWHERE = pl.BlockSpec(memory_space=pl.ANY)
INSIDE = pl.BlockSpec(memory_space=pltpu.VMEM)
PARAMS = pltpu.CompilerParams(vmem_limit_bytes=VMEM_LIMIT)
ONE = jax.ShapeDtypeStruct((PIECE, D), BF)


def cost(nbytes, flops=0):
    return pl.CostEstimate(flops=flops, bytes_accessed=nbytes, transcendentals=0)


def free():
    return pl.CostEstimate(flops=0, bytes_accessed=0, transcendentals=0)


def fence(arrays, after):
    n = len(arrays)
    return pl.pallas_call(
        lambda *refs: None,
        out_shape=tuple(jax.ShapeDtypeStruct(a.shape, a.dtype) for a in arrays),
        in_specs=[ANYWHERE] * (n + 1),
        out_specs=(ANYWHERE,) * n,
        input_output_aliases={i: i for i in range(n)},
        cost_estimate=free(),
    )(*arrays, after)


def stack_kernel(every, _, out):
    z = lax.axis_index(Z)
    for i in range(every.shape[1]):
        for k in SHARDS:
            out[i, k - 1] = every[lax.rem(z + NZ - k, NZ), i]


def stacked(every, after):
    n = every.shape[1]
    return pl.pallas_call(
        stack_kernel,
        out_shape=jax.ShapeDtypeStruct((n, 3, PIECE, D), BF),
        in_specs=[INSIDE, ANYWHERE],
        out_specs=INSIDE,
        compiler_params=PARAMS,
        cost_estimate=cost(12 * n * PIECE * D),
    )(every, after)


def collect_kernel(p0, p1, p2, _, big, to_x, to_y):
    n = p0.shape[0]
    for m, part in enumerate((p0, p1, p2)):
        big[m] = part[...]
    if n == 2:
        to_x[...] = p2[:1]
        to_y[...] = p1[1:]
    else:
        to_x[...] = p2[:, :1]
        to_y[...] = p1[:, 1:]


def collected(p0, p1, p2, after):
    n = p0.shape[0]
    if n == 2:
        cut = (1, 3), (1, 3)
    else:
        cut = (1, 1), (1, 2)
    shapes = ((3, n, 3), *cut)
    return pl.pallas_call(
        collect_kernel,
        out_shape=tuple(jax.ShapeDtypeStruct((*s, PIECE, D), BF) for s in shapes),
        in_specs=[INSIDE] * 3 + [ANYWHERE],
        out_specs=(INSIDE,) * 3,
        compiler_params=PARAMS,
        cost_estimate=cost(1),
    )(p0, p1, p2, after)


def combine_kernel(pa, pb, _, out):
    if out.shape[0] == 2:
        out[:1] = pa[...]
        out[1:] = pb[...]
    else:
        out[:, :1] = pa[...]
        out[:, 1:] = pb[...]


def combined(pa, pb, after):
    n = 2 if pa.shape[1] == 3 else 1
    return pl.pallas_call(
        combine_kernel,
        out_shape=jax.ShapeDtypeStruct((n, 3, PIECE, D), BF),
        in_specs=[INSIDE] * 2 + [ANYWHERE],
        out_specs=INSIDE,
        compiler_params=PARAMS,
        cost_estimate=cost(1),
    )(pa, pb, after)


def join_kernel(*refs):
    out = refs[-1]
    for i in range(out.shape[0]):
        out[i] = refs[i][...]


def joined(parts, after):
    n = len(parts)
    return pl.pallas_call(
        join_kernel,
        out_shape=jax.ShapeDtypeStruct((n, PIECE, D), BF),
        in_specs=[INSIDE] * n + [ANYWHERE],
        out_specs=INSIDE,
        compiler_params=PARAMS,
        cost_estimate=free(),
    )(*parts, after)


def plus_kernel(n, *refs):
    outs = refs[2 * n + 1 :]
    for i in range(n):
        for j in range(2):
            whole = refs[i][j].astype(F32) + refs[n + i][j].astype(F32)
            outs[2 * i + j][...] = whole.astype(BF)


def plus(a, b, after):
    n = len(a)
    shapes = [jax.ShapeDtypeStruct(v.shape[1:], BF) for v in a for _ in range(2)]
    return pl.pallas_call(
        functools.partial(plus_kernel, n),
        out_shape=tuple(shapes),
        in_specs=[INSIDE] * (2 * n) + [ANYWHERE],
        out_specs=(INSIDE,) * (2 * n),
        compiler_params=PARAMS,
        cost_estimate=free(),
    )(*a, *b, after)


def merge_kernel(n, *refs):
    out = refs[-1]
    for i in range(n):
        whole = refs[i][...].astype(F32) + refs[n + i][...].astype(F32)
        rows = refs[i].shape[0]
        out[i * rows : (i + 1) * rows] = whole.astype(BF)


def merged(a, b, after):
    n = len(a)
    return pl.pallas_call(
        functools.partial(merge_kernel, n),
        out_shape=jax.ShapeDtypeStruct((NZ, PIECE, D), BF),
        in_specs=[INSIDE] * (2 * n) + [ANYWHERE],
        out_specs=INSIDE,
        compiler_params=PARAMS,
        cost_estimate=free(),
    )(*a, *b, after)


def sum_kernel(n, *refs):
    if n == 1:
        parts = [refs[0][i] for i in range(refs[0].shape[0])]
    else:
        parts = [ref[...] for ref in refs[:n]]
    whole = parts[0].astype(F32)
    for part in parts[1:]:
        whole = whole + part.astype(F32)
    refs[-1][...] = whole.astype(BF)


def summed(parts, after):
    n = len(parts)
    return pl.pallas_call(
        functools.partial(sum_kernel, n),
        out_shape=ONE,
        in_specs=[INSIDE] * n + [ANYWHERE],
        out_specs=INSIDE,
        compiler_params=PARAMS,
        cost_estimate=free(),
    )(*parts, after)


def fold_kernel(parts, _, keep, send):
    for m in range(4):
        whole = parts[0, m].astype(F32)
        for i in SHARDS:
            whole = whole + parts[i, m].astype(F32)
        (send if m % 2 else keep)[m // 2] = whole.astype(BF)


def folded(parts, after):
    half = jax.ShapeDtypeStruct((2, PIECE, D), BF)
    return pl.pallas_call(
        fold_kernel,
        out_shape=(half, half),
        in_specs=[INSIDE, ANYWHERE],
        out_specs=(INSIDE, INSIDE),
        compiler_params=PARAMS,
        cost_estimate=free(),
    )(parts, after)


def pair_kernel(own, far, _, out):
    c = lax.axis_index(S)
    for core in range(2):

        @pl.when(c == core)
        def _():
            for i in range(own.shape[0]):
                out[i, core] = own[i]
                out[i, 1 - core] = far[i]


def paired(own, far, after):
    return pl.pallas_call(
        pair_kernel,
        out_shape=jax.ShapeDtypeStruct((own.shape[0], 2, PIECE, D), BF),
        in_specs=[INSIDE] * 2 + [ANYWHERE],
        out_specs=INSIDE,
        compiler_params=PARAMS,
        cost_estimate=free(),
    )(own, far, after)


def chosen(block, mine, other, act):
    c = lax.axis_index(S)

    @pl.when(c == block)
    def _():
        act(mine)

    @pl.when(c != block)
    def _():
        act(other)


def arrays_of(kind):
    return 2 if kind == 0 else 1


def extract_kernel(items, *refs):
    out, sems = refs[-2:]
    c, z, r = place()
    unit = c * 2 + r // 2
    at = 0
    for i, (block, kind) in enumerate(items):
        n = arrays_of(kind)
        mine, other = refs[at : at + n], refs[at + n : at + 2 * n]
        at += 2 * n

        def copy(source):
            pltpu.make_async_copy(source, out.at[i], sems.at[i]).start()

        def act(source):
            if kind == 2:
                copy(source[0].at[pl.ds((c * 4 + r) * PIECE, PIECE), :])
                return
            height = pl.ds(lax.rem(r, 2) * PIECE, PIECE)

            def take(ref, index):
                cols = pl.ds(pl.multiple_of(index * D, D), D)
                copy(ref.at[height, cols])

            if kind == 1:
                take(source[0], unit)
                return

            @pl.when(unit == 3)
            def _():
                take(source[1], 0)

            @pl.when(unit != 3)
            def _():
                take(source[0], unit)

        chosen(block, mine, other, act)
    for i in range(len(items)):
        pltpu.make_async_copy(out.at[i], out.at[i], sems.at[i]).wait()


def extract(items, mine, other, after):
    n = len(items)
    operands = []
    for _, kind in items:
        operands += [*mine[kind], *other[kind]]
    return pl.pallas_call(
        functools.partial(extract_kernel, items),
        out_shape=jax.ShapeDtypeStruct((n, PIECE, D), BF),
        in_specs=[ANYWHERE] * (len(operands) + 1),
        out_specs=INSIDE,
        scratch_shapes=[pltpu.SemaphoreType.DMA((n,))],
        compiler_params=PARAMS,
        cost_estimate=cost(4 * n * PIECE * D),
    )(*operands, after)


def weight_copies(block, kind, index, mine, other, own, far, out, sems):
    n = arrays_of(kind)
    c, z, r = place()
    copies = []
    height = D if kind == 2 else ROWS
    rows = pl.ds(z * height, height)
    if kind == 0:
        targets = (out.at[rows, pl.ds(0, 3 * D)], out.at[rows, pl.ds(3 * D, D)])
    else:
        targets = (out.at[rows, :],)

    def act(source):
        for i in range(n):
            pltpu.make_async_copy(source[i], targets[i], sems.at[i]).start()

    chosen(block, mine, other, act)
    for side, group in ((0, own), (1, far)):
        core = c if side == 0 else 1 - c
        for m in range(4):
            low = lax.rem(r + m, 2)
            high = lax.rem(r // 2 + m // 2, 2)
            for k in SHARDS:
                zp = lax.rem(z + NZ - k, NZ)
                if kind == 2:
                    row = zp * D + core * (D // 2) + (high * 2 + low) * PIECE
                    spot = out.at[pl.ds(row, PIECE), :]
                else:
                    row = zp * ROWS + low * PIECE
                    col = pl.multiple_of((core * 2 + high) * D, D)
                    spot = out.at[pl.ds(row, PIECE), pl.ds(col, D)]
                if m < 3:
                    piece = group[0].at[m, index, k - 1]
                else:
                    piece = group[1].at[index, k - 1]
                sem = sems.at[2 + (side * 4 + m) * 3 + k - 1]
                copies.append(pltpu.make_async_copy(piece, spot, sem))
    for copy in copies:
        copy.start()

    def wait():
        for i in range(n):
            pltpu.make_async_copy(mine[i], targets[i], sems.at[i]).wait()
        for copy in copies:
            copy.wait()

    return wait


GROUPS = (((0, 0),), ((0, 1), (0, 2)), ((1, 0),), ((1, 1), (1, 2)))


class Gatherer:
    def __init__(self, mine, other, after):
        self.mine = mine
        self.other = other
        self.after = after
        self.state = {}

    def extract(self, g):
        self.after = extract(GROUPS[g], self.mine, self.other, self.after)
        self.state[g] = lax.all_gather(self.after, Z, axis=0, tiled=False)

    def stack(self, g):
        p0 = stacked(self.state[g], self.after)
        self.after = p0
        self.state[g] = p0, cross(p0, 1), cross(p0, 2)

    def onward(self, g):
        big, to_x, to_y = collected(*self.state[g], self.after)
        self.after = to_x
        self.state[g] = big, (cross(to_x, 1), cross(to_y, 2)), swap(big)

    def share(self, g):
        big, p3, far = self.state[g]
        p3 = combined(*p3, self.after)
        self.after = p3
        self.state[g] = (big, p3), (far, swap(p3))

    def hold(self, *values):
        values = fence(values, self.after)
        self.after = values[0]
        return values

    def operands(self, g):
        own, far = self.state[g]
        shards = []
        for _, kind in GROUPS[g]:
            shards += [*self.mine[kind], *self.other[kind]]
        return (*own, *far, *shards, self.after)


def tdot(a, b):
    return lax.dot_general(a, b, (((0,), (0,)), ((), ())), preferred_element_type=F32)


def wgrad_kernel(kind, mode, *refs):
    n = 4
    ins = refs[:n]
    outs = refs[n + 1 : -1]
    acc = refs[-1]
    c, z, r = place()
    for g in range(2):
        u = lax.rem(g + r // 2, 2)
        if kind == 2:
            lo, lx, ro, rx = ins
            for zp in range(NZ):
                rows = pl.ds(pl.multiple_of(u * ROWS, ROWS), ROWS)
                acc[zp * ROWS : (zp + 1) * ROWS, :] = jnp.dot(
                    lo[c, zp, rows, :], ro[...], preferred_element_type=F32
                ) + jnp.dot(lx[zp, rows, :], rx[...], preferred_element_type=F32)
        else:
            ro, rx = ins[-2:]
            cols = pl.ds(pl.multiple_of(u * D, D), D)

            def product(lo, lx):
                acc[...] = tdot(lo[...], ro[c, :, cols]) + tdot(lx[...], rx[:, cols])

            if kind == 1:
                product(ins[0], ins[1])
            else:

                @pl.when(c * u == 0)
                def _():
                    product(ins[0].at[0], ins[1].at[0])

                @pl.when(c * u == 1)
                def _():
                    product(ins[0].at[1], ins[1].at[1])

        for par in range(2):

            @pl.when(lax.rem(r, 2) == par)
            def _():
                for zp in range(NZ):
                    for h in range(2):
                        start = (zp * 2 + h) * PIECE
                        piece = acc[start : start + PIECE, :].astype(BF)
                        low = h ^ par
                        if mode == 0:
                            outs[0][zp, g * 2 + low] = piece
                        elif mode == 1:
                            outs[low][g, zp] = piece
                        elif mode == 2:
                            outs[g][low, zp] = piece
                        elif zp < 2:
                            outs[low][g, zp] = piece
                        else:
                            outs[2 + g][low, zp - 2] = piece


def wgrad(kind, mode, operands, after):
    leading = ((4, 4), (2, 4), (2, 4), (2, 2))[mode]
    count = (1, 2, 2, 4)[mode]
    part = jax.ShapeDtypeStruct((*leading, PIECE, D), BF)
    return pl.pallas_call(
        functools.partial(wgrad_kernel, kind, mode),
        out_shape=(part,) * count,
        in_specs=[INSIDE] * len(operands) + [ANYWHERE],
        out_specs=(INSIDE,) * count,
        scratch_shapes=[pltpu.VMEM((D, D), F32)],
        compiler_params=PARAMS,
        cost_estimate=free(),
    )(*operands, after)


def finish_kernel(block, kinds, *refs):
    count = len(kinds)
    outs = list(refs[-4 - count - (0 in kinds) : -4])
    raw, acc, sems_in, sems_out = refs[-4:]
    p0, p1, p2, pa, pb = refs[:5]
    c, z, r = place()

    @pl.when(c == block)
    def _():
        copies = []
        for i in range(count):
            for core in range(2):
                flat = i * 2 + core
                last = pa.at[flat] if flat < count else pb.at[flat - count]
                sources = (p0.at[i, core], p1.at[i, core], p2.at[i, core], last)
                for m, piece in enumerate(sources):
                    n = flat * 4 + m
                    copies.append(pltpu.make_async_copy(piece, raw.at[n], sems_in.at[n]))
                    copies[-1].start()
        done = []
        at_out = 0
        for i, kind in enumerate(kinds):
            base = i * 4 * ROWS
            for core in range(2):
                for m in range(4):
                    n = (i * 2 + core) * 4 + m
                    copies[n].wait()
                    low = lax.rem(r + m, 2)
                    unit = core * 2 + lax.rem(r // 2 + m // 2, 2)
                    at = pl.multiple_of(base + unit * ROWS + low * PIECE, PIECE)
                    acc[pl.ds(at, PIECE), :] = raw[n].astype(F32)
            if kind == 2:
                moves = [(acc.at[base : base + D, :], outs[at_out])]
            else:
                moves = []
                for unit in range(4):
                    source = acc.at[base + unit * ROWS : base + (unit + 1) * ROWS, :]
                    if kind == 0 and unit == 3:
                        moves.append((source, outs[at_out + 1]))
                    else:
                        cols = outs[at_out].at[:, unit * D : (unit + 1) * D]
                        moves.append((source, cols))
            at_out += 2 if kind == 0 else 1
            for source, target in moves:
                done.append(pltpu.make_async_copy(source, target, sems_out.at[len(done)]))
                done[-1].start()
        for copy in done:
            copy.wait()


def finish(block, kinds, pieces, before, after):
    shapes = []
    for kind in kinds:
        shapes += [[(ROWS, 3 * D), (ROWS, D)], [(ROWS, FF)], [(D, D)]][kind]
    count = len(kinds)
    return pl.pallas_call(
        functools.partial(finish_kernel, block, kinds),
        out_shape=tuple(pltpu.HBM(s, F32) for s in shapes),
        in_specs=[ANYWHERE] * (6 + len(before)),
        out_specs=(ANYWHERE,) * len(shapes),
        scratch_shapes=[
            pltpu.VMEM((8 * count, PIECE, D), BF),
            pltpu.VMEM((4 * count * ROWS, D), F32),
            pltpu.SemaphoreType.DMA((8 * count,)),
            pltpu.SemaphoreType.DMA((12,)),
        ],
        input_output_aliases={6 + i: i for i in range(len(before))},
        compiler_params=PARAMS,
        cost_estimate=free(),
    )(*pieces, after, *before)


def on_core(value, bit, core):
    return move(value, lambda s, z, r: (s, z, r ^ bit) if s == core else None)


class Reducer:
    def __init__(self, after):
        self.after = after
        self.items = []
        self.modes = []
        self.state = []
        self.own = {}
        self.ready = {}
        self.results = {}

    def begin(self, block, kind, mode, operands):
        out = wgrad(kind, mode, operands, self.after)
        self.after = out[0]
        self.items.append((block, kind))
        self.modes.append(mode)
        if mode == 0:
            self.state.append(trade(out[0]))
        elif mode < 3:
            self.state.append(((out[0],), (cross(out[1], mode),)))
        else:
            keep_x, send_x, keep_y, send_y = out
            self.state.append(((keep_x, keep_y), (cross(send_x, 1), cross(send_y, 2))))

    def first(self, i):
        mode = self.modes[i]
        if mode == 0:
            keep, send = folded(self.state[i], self.after)
            self.after = keep
            self.state[i] = (keep,), (cross(send, 1),)
            return
        out = plus(*self.state[i], self.after)
        self.after = out[0]
        if mode < 3:
            self.state[i] = (out[0],), (cross(out[1], 3 - mode),)
        else:
            xk, xs, yk, ys = out
            self.state[i] = (xk, yk), (cross(xs, 2), cross(ys, 1))

    def send(self, i):
        (f,) = self.hold(self.state[i])
        self.state[i] = (trade(f),)

    def second(self, i, send=True):
        if self.modes[i] == 0:
            keep, send = plus(*self.state[i], self.after)
            self.after = keep
            self.state[i] = keep, cross(send, 2)
            return
        f = merged(*self.state[i], self.after)
        self.after = f
        self.state[i] = (trade(f),) if send else f

    def third(self, i):
        v = summed(self.state[i], self.after)
        bit = 4
        while bit < lax.axis_size(R):
            v = summed((v, cross(v, bit)), v)
            bit *= 2
        self.after = v
        self.own[self.items[i]] = v

    def unite(self, block, kinds):
        own = joined([self.own[block, kind] for kind in kinds], self.after)
        self.after = own
        self.ready[block, kinds] = own, to_core(own, block)

    def spread(self, block, kinds):
        p0 = paired(*self.ready[block, kinds], self.after)
        self.after = p0
        self.ready[block, kinds] = p0, on_core(p0, 1, block), on_core(p0, 2, block)

    def spread_on(self, block, kinds):
        p0, p1, p2 = self.ready[block, kinds]
        p1, p2 = fence((p1, p2), self.after)
        self.after = p1
        n = len(kinds)
        flat1, flat2 = p1.reshape(2 * n, PIECE, D), p2.reshape(2 * n, PIECE, D)
        pa, pb = on_core(flat2[:n], 1, block), on_core(flat1[n:], 2, block)
        self.ready[block, kinds] = p0, p1, p2, pa, pb

    def finish(self, block, kinds):
        before = []
        for kind in kinds:
            before += self.results.get(kind, [])
        out = list(finish(block, kinds, self.ready[block, kinds], before, self.after))
        self.after = out[-1]
        for kind in kinds:
            n = 2 if kind == 0 else 1
            self.results[kind], out = out[:n], out[n:]

    def hold(self, *values):
        values = fence(values, self.after)
        self.after = values[0]
        return values


def standard(v):
    mean = jnp.mean(v, axis=-1, keepdims=True)
    centred = v - mean
    rstd = lax.rsqrt(jnp.mean(centred * centred, axis=-1, keepdims=True) + 1e-06)
    return centred * rstd, rstd


def mm(a, b):
    return jnp.dot(a, b, preferred_element_type=F32)


def mmt(a, b):
    return lax.dot_general(a, b, (((1,), (1,)), ((), ())), preferred_element_type=F32)


def head_cols(h, base=0):
    return slice(base + h * HEAD_DIM, base + (h + 1) * HEAD_DIM)


def softmax_of(q, k):
    scores = mmt(q, k)
    e = jnp.exp(scores - jnp.max(scores, axis=-1, keepdims=True))
    return e / jnp.sum(e, axis=-1, keepdims=True)


def shape_of(dtype, *dims):
    return jax.ShapeDtypeStruct(dims, dtype)


def row(ref, i):
    return ref[i : i + 1, :]


def attend_kernel(block, *refs):
    x, ada, qv_bias, proj_bias = refs[:4]
    own, far, mine, other = refs[4:6], refs[6:8], refs[8:10], refs[10:12]
    w_out, sides, q, k, v, attended, mid, mlp_in, w, sems = refs[13:]
    attn_in, mixed = sides.at[0], sides.at[1]
    wait = weight_copies(block, 0, 0, mine, other, own, far, w, sems)
    xf = x[...].astype(F32)
    n1, _ = standard(xf)
    attn_in[...] = (n1 * (1.0 + row(ada, 1)) + row(ada, 0)).astype(BF)
    wait()
    keep = pltpu.make_async_copy(w, w_out, sems.at[26])
    keep.start()
    q[...] = ((mm(attn_in[...], w[:, :D]) + qv_bias[:, :D]) * HEAD_DIM**-0.5).astype(BF)
    k[...] = mm(attn_in[...], w[:, D : 2 * D]).astype(BF)
    v[...] = (mm(attn_in[...], w[:, 2 * D : 3 * D]) + qv_bias[:, D:]).astype(BF)
    for h in range(HEADS):
        cols = head_cols(h)
        probs = softmax_of(q[:, cols], k[:, cols]).astype(BF)
        mixed[:, cols] = mm(probs, v[:, cols]).astype(BF)
    attended[...] = mm(mixed[...], w[:, 3 * D :]) + proj_bias[...]
    mid[...] = x[...].astype(F32) + row(ada, 2) * attended[...]
    n2, _ = standard(mid[...])
    mlp_in[...] = (n2 * (1.0 + row(ada, 4)) + row(ada, 3)).astype(BF)
    keep.wait()


def attend(block, x, ada, biases, gathered):
    t = x.shape[0]
    low = shape_of(BF, t, D)
    high = shape_of(F32, t, D)
    return pl.pallas_call(
        functools.partial(attend_kernel, block),
        out_shape=(shape_of(BF, D, FF), shape_of(BF, 2, t, D), low, low, low, high, high, low),
        in_specs=[INSIDE] * 4 + [ANYWHERE] * 9,
        out_specs=(ANYWHERE,) + (INSIDE,) * 7,
        scratch_shapes=[pltpu.VMEM((D, FF), BF), pltpu.SemaphoreType.DMA((27,))],
        compiler_params=PARAMS,
        cost_estimate=cost(4 * D * FF, 2 * t * D * FF),
    )(x, ada, biases[0], biases[1], *gathered)


def mlp_kernel(block, *refs):
    mid, mlp_in, ada, up_bias, down_bias = refs[:5]
    own, far = refs[5:7], refs[7:9]
    wu_out, wd_out, hidden, act_t, branch, y, wu, wd, act, sems_u, sems_d = refs[14:]
    wait_u = weight_copies(block, 1, 0, refs[9:10], refs[10:11], own, far, wu, sems_u)
    wait_d = weight_copies(block, 2, 1, refs[11:12], refs[12:13], own, far, wd, sems_d)
    wait_u()
    keep_u = pltpu.make_async_copy(wu, wu_out, sems_u.at[26])
    keep_u.start()
    for j in range(4):
        cols = slice(j * D, (j + 1) * D)
        hid = mm(mlp_in[...], wu[:, cols]) + up_bias[:, cols]
        hidden[:, cols] = hid
        part = jax.nn.gelu(hid, approximate=True)
        act[:, cols] = part.astype(BF)
        turned = part.T.astype(BF)
        act_t[0, j] = turned[: D // 2]
        act_t[1, j] = turned[D // 2 :]
    wait_d()
    keep_d = pltpu.make_async_copy(wd, wd_out, sems_d.at[26])
    keep_d.start()
    branch[...] = mm(act[...], wd[...]) + down_bias[...]
    y[...] = (mid[...] + row(ada, 5) * branch[...]).astype(BF)
    keep_u.wait()
    keep_d.wait()


def mlp(block, mid, mlp_in, ada, biases, gathered):
    t = mid.shape[0]
    return pl.pallas_call(
        functools.partial(mlp_kernel, block),
        out_shape=(
            shape_of(BF, D, FF),
            shape_of(BF, FF, D),
            shape_of(F32, t, FF),
            shape_of(BF, 2, NZ, D // 2, t),
            shape_of(F32, t, D),
            shape_of(BF, t, D),
        ),
        in_specs=[INSIDE] * 5 + [ANYWHERE] * 9,
        out_specs=(ANYWHERE,) * 2 + (INSIDE,) * 4,
        scratch_shapes=[
            pltpu.VMEM((D, FF), BF),
            pltpu.VMEM((FF, D), BF),
            pltpu.VMEM((t, FF), BF),
            pltpu.SemaphoreType.DMA((27,)),
            pltpu.SemaphoreType.DMA((27,)),
        ],
        compiler_params=PARAMS,
        cost_estimate=cost(8 * D * FF, 4 * t * D * FF),
    )(mid, mlp_in, ada, biases[2], biases[3], *gathered)


def column_sum(v):
    return jnp.sum(v, axis=0, keepdims=True)


def norm_back(g, n, rstd):
    return rstd * (
        g - jnp.mean(g, axis=-1, keepdims=True) - n * jnp.mean(g * n, axis=-1, keepdims=True)
    )


def gelu_slope(v):
    c = math.sqrt(2.0 / math.pi)
    t = jnp.tanh(c * (v + 0.044715 * v * v * v))
    return 0.5 * (1.0 + t) + 0.5 * v * (1.0 - t * t) * (c * (1.0 + 3.0 * 0.044715 * v * v))


def mlp_back_kernel(*refs):
    grad, d_branch, ada, mid, attended, hidden, branch, wu_in, wd_in = refs[:9]
    d_hidden, d_mid, d_att, stats, wu, wd, acc, sems = refs[10:]
    copies = []
    for j in range(4):
        part = slice(j * D, (j + 1) * D)
        down = pltpu.make_async_copy(wd_in.at[part, :], wd.at[part, :], sems.at[2 * j])
        up = pltpu.make_async_copy(wu_in.at[:, part], wu.at[:, part], sems.at[2 * j + 1])
        copies.append((down, up))
    for down, up in copies:
        down.start()
        up.start()
    stats[...] = jnp.zeros_like(stats)
    stats[5:6, :] = column_sum(grad[...].astype(F32) * branch[...])
    stats[13:14, :] = column_sum(d_branch[...].astype(F32))
    for j in range(4):
        part = slice(j * D, (j + 1) * D)
        copies[j][0].wait()
        d_act = mmt(d_branch[...], wd[part, :])
        d_hid = (d_act * gelu_slope(hidden[:, part])).astype(BF)
        d_hidden[j // 2, :, (j % 2) * D : (j % 2 + 1) * D] = d_hid
        stats[9 + j : 10 + j, :] = column_sum(d_hid.astype(F32))
        copies[j][1].wait()
        product = mmt(d_hid, wu[:, part])
        if j == 0:
            acc[...] = product
        else:
            acc[...] += product
    n2, r2 = standard(mid[...])
    stats[3:4, :] = column_sum(acc[...])
    stats[4:5, :] = column_sum(acc[...] * n2)
    whole = grad[...].astype(F32) + norm_back(acc[...] * (1.0 + row(ada, 4)), n2, r2)
    d_mid[...] = whole
    d_att[...] = (row(ada, 2) * whole).astype(BF)
    stats[2:3, :] = column_sum(whole * attended[...])
    stats[8:9, :] = column_sum(d_att[...].astype(F32))


def mlp_back(grad, d_branch, ada, mid, attended, hidden, branch, wu, wd, after):
    t = grad.shape[0]
    return pl.pallas_call(
        mlp_back_kernel,
        out_shape=(
            shape_of(BF, 2, t, HALF),
            shape_of(F32, t, D),
            shape_of(BF, t, D),
            shape_of(F32, 16, D),
        ),
        in_specs=[INSIDE] * 7 + [ANYWHERE] * 3,
        out_specs=(INSIDE,) * 4,
        scratch_shapes=[
            pltpu.VMEM((D, FF), BF),
            pltpu.VMEM((FF, D), BF),
            pltpu.VMEM((t, D), F32),
            pltpu.SemaphoreType.DMA((8,)),
        ],
        compiler_params=PARAMS,
        cost_estimate=free(),
    )(grad, d_branch, ada, mid, attended, hidden, branch, wu, wd, after)


def attend_back_kernel(*refs):
    x, d_mid, d_att, ada, q_ref, k_ref, v_ref, stats, w_in = refs[:9]
    out, d_x, d_x_low, small, w, mixed, sem = refs[10:]
    copies = [
        pltpu.make_async_copy(w_in.at[:, 3 * D :], w.at[:, 3 * D :], sem.at[0]),
        pltpu.make_async_copy(w_in.at[:, : 3 * D], w.at[:, : 3 * D], sem.at[1]),
    ]
    for copy in copies:
        copy.start()
    copies[0].wait()
    mixed[...] = mmt(d_att[...], w[:, 3 * D :]).astype(BF)
    for h in range(HEADS):
        cols = head_cols(h)
        q, k, v, dm = (ref[:, cols] for ref in (q_ref, k_ref, v_ref, mixed))
        soft = softmax_of(q, k)
        d_probs = mmt(dm, v)
        inner = jnp.sum(d_probs * soft, axis=-1, keepdims=True)
        d_s = (soft * (d_probs - inner)).astype(BF)
        out[0, :, cols] = (mm(d_s, k) * HEAD_DIM**-0.5).astype(BF)
        out[0, :, head_cols(h, D)] = tdot(d_s, q).astype(BF)
        out[1, :, cols] = tdot(soft.astype(BF), dm).astype(BF)
    out[1, :, D:] = d_att[...]
    copies[1].wait()
    d_in = mmt(out[0, :, :D], w[:, :D])
    d_in += mmt(out[0, :, D:], w[:, D : 2 * D])
    d_in += mmt(out[1, :, :D], w[:, 2 * D : 3 * D])
    n1, r1 = standard(x[...].astype(F32))
    rows = [
        column_sum(d_in),
        column_sum(d_in * n1),
        stats[2:6, :],
        column_sum(out[0, :, :D].astype(F32)),
        column_sum(out[1, :, :D].astype(F32)),
        stats[8:, :],
    ]
    small[...] = jnp.concatenate(rows, axis=0).astype(BF)
    whole = d_mid[...] + norm_back(d_in * (1.0 + row(ada, 1)), n1, r1)
    d_x[...] = whole
    d_x_low[...] = whole.astype(BF)


def attend_back(x, d_mid, d_att, ada, q, k, v, stats, wa, after):
    t = x.shape[0]
    return pl.pallas_call(
        attend_back_kernel,
        out_shape=(
            shape_of(BF, 2, t, HALF),
            shape_of(F32, t, D),
            shape_of(BF, t, D),
            shape_of(BF, 16, D),
        ),
        in_specs=[INSIDE] * 8 + [ANYWHERE] * 2,
        out_specs=(INSIDE,) * 4,
        scratch_shapes=[
            pltpu.VMEM((D, FF), BF),
            pltpu.VMEM((t, D), BF),
            pltpu.SemaphoreType.DMA((2,)),
        ],
        compiler_params=PARAMS,
        cost_estimate=free(),
    )(x, d_mid, d_att, ada, q, k, v, stats, wa, after)


def far_half(halves):
    c = lax.axis_index(S)
    return swap(lax.dynamic_index_in_dim(halves, 1 - c, 0, keepdims=False))


def rows_sum(v):
    return jnp.sum(v.astype(F32), axis=0)


def embed_time(steps):
    half = D // 2
    freq = jnp.exp(-math.log(10000.0) * jnp.arange(half, dtype=F32) / half)
    angles = steps.astype(F32)[:, None] * freq[None, :]
    return jnp.concatenate([jnp.cos(angles), jnp.sin(angles)], axis=-1)


def across(value):
    out = value[None]
    bit = 1
    while bit < lax.axis_size(R):
        out = jnp.concatenate([out, cross(out, bit)])
        bit *= 2
    return out


def in_order(value):
    nr = lax.axis_size(R)
    return jnp.take(value, lax.axis_index(R) ^ jnp.arange(nr), axis=0)


def per_device(
    inputs,
    cotangent,
    timesteps,
    labels,
    class_table,
    qkv_weight,
    qv_bias,
    proj_weight,
    proj_bias,
    up_weight,
    up_bias,
    down_weight,
    down_bias,
    ada_weight,
    ada_bias,
):
    c = lax.axis_index(S)
    z = lax.axis_index(Z)
    is_first = c == 0

    ids = jnp.concatenate([timesteps, labels], axis=1)
    vectors = [v[0].astype(F32) for v in (qv_bias, proj_bias, up_bias, down_bias, ada_bias)]
    small = along_z(jnp.concatenate(vectors + [ids.reshape(-1).astype(F32)]))
    ids_z = small[:, -4:].astype(jnp.int32).reshape(NZ, 2, 2)
    vec_mine = small[:, :-4]
    vec_other = swap(vec_mine)

    def cond_of(steps, classes):
        return embed_time(steps) + jnp.take(class_table, classes, axis=0).astype(F32)

    cond_z = cond_of(ids_z[..., 0].reshape(-1), ids_z[..., 1].reshape(-1))
    silu_z = jax.nn.silu(cond_z).astype(BF)
    rows_z = lax.dynamic_slice_in_dim(silu_z, z * ROWS, ROWS, 1)
    partial = mm(rows_z, ada_weight[0]).reshape(NZ, 2, -1)
    ada_sum = jnp.sum(trade(partial), axis=0)
    lengths = (qv_bias.shape[1], proj_bias.shape[1], up_bias.shape[1], down_bias.shape[1], ada_bias.shape[1])

    def split_vectors(vec):
        out = []
        at = 0
        for n in lengths:
            out.append(vec[:, at : at + n].reshape(-1))
            at += n
        return out

    mine_split = split_vectors(vec_mine)
    other_split = split_vectors(vec_other)
    ada_sum = ada_sum + mine_split[4][None]
    ada_keep = lax.dynamic_index_in_dim(ada_sum, c, 0, keepdims=False)
    ada_got = swap(lax.dynamic_index_in_dim(ada_sum, 1 - c, 0, keepdims=False))
    adas = []
    biases = []
    for block in range(2):
        here = c == block
        adas.append(jnp.where(here, ada_keep, ada_got).reshape(6, D))
        biases.append(
            [jnp.where(here, a, b)[None] for a, b in zip(mine_split[:4], other_split[:4])]
        )

    mine = ((qkv_weight[0], proj_weight[0]), (up_weight[0],), (down_weight[0],))
    other = tuple(tuple(swap(w) for w in group) for group in mine)
    gatherer = Gatherer(mine, other, qkv_weight[0])
    x = lax.dynamic_index_in_dim(inputs, c, 0, keepdims=False)[0]
    cot = lax.dynamic_index_in_dim(cotangent, c, 0, keepdims=False)[0]
    kept = []
    kept_mlp = []

    def run_attend(block, value):
        got = attend(block, value, adas[block], biases[block], gatherer.operands(2 * block))
        gatherer.after = got[-1]
        kept.append(got)
        return swap(got[1])

    def run_mlp(block):
        mid, mlp_in = kept[block][-2:]
        got = mlp(block, mid, mlp_in, adas[block], biases[block], gatherer.operands(2 * block + 1))
        gatherer.after = got[-1]
        kept_mlp.append(got)
        return far_half(got[3]), swap(mlp_in)

    def branch_grad(block, grad):
        return (adas[block][5:] * grad.astype(F32)).astype(BF)

    for g in range(4):
        gatherer.extract(g)
    ids_all = in_order(across(ids_z)).reshape(-1, 2)
    gatherer.stack(0)
    (ids_all,) = gatherer.hold(ids_all)
    gatherer.onward(0)
    d_branch1 = branch_grad(1, cot)
    far_branch1 = swap(d_branch1)
    gatherer.share(0)
    gatherer.stack(1)
    far_sides0 = run_attend(0, x)
    gatherer.stack(2)
    far_sides0, far_branch1 = gatherer.hold(far_sides0, far_branch1)
    gatherer.onward(1)
    gatherer.share(1)
    gatherer.onward(2)
    gatherer.stack(3)
    far_mlp0 = run_mlp(0)
    y0 = kept_mlp[0][5]
    gatherer.share(2)
    far_mlp0 = gatherer.hold(*far_mlp0)
    far_sides1 = run_attend(1, y0)
    gatherer.onward(3)
    (far_sides1,) = gatherer.hold(far_sides1)
    gatherer.share(3)
    far_mlp1 = run_mlp(1)
    y1 = kept_mlp[1][5]

    reducer = Reducer(y1)

    def run_mlp_back(block, grad, d_branch):
        attended, mid, mlp_in = kept[block][-3:]
        wu, wd, hidden, act_t, branch, _ = kept_mlp[block]
        got = mlp_back(
            grad, d_branch, adas[block], mid, attended, hidden, branch, wu, wd, reducer.after
        )
        reducer.after = got[0]
        return got, far_half(got[0])

    def run_attend_back(block, value, back):
        wa, sides, q, k, v = kept[block][:5]
        _, d_mid, d_att, stats = back
        got = attend_back(
            value, d_mid, d_att, adas[block], q, k, v, stats, wa, reducer.after
        )
        reducer.after = got[2]
        return got

    def begin(block, kind, mode, *operands):
        reducer.begin(block, kind, mode, operands)

    back1, far_hidden1 = run_mlp_back(1, cot, d_branch1)
    begin(1, 2, 0, kept_mlp[1][3], far_mlp1[0], d_branch1, far_branch1)
    begin(1, 1, 3, kept[1][-1], far_mlp1[1], back1[0], far_hidden1)
    d_all1, dx1f, dx1, small1 = run_attend_back(1, y0, back1)
    far_all1 = far_half(d_all1)
    d_branch0 = branch_grad(0, dx1)
    far_branch0 = swap(d_branch0)
    reducer.first(1)
    begin(1, 0, 3, kept[1][1], far_sides1, d_all1, far_all1)
    back0, far_hidden0 = run_mlp_back(0, dx1, d_branch0)
    begin(0, 2, 3, kept_mlp[0][3], far_mlp0[0], d_branch0, far_branch0)
    reducer.first(2)
    reducer.second(1, send=False)
    begin(0, 1, 3, kept[0][-1], far_mlp0[1], back0[0], far_hidden0)
    reducer.first(0)
    reducer.send(1)
    d_all0, dx0, dx0_low, small0 = run_attend_back(0, x, back0)
    far_all0 = far_half(d_all0)
    reducer.first(3)
    reducer.third(1)
    reducer.second(2)
    begin(0, 0, 3, kept[0][1], far_sides0, d_all0, far_all0)
    small_keep = jnp.where(is_first, small0, small1)
    small_got = swap(jnp.where(is_first, small1, small0))
    reducer.first(4)
    reducer.third(2)
    reducer.second(3)
    reducer.second(0)
    (small_got,) = reducer.hold(small_got)
    small = jnp.stack(
        [jnp.where(is_first, small_keep, small_got), jnp.where(is_first, small_got, small_keep)]
    )
    block1, block0, last = (2, 1, 0), (2, 1), (0,)
    reducer.first(5)
    reducer.third(0)
    reducer.unite(1, block1)
    reducer.third(3)
    small = along_z(small)
    reducer.spread(1, block1)
    (small,) = reducer.hold(small)
    small = small[None]
    bits = [1 << i for i in range(lax.axis_size(R).bit_length() - 1)]
    hop = cross(small, 1)
    reducer.second(4)
    reducer.second(5)
    reducer.third(4)
    reducer.unite(0, block0)
    reducer.spread_on(1, block1)
    (hop,) = reducer.hold(hop)
    small = jnp.concatenate([small, hop])
    hop = cross(small, 2)
    reducer.spread(0, block0)
    reducer.third(5)
    reducer.unite(0, last)
    reducer.spread_on(0, block0)
    reducer.spread(0, last)
    (hop,) = reducer.hold(hop)
    small = jnp.concatenate([small, hop])
    for bit in bits[2:]:
        small = jnp.concatenate([small, cross(small, bit)])
    reducer.spread_on(0, last)
    reducer.finish(1, block1)
    reducer.finish(0, block0)
    reducer.finish(0, last)
    (qkv_grad, proj_grad), (up_grad,), (down_grad,) = (reducer.results[k] for k in range(3))

    def both_micros(v0, v1):
        keep = jnp.where(is_first, v0, v1)
        got = swap(jnp.where(is_first, v1, v0))
        return jnp.stack([jnp.where(is_first, keep, got), jnp.where(is_first, got, keep)])

    block_outputs = both_micros(y0, y1)[None, :, None]
    input_grads = both_micros(dx0, dx1.astype(F32))[None, :, None]

    small = in_order(small).reshape(-1, 16, D)
    sums = rows_sum(small[:, 6:14])
    dada_own = small[:, :6].reshape(-1, 6 * D)

    def own_slice(vec):
        vec = vec.reshape(-1)
        n = vec.shape[0] // NZ
        return lax.dynamic_slice_in_dim(vec, z * n, n, 0)[None]

    qv_bias_grad = own_slice(sums[:2])
    proj_bias_grad = own_slice(sums[2])
    up_bias_grad = own_slice(sums[3:7])
    down_bias_grad = own_slice(sums[7])

    cond_all = cond_of(ids_all[:, 0], ids_all[:, 1])
    labels_all = ids_all[:, 1]
    cond_rows = lax.dynamic_slice_in_dim(cond_all, z * ROWS, ROWS, 1)
    silu_rows = jax.nn.silu(cond_rows).astype(BF)
    ada_grad = lax.dot_general(
        silu_rows, dada_own, (((0,), (0,)), ((), ())), preferred_element_type=F32
    )
    ada_bias_grad = own_slice(rows_sum(dada_own))
    d_silu = mmt(dada_own, ada_weight[0])
    _, silu_back = jax.vjp(jax.nn.silu, cond_rows)
    d_cond = silu_back(d_silu)[0]
    d_cond = d_cond + swap(d_cond)
    d_cond_all = along_z(d_cond).transpose(1, 0, 2).reshape(-1, D)
    row_count = class_table.shape[0] // (2 * NZ)
    row_ids = (c * NZ + z) * row_count + jnp.arange(row_count, dtype=jnp.int32)
    owner = (row_ids[:, None] == labels_all[None, :]).astype(F32)
    table_grad = jnp.dot(owner, d_cond_all, precision=lax.Precision.HIGHEST)

    return (
        block_outputs,
        input_grads,
        table_grad,
        qkv_grad[None],
        qv_bias_grad,
        proj_grad[None],
        proj_bias_grad,
        up_grad[None],
        up_bias_grad,
        down_grad[None],
        down_bias_grad,
        ada_grad[None],
        ada_bias_grad,
    )


def solution(mesh):
    rows = P(None, (Z, R), None, None)
    matrix = P(S, Z, None)
    vector = P(S, Z)
    pair = P(None, (Z, R))
    in_specs = (rows, rows, pair, pair, P()) + (matrix, vector) * 5
    acts = P(S, None, (Z, R), None, None)
    out_specs = (acts, acts, P((S, Z), None)) + (matrix, vector) * 5
    return jax.shard_map(
        per_device, mesh=mesh, in_specs=in_specs, out_specs=out_specs, check_vma=False
    )
```
